32 devices in a mesh: groups: 2 (over y), chan: 4 (over z), pipe: 2 (over x), space: 2 (over core).
Axes of the slice: x: 2, y: 2, z: 4, core: 2. Of those that a mesh axis runs over, the one named last changes fastest.
Arguments:
- activations: bfloat16 [2, 4, 8, 8, 16, 256], P('pipe', 'groups', None, 'space', 'chan'), parts along dimension 1, may hold values from -6 to 6
- cotangent: bfloat16 [4, 8, 8, 16, 256], P('groups', None, 'space', 'chan'), parts along dimension 0, may hold values from -1.5 to 1.5
- space_weight: bfloat16 [2, 3, 3, 256, 256], P('pipe'), may hold values from -0.125 to 0.125
- time_weight: bfloat16 [2, 3, 256, 256], P('pipe'), may hold values from -0.21875 to 0.21875
Outputs:
- input_grads: bfloat16 [2, 4, 8, 8, 16, 256], P('pipe', 'groups', None, 'space', 'chan'), parts along dimension 1
- space_grads: float32 [2, 6, 3, 256, 256], P('pipe', 'groups', None, None, 'chan'), parts along dimension 1
- time_grads: float32 [2, 6, 256, 256], P('pipe', 'groups', None, 'chan'), parts along dimension 1
The draws below stay inside these ranges and needn't reach their ends.
There are 2 independent parts, one for each index of `groups`. The reference program is written for one: setup_inputs(seed, part) draws one part's arguments, and reference() takes and returns one part's arrays. A program takes and returns all parts, laid end to end along the dimension named above; an argument that names none is the same for every part. Nothing has to cross between parts.
All inputs are finite; a program needn't handle non-finite values.
Results may differ from the reference program's by a relative error of at most 0.0048.
Values may be sent and summed in bfloat16 or wider, within the bound.
No kernel may reach another device: no remote copies, remote signals or barrier semaphores. Data moves between devices by JAX's collectives and lax.ppermute only.
A program may use at most 64 MiB of HBM per device.

```python
import jax
import jax.numpy as jnp
from jax import lax

CHANNELS = 256
FRAMES = 8
CLIPS = 2
SECTIONS = 2
HEIGHT = 8
WIDTH = 16
N_PIPE = 2


def spiked(entries, own_key, source, target, blocks, factor):
    owner, partner = [(jnp.arange(entries.shape[position]) // (entries.shape[position] // blocks)).reshape([-1 if axis == position else 1 for axis in range(entries.ndim)]) for position in (source, target)]
    chosen = jax.random.permutation(own_key, blocks)[partner]
    strong = (owner == chosen) | (owner == (partner + blocks // 2) % blocks)
    return jnp.where(strong, factor * entries, entries)


def block_levels(rng, extent, pieces, least, top_value):
    gain = 1.0
    for axis_at, blocks in pieces:
        draws = jax.random.uniform(jax.random.fold_in(jax.random.fold_in(rng, 6), axis_at), (blocks,), jnp.float32, least / len(pieces), top_value / len(pieces))
        gain = gain * jnp.repeat(jnp.exp(draws), extent[axis_at] // blocks).reshape((-1,) + (1,) * (len(extent) - 1 - axis_at))
    return gain


def scatter_about(own_key, shape, scale, reach, shards=(), held_as=jnp.bfloat16):
    entries = scale * jax.random.normal(own_key, shape, jnp.float32)
    if shards:
        entries = entries * block_levels(own_key, shape, shards, -0.22, 0.18)
    return jnp.clip(entries, -reach, reach).astype(held_as)


def gaussian_with(rng, extent, spread, reach, pieces, heavy, held_as=jnp.bfloat16):
    values = spread * jax.random.normal(rng, extent, jnp.float32)
    if pieces:
        values = values * block_levels(rng, extent, pieces, -0.22, 0.18)
    return jnp.clip(spiked(values, jax.random.fold_in(rng, 3), *heavy), -reach, reach).astype(held_as)


def setup_inputs(seed: int = 0, part: int = 0) -> dict:
    streams_of = jax.random.split(jax.random.key(seed), 5)
    part_keys = jax.random.split(jax.random.fold_in(streams_of[4], part), 5)
    return {
        "activations": scatter_about(part_keys[0], (SECTIONS, CLIPS, FRAMES, HEIGHT, WIDTH, CHANNELS), 1.0, 6.0, ((0, 2), (3, 2), (4, 4))),
        "cotangent": gaussian_with(part_keys[1], (CLIPS, FRAMES, HEIGHT, WIDTH, CHANNELS), 0.25, 1.5, ((2, 2), (3, 4)), (3, 4, 4, 2.0)),
        "space_weight": scatter_about(streams_of[2], (SECTIONS, 3, 3, CHANNELS, CHANNELS), (9 * CHANNELS) ** -0.5, 0.125, ((0, 2),)),
        "time_weight": scatter_about(streams_of[3], (SECTIONS, 3, CHANNELS, CHANNELS), (3 * CHANNELS) ** -0.5, 0.21875, ((0, 2),)),
    }


def silu_slope(hidden):
    sigmoid_val = jax.nn.sigmoid(hidden)
    return sigmoid_val * (1.0 + hidden * (1.0 - sigmoid_val))

def tap_columns(padded, row_count, col_count):
    channels = padded.shape[-1]
    return jnp.concatenate([padded[:, row_tap:row_tap + row_count, col_tap:col_tap + col_count, :].reshape(-1, channels) for row_tap in range(3) for col_tap in range(3)], axis=1)

def back_columns(grad_pad, row_count, col_count):
    channels = grad_pad.shape[-1]
    return jnp.concatenate([grad_pad[:, 2 - row_tap:2 - row_tap + row_count, 2 - col_tap:2 - col_tap + col_count, :].reshape(-1, channels) for row_tap in range(3) for col_tap in range(3)], axis=1)

def temporal_grad(upstream, time_kernel):
    frames = upstream.shape[0]
    channels = upstream.shape[-1]
    later = jnp.pad(upstream, ((0, 2), (0, 0), (0, 0), (0, 0)))
    act_grad = None
    for time_tap in range(3):
        lagged = later[time_tap:time_tap + frames].reshape(-1, channels)
        term = lax.dot_general(lagged, time_kernel[time_tap], (((1,), (1,)), ((), ())), preferred_element_type=jnp.float32)
        act_grad = term if act_grad is None else act_grad + term
    return act_grad

def lagged_products(active, upstream):
    frames = active.shape[0]
    channels = active.shape[-1]
    earlier = jnp.pad(active, ((2, 0), (0, 0), (0, 0), (0, 0)))
    flat_up = upstream.reshape(-1, channels)
    return jnp.stack([lax.dot_general(earlier[2 - time_tap:2 - time_tap + frames].reshape(-1, channels), flat_up, (((0,), (0,)), ((), ())), preferred_element_type=jnp.float32) for time_tap in range(3)])

def block_backward(inputs, upstream, space_kernel, time_kernel):
    frames, height, width_cells, channels = inputs.shape
    padded = jnp.pad(inputs, ((0, 0), (1, 1), (1, 1), (0, 0)))
    columns = tap_columns(padded, height, width_cells)
    hidden = jnp.dot(columns, space_kernel.reshape(9 * channels, channels), preferred_element_type=jnp.float32)
    active = jax.nn.silu(hidden).astype(jnp.bfloat16)
    act_grad = temporal_grad(upstream, time_kernel)
    hidden_grad = (act_grad * silu_slope(hidden)).astype(jnp.bfloat16)
    grad_pad = jnp.pad(hidden_grad.reshape(frames, height, width_cells, channels), ((0, 0), (1, 1), (1, 1), (0, 0)))
    back_kernel = jnp.transpose(space_kernel.reshape(9, channels, channels), (0, 2, 1)).reshape(9 * channels, channels)
    conv_grad = jnp.dot(back_columns(grad_pad, height, width_cells), back_kernel, preferred_element_type=jnp.float32)
    space_grad = lax.dot_general(columns, hidden_grad, (((0,), (0,)), ((), ())), preferred_element_type=jnp.float32).reshape(3, 3, channels, channels)
    time_grad = lagged_products(active.reshape(frames, height, width_cells, channels), upstream)
    input_grad = (upstream.reshape(-1, channels).astype(jnp.float32) + conv_grad).astype(jnp.bfloat16).reshape(frames, height, width_cells, channels)
    return (input_grad, space_grad, time_grad)

def reference(activations, cotangent, space_weight, time_weight):
    channels = space_weight.shape[-1]
    upstream = cotangent
    input_list = []
    space_list = []
    time_list = []
    for section_index in range(N_PIPE - 1, -1, -1):

        def one_clip(totals, clip_pair, section_index=section_index):
            grad_in, grad_space, grad_time = block_backward(clip_pair[0], clip_pair[1], space_weight[section_index], time_weight[section_index])
            return ((totals[0] + grad_space, totals[1] + grad_time), grad_in)
        initial = (jnp.zeros((3, 3, channels, channels), jnp.float32), jnp.zeros((3, channels, channels), jnp.float32))
        totals, upstream = lax.scan(one_clip, initial, (activations[section_index], upstream))
        input_list.insert(0, upstream)
        space_list.insert(0, totals[0])
        time_list.insert(0, totals[1])
    return (jnp.stack(input_list), jnp.stack(space_list), jnp.stack(time_list))
```

```python
import functools

import jax
import jax.numpy as jnp
from jax import lax
from jax.experimental import pallas as pl
from jax.experimental.pallas import tpu as pltpu
from jax.sharding import PartitionSpec as P

F32 = jnp.float32
BF16 = jnp.bfloat16
VMEM_LIMIT = 50 * 1024 * 1024


def frame_shift(term, lag, frames):
    rows = term.shape[0]
    moved = pltpu.roll(term, rows - lag, 0)
    frame = lax.broadcasted_iota(jnp.int32, term.shape, 0) % frames
    return jnp.where(frame < frames - lag, moved, 0.0)


def fill_padded(padded, blocks, pad):
    rows_all, cols_all, steps, channels = padded.shape
    padded[0:pad] = jnp.zeros((pad, cols_all, steps, channels), padded.dtype)
    padded[rows_all - pad :] = jnp.zeros((pad, cols_all, steps, channels), padded.dtype)
    padded[:, 0:pad] = jnp.zeros((rows_all, pad, steps, channels), padded.dtype)
    padded[:, cols_all - pad :] = jnp.zeros((rows_all, pad, steps, channels), padded.dtype)
    space, chan, rows, cols = blocks.shape[:4]
    for i in range(space):
        for j in range(chan):
            padded[pad + i * rows : pad + (i + 1) * rows, pad + j * cols : pad + (j + 1) * cols] = (
                blocks[i, j]
            )


def slope_of(hidden):
    sig = jax.nn.sigmoid(hidden)
    return sig * (1.0 + hidden * (1.0 - sig))


def window_slope_kernel(x_ref, w_ref, slope_ref, xp_ref):
    space, chan, rows, cols, steps, channels = x_ref.shape
    fill_padded(xp_ref, x_ref, 2)
    r0 = lax.axis_index("space") * rows
    c0 = lax.axis_index("chan") * cols
    hidden = None
    for u in range(3):
        for v in range(3):
            piece = xp_ref[pl.ds(r0 + u, rows + 2), pl.ds(c0 + v, cols + 2)]
            term = jnp.dot(
                piece.reshape(-1, channels), w_ref[3 * u + v], preferred_element_type=F32
            )
            hidden = term if hidden is None else hidden + term
    slope_ref[...] = slope_of(hidden)


def own_window(gp_ref, slope_ref, wt_ref, twc_ref, out_ref, hg_ref, frames):
    rows, cols, steps, channels = out_ref.shape
    r0 = lax.axis_index("space") * rows
    c0 = lax.axis_index("chan") * cols
    window = gp_ref[pl.ds(r0, rows + 2), pl.ds(c0, cols + 2)].reshape(-1, channels)
    lagged = jnp.dot(window, twc_ref[...], preferred_element_type=F32)
    act = lagged[:, :channels]
    for lag in (1, 2):
        act = act + frame_shift(lagged[:, lag * channels : (lag + 1) * channels], lag, frames)
    hg_ref[...] = (act * slope_ref[...]).astype(BF16).reshape(hg_ref.shape)
    conv = None
    for u in range(3):
        for v in range(3):
            piece = hg_ref[2 - u : 2 - u + rows, 2 - v : 2 - v + cols]
            term = jnp.dot(
                piece.reshape(-1, channels), wt_ref[3 * u + v], preferred_element_type=F32
            )
            conv = term if conv is None else conv + term
    own = gp_ref[pl.ds(r0 + 1, rows), pl.ds(c0 + 1, cols)].reshape(-1, channels)
    out_ref[...] = (own.astype(F32) + conv).astype(BF16).reshape(out_ref.shape)


def tick_kernel(frames, g_ref, slope_ref, wt_ref, twc_ref, out_ref, gp_ref, hg_ref):
    fill_padded(gp_ref, g_ref, 1)
    own_window(gp_ref, slope_ref, wt_ref, twc_ref, out_ref, hg_ref, frames)


def tile_kernel(share, x_ref, w_ref, act_ref, xt_ref, slope_ref, xp_ref):
    space, chan, rows, cols, steps, channels = x_ref.shape
    fill_padded(xp_ref, x_ref, 1)
    width = chan * cols
    span = width * steps
    for i in range(space * rows):
        hidden = None
        for u in range(3):
            for v in range(3):
                piece = xp_ref[i + u, v : v + width].reshape(-1, channels)
                term = jnp.dot(piece, w_ref[3 * u + v], preferred_element_type=F32)
                hidden = term if hidden is None else hidden + term
        active = (hidden * jax.nn.sigmoid(hidden)).astype(BF16)
        act_ref[:, i * span : (i + 1) * span] = active.T
        slope_ref[i * span : (i + 1) * span, :] = slope_of(hidden[:, :share])
        xt_ref[:, i * span : (i + 1) * span] = xp_ref[i + 1, 1 : 1 + width].reshape(-1, channels).T


def final_kernel(
    frames,
    g_ref,
    slope_w_ref,
    slope_s_ref,
    act_ref,
    xt_ref,
    wt_ref,
    twc_ref,
    pick_ref,
    out_ref,
    space_ref,
    time_ref,
    gp_ref,
    hg_ref,
    hs_ref,
    hcols_ref,
    gcols_ref,
):
    space, chan, rows, cols, steps, channels = g_ref.shape
    share = slope_s_ref.shape[1]
    width = chan * cols
    height = space * rows
    span = width * steps
    fill_padded(gp_ref, g_ref, 1)
    own_window(gp_ref, slope_w_ref, wt_ref, twc_ref, out_ref, hg_ref, frames)
    hs_ref[...] = jnp.zeros(hs_ref.shape, BF16)
    for i in range(height):
        block = gp_ref[i + 1, 1 : 1 + width].reshape(-1, channels)
        mixed = jnp.dot(block, pick_ref[...], preferred_element_type=F32)
        act = mixed[:, :share]
        for lag in (1, 2):
            act = act + frame_shift(mixed[:, lag * share : (lag + 1) * share], lag, frames)
        grad = (act * slope_s_ref[i * span : (i + 1) * span, :]).astype(BF16)
        hs_ref[i + 1, 1 : 1 + width] = grad.reshape(width, steps, share)
        own = mixed[:, 3 * share :]
        for lag in range(3):
            shifted = own if lag == 0 else frame_shift(own, lag, frames)
            gcols_ref[i * span : (i + 1) * span, lag * share : (lag + 1) * share] = shifted.astype(
                BF16
            )
    for u in range(3):
        for v in range(3):
            tap = 3 * u + v
            for i in range(height):
                hcols_ref[i * span : (i + 1) * span, tap * share : (tap + 1) * share] = hs_ref[
                    i + 2 - u, 2 - v : 2 - v + width
                ].reshape(-1, share)
    time_sum = jnp.dot(act_ref[...], gcols_ref[...], preferred_element_type=F32)
    first = lax.axis_index("chan")
    for j in range(chan):
        place = pl.multiple_of(lax.rem(first + j, chan) * share, share)
        for lag in range(3):
            time_ref[lag, pl.ds(place, share), :] = time_sum[
                j * share : (j + 1) * share, lag * share : (lag + 1) * share
            ]
    space_sum = jnp.dot(xt_ref[...], hcols_ref[...], preferred_element_type=F32)
    for tap in range(9):
        space_ref[tap] = space_sum[:, tap * share : (tap + 1) * share]


def call(kernel, outs, scratch, flops, moved, *operands):
    return pl.pallas_call(
        kernel,
        out_shape=outs,
        scratch_shapes=scratch,
        compiler_params=pltpu.CompilerParams(vmem_limit_bytes=VMEM_LIMIT),
        cost_estimate=pl.CostEstimate(flops=flops, bytes_accessed=moved, transcendentals=0),
    )(*operands)


def per_device(activations, cotangent, space_weight, time_weight):
    clips, frames, rows, cols, channels = activations.shape[1:]
    steps = clips * frames
    space, chan = lax.axis_size("space"), lax.axis_size("chan")
    depth = lax.axis_size("pipe")
    stage = lax.axis_index("pipe")
    share = channels // chan
    height, width = space * rows, chan * cols
    count = height * width * steps
    win = (rows + 2) * (cols + 2) * steps
    first_col = lax.axis_index("chan") * share

    def cells(array):
        return jnp.transpose(array, (2, 3, 0, 1, 4)).reshape(rows, cols, steps, channels)

    def gathered(block):
        whole = lax.all_gather(block, ("space", "chan"), axis=0, tiled=False)
        return whole.reshape(space, chan, rows, cols, steps, channels)

    x_own = cells(activations[0])
    cot_own = cells(cotangent)
    x_all = gathered(x_own)
    up_all = gathered(cot_own)

    order = jnp.roll(space_weight[0].reshape(9, channels, channels), -first_col, axis=2)
    order_back = jnp.transpose(order, (0, 2, 1))
    time_rolled = jnp.roll(time_weight[0], -first_col, axis=1)
    time_back = jnp.transpose(time_rolled, (2, 0, 1))
    time_cat = time_back.reshape(channels, 3 * channels)
    chosen = jax.nn.one_hot(first_col + jnp.arange(share), channels, axis=0, dtype=BF16)
    pick = jnp.concatenate([time_back[:, k, :share] for k in range(3)] + [chosen], axis=1)

    cell = (steps, channels)
    slope_w = call(
        window_slope_kernel,
        jax.ShapeDtypeStruct((win, channels), F32),
        [pltpu.VMEM((height + 4, width + 4) + cell, BF16)],
        2 * win * 9 * channels * channels,
        4_000_000,
        x_all,
        order,
    )
    padded = pltpu.VMEM((height + 2, width + 2) + cell, BF16)
    hg_win = pltpu.VMEM((rows + 2, cols + 2) + cell, BF16)
    for _ in range(depth - 1):
        g_own = call(
            functools.partial(tick_kernel, frames),
            jax.ShapeDtypeStruct((rows, cols) + cell, BF16),
            [padded, hg_win],
            2 * win * 9 * channels * channels,
            4_000_000,
            up_all,
            slope_w,
            order_back,
            time_cat,
        )
        received = lax.ppermute(g_own, "pipe", [(i, i - 1) for i in range(1, depth)])
        up_all = gathered(jnp.where(stage == depth - 1, cot_own, received))
    act_t, x_t, slope_s = call(
        functools.partial(tile_kernel, share),
        (
            jax.ShapeDtypeStruct((channels, count), BF16),
            jax.ShapeDtypeStruct((channels, count), BF16),
            jax.ShapeDtypeStruct((count, share), F32),
        ),
        [padded],
        2 * count * 9 * channels * channels,
        6_000_000,
        x_all,
        order,
    )
    grads, space_grad, time_grad = call(
        functools.partial(final_kernel, frames),
        (
            jax.ShapeDtypeStruct((rows, cols) + cell, BF16),
            jax.ShapeDtypeStruct((9, channels, share), F32),
            jax.ShapeDtypeStruct((3, channels, share), F32),
        ),
        [
            padded,
            hg_win,
            pltpu.VMEM((height + 2, width + 2, steps, share), BF16),
            pltpu.VMEM((count, 9 * share), BF16),
            pltpu.VMEM((count, 3 * share), BF16),
        ],
        4 * win * 9 * channels * channels,
        8_000_000,
        up_all,
        slope_w,
        slope_s,
        act_t,
        x_t,
        order_back,
        time_cat,
        pick,
    )
    grads = jnp.transpose(
        grads.reshape(rows, cols, clips, frames, channels), (2, 3, 0, 1, 4)
    )
    return (
        grads[None],
        space_grad.reshape(3, 3, channels, share)[None],
        time_grad[None],
    )


def solution(mesh):
    return jax.shard_map(
        per_device,
        mesh=mesh,
        in_specs=(
            P("pipe", "groups", None, "space", "chan", None),
            P("groups", None, "space", "chan", None),
            P("pipe", None, None, None, None),
            P("pipe", None, None, None),
        ),
        out_specs=(
            P("pipe", "groups", None, "space", "chan", None),
            P("pipe", "groups", None, None, "chan"),
            P("pipe", "groups", None, "chan"),
        ),
        check_vma=False,
    )
```

```python
import functools

import jax
import jax.numpy as jnp
from jax import lax
from jax.experimental import pallas as pl
from jax.experimental.pallas import tpu as pltpu
from jax.sharding import PartitionSpec as P

F32 = jnp.float32
BF16 = jnp.bfloat16
VMEM_LIMIT = 50 * 1024 * 1024


def frame_shift(term, lag, frames):
    rows = term.shape[0]
    moved = pltpu.roll(term, rows - lag, 0)
    frame = lax.broadcasted_iota(jnp.int32, term.shape, 0) % frames
    return jnp.where(frame < frames - lag, moved, 0.0)


def fill_padded(padded, halves, pad):
    rows_all, cols_all, steps, channels = padded.shape
    padded[0:pad] = jnp.zeros((pad, cols_all, steps, channels), padded.dtype)
    padded[rows_all - pad :] = jnp.zeros((pad, cols_all, steps, channels), padded.dtype)
    padded[:, 0:pad] = jnp.zeros((rows_all, pad, steps, channels), padded.dtype)
    padded[:, cols_all - pad :] = jnp.zeros((rows_all, pad, steps, channels), padded.dtype)
    first = lax.axis_index("space")
    for k, half in enumerate(halves):
        chan, rows, cols = half.shape[:3]
        top = pad + lax.rem(first + k, len(halves)) * rows
        for j in range(chan):
            padded[pl.ds(top, rows), pad + j * cols : pad + (j + 1) * cols] = half[j]


def slope_of(hidden):
    sig = jax.nn.sigmoid(hidden)
    return sig * (1.0 + hidden * (1.0 - sig))


def window_slope_kernel(space, *refs):
    x_refs, (w_ref, slope_ref, xp_ref) = refs[:space], refs[space:]
    chan, rows, cols, steps, channels = x_refs[0].shape
    fill_padded(xp_ref, x_refs, 2)
    r0 = lax.axis_index("space") * rows
    c0 = lax.axis_index("chan") * cols
    hidden = None
    for u in range(3):
        for v in range(3):
            piece = xp_ref[pl.ds(r0 + u, rows + 2), pl.ds(c0 + v, cols + 2)]
            term = jnp.dot(
                piece.reshape(-1, channels), w_ref[3 * u + v], preferred_element_type=F32
            )
            hidden = term if hidden is None else hidden + term
    slope_ref[...] = slope_of(hidden)


def own_window(gp_ref, slope_ref, wt_ref, twc_ref, out_ref, hg_ref, frames):
    rows, cols, steps, channels = out_ref.shape
    r0 = lax.axis_index("space") * rows
    c0 = lax.axis_index("chan") * cols
    window = gp_ref[pl.ds(r0, rows + 2), pl.ds(c0, cols + 2)].reshape(-1, channels)
    lagged = jnp.dot(window, twc_ref[...], preferred_element_type=F32)
    act = lagged[:, :channels]
    for lag in (1, 2):
        act = act + frame_shift(lagged[:, lag * channels : (lag + 1) * channels], lag, frames)
    hg_ref[...] = (act * slope_ref[...]).astype(BF16).reshape(hg_ref.shape)
    conv = None
    for u in range(3):
        for v in range(3):
            piece = hg_ref[2 - u : 2 - u + rows, 2 - v : 2 - v + cols]
            term = jnp.dot(
                piece.reshape(-1, channels), wt_ref[3 * u + v], preferred_element_type=F32
            )
            conv = term if conv is None else conv + term
    own = gp_ref[pl.ds(r0 + 1, rows), pl.ds(c0 + 1, cols)].reshape(-1, channels)
    out_ref[...] = (own.astype(F32) + conv).astype(BF16).reshape(out_ref.shape)


def tick_kernel(space, frames, *refs):
    g_refs, (slope_ref, wt_ref, twc_ref, out_ref, gp_ref, hg_ref) = refs[:space], refs[space:]
    fill_padded(gp_ref, g_refs, 1)
    own_window(gp_ref, slope_ref, wt_ref, twc_ref, out_ref, hg_ref, frames)


def tile_kernel(space, share, *refs):
    x_refs, (w_ref, act_ref, xt_ref, slope_ref, xp_ref) = refs[:space], refs[space:]
    chan, rows, cols, steps, channels = x_refs[0].shape
    fill_padded(xp_ref, x_refs, 1)
    width = chan * cols
    span = width * steps
    for i in range(space * rows):
        hidden = None
        for u in range(3):
            for v in range(3):
                piece = xp_ref[i + u, v : v + width].reshape(-1, channels)
                term = jnp.dot(piece, w_ref[3 * u + v], preferred_element_type=F32)
                hidden = term if hidden is None else hidden + term
        active = (hidden * jax.nn.sigmoid(hidden)).astype(BF16)
        act_ref[:, i * span : (i + 1) * span] = active.T
        slope_ref[i * span : (i + 1) * span, :] = slope_of(hidden[:, :share])
        xt_ref[:, i * span : (i + 1) * span] = xp_ref[i + 1, 1 : 1 + width].reshape(-1, channels).T


def final_kernel(space, frames, *refs):
    g_refs = refs[:space]
    slope_w_ref, slope_s_ref, act_ref, xt_ref, wt_ref, twc_ref, pick_ref = refs[space : space + 7]
    out_ref, space_ref, time_ref, gp_ref, hg_ref, hs_ref, hcols_ref, gcols_ref, roll_ref = refs[space + 7 :]
    chan, rows, cols, steps, channels = g_refs[0].shape
    share = slope_s_ref.shape[1]
    width = chan * cols
    height = space * rows
    span = width * steps
    fill_padded(gp_ref, g_refs, 1)
    own_window(gp_ref, slope_w_ref, wt_ref, twc_ref, out_ref, hg_ref, frames)
    hs_ref[...] = jnp.zeros(hs_ref.shape, BF16)
    for i in range(height):
        block = gp_ref[i + 1, 1 : 1 + width].reshape(-1, channels)
        mixed = jnp.dot(block, pick_ref[...], preferred_element_type=F32)
        act = mixed[:, :share]
        for lag in (1, 2):
            act = act + frame_shift(mixed[:, lag * share : (lag + 1) * share], lag, frames)
        grad = (act * slope_s_ref[i * span : (i + 1) * span, :]).astype(BF16)
        hs_ref[i + 1, 1 : 1 + width] = grad.reshape(width, steps, share)
        own = mixed[:, 3 * share :]
        for lag in range(3):
            shifted = own if lag == 0 else frame_shift(own, lag, frames)
            gcols_ref[i * span : (i + 1) * span, lag * share : (lag + 1) * share] = shifted.astype(
                BF16
            )
    for u in range(3):
        for v in range(3):
            tap = 3 * u + v
            for i in range(height):
                hcols_ref[i * span : (i + 1) * span, tap * share : (tap + 1) * share] = hs_ref[
                    i + 2 - u, 2 - v : 2 - v + width
                ].reshape(-1, share)
    time_sum = jnp.dot(act_ref[...], gcols_ref[...], preferred_element_type=F32)
    first = lax.axis_index("chan")
    for j in range(chan):
        place = pl.multiple_of(lax.rem(first + j, chan) * share, share)
        for lag in range(3):
            roll_ref[lag, pl.ds(place, share), :] = time_sum[
                j * share : (j + 1) * share, lag * share : (lag + 1) * share
            ]
    for lag in range(3):
        time_ref[lag] = roll_ref[lag].T
    space_sum = jnp.dot(xt_ref[...], hcols_ref[...], preferred_element_type=F32)
    space_ref[...] = space_sum.T.reshape(space_ref.shape)


def call(kernel, outs, scratch, flops, moved, *operands):
    return pl.pallas_call(
        kernel,
        out_shape=outs,
        scratch_shapes=scratch,
        compiler_params=pltpu.CompilerParams(vmem_limit_bytes=VMEM_LIMIT),
        cost_estimate=pl.CostEstimate(flops=flops, bytes_accessed=moved, transcendentals=0),
    )(*operands)


def per_device(activations, cotangent, space_weight, time_weight):
    clips, frames, rows, cols, channels = activations.shape[1:]
    steps = clips * frames
    space, chan = lax.axis_size("space"), lax.axis_size("chan")
    depth = lax.axis_size("pipe")
    stage = lax.axis_index("pipe")
    share = channels // chan
    height, width = space * rows, chan * cols
    count = height * width * steps
    win = (rows + 2) * (cols + 2) * steps
    first_col = lax.axis_index("chan") * share

    def cells(array):
        return jnp.transpose(array, (2, 3, 0, 1, 4)).reshape(rows, cols, steps, channels)

    def gathered(block):
        half = lax.all_gather(block, "chan", axis=0, tiled=False)
        return [half] + [
            lax.ppermute(half, "space", [((i + k) % space, i) for i in range(space)])
            for k in range(1, space)
        ]

    x_own = cells(activations[0])
    cot_own = cells(cotangent)
    x_all = gathered(x_own)
    up_all = gathered(cot_own)

    order = jnp.roll(space_weight[0].reshape(9, channels, channels), -first_col, axis=2)
    order_back = jnp.transpose(order, (0, 2, 1))
    time_rolled = jnp.roll(time_weight[0], -first_col, axis=1)
    time_back = jnp.transpose(time_rolled, (2, 0, 1))
    time_cat = time_back.reshape(channels, 3 * channels)
    chosen = jax.nn.one_hot(first_col + jnp.arange(share), channels, axis=0, dtype=BF16)
    pick = jnp.concatenate([time_back[:, k, :share] for k in range(3)] + [chosen], axis=1)

    cell = (steps, channels)
    slope_w = call(
        functools.partial(window_slope_kernel, space),
        jax.ShapeDtypeStruct((win, channels), F32),
        [pltpu.VMEM((height + 4, width + 4) + cell, BF16)],
        2 * win * 9 * channels * channels,
        4_000_000,
        *x_all,
        order,
    )
    padded = pltpu.VMEM((height + 2, width + 2) + cell, BF16)
    hg_win = pltpu.VMEM((rows + 2, cols + 2) + cell, BF16)
    for _ in range(depth - 1):
        g_own = call(
            functools.partial(tick_kernel, space, frames),
            jax.ShapeDtypeStruct((rows, cols) + cell, BF16),
            [padded, hg_win],
            2 * win * 9 * channels * channels,
            4_000_000,
            *up_all,
            slope_w,
            order_back,
            time_cat,
        )
        received = lax.ppermute(g_own, "pipe", [(i, i - 1) for i in range(1, depth)])
        up_all = gathered(jnp.where(stage == depth - 1, cot_own, received))
    act_t, x_t, slope_s = call(
        functools.partial(tile_kernel, space, share),
        (
            jax.ShapeDtypeStruct((channels, count), BF16),
            jax.ShapeDtypeStruct((channels, count), BF16),
            jax.ShapeDtypeStruct((count, share), F32),
        ),
        [padded],
        2 * count * 9 * channels * channels,
        6_000_000,
        *x_all,
        order,
    )
    grads, space_grad, time_grad = call(
        functools.partial(final_kernel, space, frames),
        (
            jax.ShapeDtypeStruct((rows, cols) + cell, BF16),
            jax.ShapeDtypeStruct((9, share, channels), F32),
            jax.ShapeDtypeStruct((3, share, channels), F32),
        ),
        [
            padded,
            hg_win,
            pltpu.VMEM((height + 2, width + 2, steps, share), BF16),
            pltpu.VMEM((count, 9 * share), BF16),
            pltpu.VMEM((count, 3 * share), BF16),
            pltpu.VMEM((3, channels, share), F32),
        ],
        4 * win * 9 * channels * channels,
        8_000_000,
        *up_all,
        slope_w,
        slope_s,
        act_t,
        x_t,
        order_back,
        time_cat,
        pick,
    )
    grads = jnp.transpose(
        grads.reshape(rows, cols, clips, frames, channels), (2, 3, 0, 1, 4)
    )
    return (
        grads[None],
        jnp.swapaxes(space_grad, 1, 2).reshape(3, 3, channels, share)[None],
        jnp.swapaxes(time_grad, 1, 2)[None],
    )


def solution(mesh):
    return jax.shard_map(
        per_device,
        mesh=mesh,
        in_specs=(
            P("pipe", "groups", None, "space", "chan", None),
            P("groups", None, "space", "chan", None),
            P("pipe", None, None, None, None),
            P("pipe", None, None, None),
        ),
        out_specs=(
            P("pipe", "groups", None, "space", "chan", None),
            P("pipe", "groups", None, None, "chan"),
            P("pipe", "groups", None, "chan"),
        ),
        check_vma=False,
    )
```

```python
import functools

import jax
import jax.numpy as jnp
from jax import lax
from jax.experimental import pallas as pl
from jax.experimental.pallas import tpu as pltpu
from jax.sharding import PartitionSpec as P

F32 = jnp.float32
BF16 = jnp.bfloat16
MIB = 1024 * 1024
ROWS_IN = (((1,), (1,)), ((), ()))


def dot(left, right):
    return jnp.dot(left, right, preferred_element_type=F32)


def dot_back(left, right):
    return lax.dot_general(left, right, ROWS_IN, preferred_element_type=F32)


def frame_shift(term, lag, frames):
    rows = term.shape[0]
    moved = pltpu.roll(term, rows - lag, 0)
    frame = lax.broadcasted_iota(jnp.int32, term.shape, 0) % frames
    return jnp.where(frame < frames - lag, moved, 0.0)


def slope_of(hidden):
    sig = jax.nn.sigmoid(hidden)
    return sig * (1.0 + hidden * (1.0 - sig))


def pack_kernel(x_ref, cot_ref, xc_ref, cc_ref, right_ref, left_ref, side_ref, dr_ref, dl_ref):
    rows, cols, steps, channels = xc_ref.shape
    for src, dst in ((x_ref, xc_ref), (cot_ref, cc_ref)):
        for r in range(rows):
            dst[r] = jnp.swapaxes(src[:, :, r].reshape(steps, cols, channels), 0, 1)
    cells = rows * cols
    for msg, col in ((right_ref, cols - 1), (left_ref, 0)):
        msg[:cells] = xc_ref[...].reshape(cells, steps, channels)
        for r in range(rows):
            msg[cells + r] = cc_ref[r, col]
    top = lax.axis_index("space") == 0
    for here, row, edge in ((top, rows - 2, rows - 1), (jnp.logical_not(top), 0, 0)):

        @pl.when(here)
        def _(row=row, edge=edge):
            side_ref[:2] = xc_ref[row : row + 2]
            side_ref[2] = cc_ref[edge]
            for msg, col, last in ((dr_ref, cols - 2, cols - 1), (dl_ref, 0, 0)):
                for i in range(2):
                    msg[2 * i : 2 * i + 2] = xc_ref[row + i, col : col + 2]
                msg[4] = cc_ref[edge, last]


def conv_back(hg_ref, w_ref, rows, cols):
    channels = w_ref.shape[-1]
    conv = None
    for u in range(3):
        for v in range(3):
            piece = hg_ref[2 - u : 2 - u + rows, 2 - v : 2 - v + cols]
            term = dot_back(piece.reshape(-1, channels), w_ref[3 * u + v])
            conv = term if conv is None else conv + term
    return conv


def window_grad(window, slope_ref, tw_ref, hg_ref, frames):
    act = dot_back(window, tw_ref[0])
    for lag in (1, 2):
        act = act + frame_shift(dot_back(window, tw_ref[lag]), lag, frames)
    hg_ref[...] = (act * slope_ref[...]).astype(BF16).reshape(hg_ref.shape)


def send_on(out_ref, own, conv, cot_ref):
    first = lax.axis_index("pipe") == 0

    @pl.when(first)
    def _():
        out_ref[...] = cot_ref[...]

    @pl.when(jnp.logical_not(first))
    def _():
        out_ref[...] = (own.astype(F32) + conv).astype(BF16).reshape(out_ref.shape)


def first_kernel(
    frames, x_ref, cot_ref, l_ref, r_ref, s_ref, dl_ref, dr_ref, w_ref, tw_ref,
    slope_ref, out_ref, xw_ref, cw_ref, hg_ref,
):
    rows, cols, steps, channels = x_ref.shape
    cells = rows * cols
    bottom = lax.axis_index("space")
    xw_ref[2 : 2 + rows, 2 : 2 + cols] = x_ref[...]
    cw_ref[1 : 1 + rows, 1 : 1 + cols] = cot_ref[...]
    for r in range(rows):
        xw_ref[2 + r, 0:2] = l_ref[r * cols + cols - 2 : r * cols + cols]
        xw_ref[2 + r, cols + 2 : cols + 4] = r_ref[r * cols : r * cols + 2]
        cw_ref[1 + r, 0] = l_ref[cells + r]
        cw_ref[1 + r, cols + 1] = r_ref[cells + r]
    near = (1 - bottom) * (rows + 2)
    far = bottom * (rows + 2)
    for i in range(2):
        xw_ref[near + i, 2 : 2 + cols] = s_ref[i]
        xw_ref[near + i, 0:2] = dl_ref[2 * i : 2 * i + 2]
        xw_ref[near + i, cols + 2 : cols + 4] = dr_ref[2 * i : 2 * i + 2]
        xw_ref[far + i] = jnp.zeros(xw_ref.shape[1:], BF16)
    near = (1 - bottom) * (rows + 1)
    far = bottom * (rows + 1)
    cw_ref[near, 1 : 1 + cols] = s_ref[2]
    cw_ref[near, 0] = dl_ref[4]
    cw_ref[near, cols + 1] = dr_ref[4]
    cw_ref[far] = jnp.zeros(cw_ref.shape[1:], BF16)
    hidden = None
    for u in range(3):
        for v in range(3):
            piece = xw_ref[u : u + rows + 2, v : v + cols + 2]
            term = dot(piece.reshape(-1, channels), w_ref[3 * u + v])
            hidden = term if hidden is None else hidden + term
    slope_ref[...] = slope_of(hidden)
    window_grad(cw_ref[...].reshape(-1, channels), slope_ref, tw_ref, hg_ref, frames)
    conv = conv_back(hg_ref, w_ref, rows, cols)
    send_on(out_ref, cot_ref[...].reshape(-1, channels), conv, cot_ref)


def collect_kernel(wrapped, *refs):
    pieces, out_ref = refs[:-1], refs[-1]
    chan = len(pieces) - wrapped
    rows, cols, steps, channels = pieces[0].shape
    me = lax.axis_index("chan")

    def put(d, piece):
        place = lax.rem(me - d + chan, chan) * cols
        for r in range(rows):
            out_ref[r, pl.ds(place, cols)] = (
                piece[r] if piece.ndim == 4 else piece[r * cols : (r + 1) * cols]
            )

    for d in range(chan):
        if not wrapped or d not in (1, chan - 1):
            put(d, pieces[d])
    if wrapped:
        edge = pieces[chan]
        for d, at in ((1, 0), (chan - 1, chan - 1)):
            pl.when(me == at)(functools.partial(put, d, edge))
            pl.when(me != at)(functools.partial(put, d, pieces[d]))


def fill_padded(padded, own, other):
    rows_all, cols_all, steps, channels = padded.shape
    zero_row = jnp.zeros((1, cols_all, steps, channels), padded.dtype)
    padded[0:1] = zero_row
    padded[rows_all - 1 :] = zero_row
    for r in range(1, rows_all - 1):
        for c in (0, cols_all - 1):
            padded[r, c] = jnp.zeros((steps, channels), padded.dtype)
    rows = own.shape[0]
    bottom = lax.axis_index("space")
    for half, top in ((own, bottom * rows), (other, (1 - bottom) * rows)):
        padded[pl.ds(1 + top, rows), 1 : cols_all - 1] = half[...]


def own_window(gp_ref, slope_ref, w_ref, tw_ref, hg_ref, frames, rows, cols):
    channels = w_ref.shape[-1]
    r0 = lax.axis_index("space") * rows
    c0 = lax.axis_index("chan") * cols
    window = gp_ref[pl.ds(r0, rows + 2), pl.ds(c0, cols + 2)].reshape(-1, channels)
    window_grad(window, slope_ref, tw_ref, hg_ref, frames)
    own = gp_ref[pl.ds(r0 + 1, rows), pl.ds(c0 + 1, cols)].reshape(-1, channels)
    return own, conv_back(hg_ref, w_ref, rows, cols)


def tick_kernel(
    frames, g_ref, other_ref, cot_ref, slope_ref, w_ref, tw_ref, out_ref, gp_ref, hg_ref
):
    rows, cols = cot_ref.shape[:2]
    fill_padded(gp_ref, g_ref, other_ref)
    own, conv = own_window(gp_ref, slope_ref, w_ref, tw_ref, hg_ref, frames, rows, cols)
    send_on(out_ref, own, conv, cot_ref)


def tile_kernel(share, x_ref, other_ref, w_ref, act_ref, xt_ref, slope_ref, xp_ref):
    rows, width, steps, channels = x_ref.shape
    fill_padded(xp_ref, x_ref, other_ref)
    span = width * steps
    turn = lax.rem(channels - lax.axis_index("chan") * share, channels)
    for i in range(2 * rows):
        hidden = None
        for u in range(3):
            for v in range(3):
                piece = xp_ref[i + u, v : v + width].reshape(-1, channels)
                term = dot(piece, w_ref[3 * u + v])
                hidden = term if hidden is None else hidden + term
        active = (hidden * jax.nn.sigmoid(hidden)).astype(BF16)
        act_ref[:, i * span : (i + 1) * span] = active.T
        slope_ref[i * span : (i + 1) * span, :] = slope_of(pltpu.roll(hidden, turn, 1)[:, :share])
        xt_ref[:, i * span : (i + 1) * span] = xp_ref[i + 1, 1 : 1 + width].reshape(-1, channels).T


def final_kernel(
    frames, g_ref, other_ref, slope_w_ref, slope_s_ref, act_ref, xt_ref, w_ref, tw_ref,
    out_ref, space_ref, time_ref, gp_ref, hg_ref, hs_ref, hcols_ref, gcols_ref, pick_ref,
):
    rows, width, steps, channels = g_ref.shape
    clips, _, _, cols, _ = out_ref.shape
    share = slope_s_ref.shape[1]
    height = 2 * rows
    span = width * steps
    fill_padded(gp_ref, g_ref, other_ref)
    first = pl.multiple_of(lax.axis_index("chan") * share, share)
    for lag in range(3):
        pick_ref[lag * share : (lag + 1) * share, :] = tw_ref[lag, pl.ds(first, share), :]
    at = lax.broadcasted_iota(jnp.int32, (share, channels), 1) - first
    chosen = at == lax.broadcasted_iota(jnp.int32, (share, channels), 0)
    pick_ref[3 * share :, :] = jnp.where(chosen, 1.0, 0.0).astype(BF16)
    hs_ref[...] = jnp.zeros(hs_ref.shape, BF16)
    for i in range(height):
        block = gp_ref[i + 1, 1 : 1 + width].reshape(-1, channels)
        mixed = dot_back(block, pick_ref[...])
        act = mixed[:, :share]
        for lag in (1, 2):
            act = act + frame_shift(mixed[:, lag * share : (lag + 1) * share], lag, frames)
        grad = (act * slope_s_ref[i * span : (i + 1) * span, :]).astype(BF16)
        hs_ref[i + 1, 1 : 1 + width] = grad.reshape(width, steps, share)
        own = mixed[:, 3 * share :]
        for lag in range(3):
            shifted = own if lag == 0 else frame_shift(own, lag, frames)
            gcols_ref[i * span : (i + 1) * span, lag * share : (lag + 1) * share] = shifted.astype(
                BF16
            )
    for u in range(3):
        for v in range(3):
            tap = 3 * u + v
            for i in range(height):
                hcols_ref[i * span : (i + 1) * span, tap * share : (tap + 1) * share] = hs_ref[
                    i + 2 - u, 2 - v : 2 - v + width
                ].reshape(-1, share)
    time_ref[...] = dot(act_ref[...], gcols_ref[...]).T.reshape(time_ref.shape)
    space_ref[...] = dot(xt_ref[...], hcols_ref[...]).T.reshape(space_ref.shape)
    own, conv = own_window(gp_ref, slope_w_ref, w_ref, tw_ref, hg_ref, frames, rows, cols)
    grads = (own.astype(F32) + conv).astype(BF16).reshape(rows, cols, steps, channels)
    for r in range(rows):
        out_ref[:, :, r] = jnp.swapaxes(grads[r], 0, 1).reshape(clips, frames, cols, channels)


def call(kernel, outs, scratch, limit, flops, moved, *operands):
    return pl.pallas_call(
        kernel,
        out_shape=outs,
        scratch_shapes=scratch,
        compiler_params=pltpu.CompilerParams(vmem_limit_bytes=limit * MIB),
        cost_estimate=pl.CostEstimate(flops=flops, bytes_accessed=moved, transcendentals=0),
    )(*operands)


def per_device(activations, cotangent, space_weight, time_weight):
    clips, frames, rows, cols, channels = activations.shape[1:]
    steps = clips * frames
    chan, depth = lax.axis_size("chan"), lax.axis_size("pipe")
    share = channels // chan
    height, width = 2 * rows, chan * cols
    count = height * width * steps
    win = (rows + 2) * (cols + 2) * steps
    large = 24 if chan <= 4 else 56
    w = space_weight[0].reshape(9, channels, channels)
    tw = time_weight[0]
    cell = (steps, channels)

    def bf16(*shape):
        return jax.ShapeDtypeStruct(shape + cell, BF16)

    x_own, cot_own, to_right, to_left, to_side, to_dr, to_dl = call(
        pack_kernel,
        (
            bf16(rows, cols), bf16(rows, cols), bf16(rows * cols + rows),
            bf16(rows * cols + rows), bf16(3, cols), bf16(5), bf16(5),
        ),
        [],
        16,
        1_000_000,
        1_000_000,
        activations[0],
        cotangent,
    )

    def moved(message, by, flip):
        pairs = [
            (2 * c + s, 2 * (c + by) + (1 - s if flip else s))
            for c in range(chan)
            for s in range(2)
            if 0 <= c + by < chan
        ]
        return lax.ppermute(message, ("chan", "space"), pairs)

    from_left = moved(to_right, 1, False)
    from_right = moved(to_left, -1, False)
    from_dl = moved(to_dr, 1, True)
    from_dr = moved(to_dl, -1, True)
    from_side = moved(to_side, 0, True)
    pieces = [x_own, from_left]
    for d in range(2, chan - 1):
        pieces.append(lax.ppermute(x_own, "chan", [(i, (i + d) % chan) for i in range(chan)]))
    pieces.append(from_right)
    pieces.append(lax.ppermute(x_own, "chan", [(0, chan - 1), (chan - 1, 0)]))

    def gathered(wrapped, parts):
        half = call(
            functools.partial(collect_kernel, wrapped),
            bf16(rows, width),
            [],
            16,
            1_000_000,
            1_000_000,
            *parts,
        )
        return half, lax.ppermute(half, "space", [(0, 1), (1, 0)])

    slope_w, payload = call(
        functools.partial(first_kernel, frames),
        (jax.ShapeDtypeStruct((win, channels), F32), bf16(rows, cols)),
        [
            pltpu.VMEM((rows + 4, cols + 4) + cell, BF16),
            pltpu.VMEM((rows + 2, cols + 2) + cell, BF16),
            pltpu.VMEM((rows + 2, cols + 2) + cell, BF16),
        ],
        20,
        2 * win * 18 * channels * channels,
        4_000_000,
        x_own, cot_own, from_left, from_right, from_side, from_dl, from_dr, w, tw,
    )

    padded = pltpu.VMEM((height + 2, width + 2) + cell, BF16)
    hg_win = pltpu.VMEM((rows + 2, cols + 2) + cell, BF16)
    for tick in range(depth - 1):
        if tick:
            payload = call(
                functools.partial(tick_kernel, frames),
                bf16(rows, cols),
                [padded, hg_win],
                large,
                2 * win * 12 * channels * channels,
                4_000_000,
                *g_all, cot_own, slope_w, w, tw,
            )
        arrived = []
        for d in range(chan):
            pairs = [
                (c * depth + p, (c + d) % chan * depth + (p - 1) % depth)
                for p in range(depth)
                for c in range(chan)
            ]
            arrived.append(lax.ppermute(payload, ("chan", "pipe"), pairs))
        g_all = gathered(0, arrived)

    x_all = gathered(1, pieces)
    act_t, x_t, slope_s = call(
        functools.partial(tile_kernel, share),
        (
            jax.ShapeDtypeStruct((channels, count), BF16),
            jax.ShapeDtypeStruct((channels, count), BF16),
            jax.ShapeDtypeStruct((count, share), F32),
        ),
        [padded],
        large,
        2 * count * 9 * channels * channels,
        6_000_000,
        *x_all,
        w,
    )
    grads, space_grad, time_grad = call(
        functools.partial(final_kernel, frames),
        (
            jax.ShapeDtypeStruct((clips, frames, rows, cols, channels), BF16),
            jax.ShapeDtypeStruct((9, share, channels), F32),
            jax.ShapeDtypeStruct((3, share, channels), F32),
        ),
        [
            padded,
            hg_win,
            pltpu.VMEM((height + 2, width + 2, steps, share), BF16),
            pltpu.VMEM((count, 9 * share), BF16),
            pltpu.VMEM((count, 3 * share), BF16),
            pltpu.VMEM((4 * share, channels), BF16),
        ],
        large,
        4 * win * 9 * channels * channels,
        8_000_000,
        *g_all, slope_w, slope_s, act_t, x_t, w, tw,
    )
    return (
        grads[None],
        jnp.swapaxes(space_grad, 1, 2).reshape(3, 3, channels, share)[None],
        jnp.swapaxes(time_grad, 1, 2)[None],
    )


def solution(mesh):
    return jax.shard_map(
        per_device,
        mesh=mesh,
        in_specs=(
            P("pipe", "groups", None, "space", "chan", None),
            P("groups", None, "space", "chan", None),
            P("pipe", None, None, None, None),
            P("pipe", None, None, None),
        ),
        out_specs=(
            P("pipe", "groups", None, "space", "chan", None),
            P("pipe", "groups", None, None, "chan"),
            P("pipe", "groups", None, "chan"),
        ),
        check_vma=False,
    )
```

```python
import functools

import jax
import jax.numpy as jnp
from jax import lax
from jax.experimental import pallas as pl
from jax.experimental.pallas import tpu as pltpu
from jax.sharding import PartitionSpec as P

F32 = jnp.float32
BF16 = jnp.bfloat16
MIB = 1024 * 1024
ROWS_IN = (((1,), (1,)), ((), ()))


def dot(left, right):
    return jnp.dot(left, right, preferred_element_type=F32)


def dot_back(left, right):
    return lax.dot_general(left, right, ROWS_IN, preferred_element_type=F32)


def frame_shift(term, lag, frames):
    rows = term.shape[0]
    moved = pltpu.roll(term, rows - lag, 0)
    frame = lax.broadcasted_iota(jnp.int32, term.shape, 0) % frames
    return jnp.where(frame < frames - lag, moved, 0.0)


def slope_of(hidden):
    sig = jax.nn.sigmoid(hidden)
    return sig * (1.0 + hidden * (1.0 - sig))


def pack_kernel(both_ref, xc_ref, cc_ref, right_ref, left_ref):
    rows, cols, steps, channels = xc_ref.shape
    for n, dst in enumerate((xc_ref, cc_ref)):
        for r in range(rows):
            dst[r] = jnp.swapaxes(both_ref[n, :, :, r].reshape(steps, cols, channels), 0, 1)
    cells = rows * cols
    for msg, col in ((right_ref, cols - 1), (left_ref, 0)):
        msg[:cells] = xc_ref[...].reshape(cells, steps, channels)
        for r in range(rows):
            msg[cells + r] = cc_ref[r, col]


def weights_kernel(share, w_in, tw_in, after_ref, w_ref, tw_ref, pick_ref):
    channels = w_ref.shape[-1]
    w_ref[...] = w_in[...]
    tw_ref[...] = tw_in[...]
    first = pl.multiple_of(lax.axis_index("chan") * share, share)
    for lag in range(3):
        pick_ref[lag * share : (lag + 1) * share, :] = tw_in[lag, pl.ds(first, share), :]
    at = lax.broadcasted_iota(jnp.int32, (share, channels), 1) - first
    chosen = at == lax.broadcasted_iota(jnp.int32, (share, channels), 0)
    pick_ref[3 * share :, :] = jnp.where(chosen, 1.0, 0.0).astype(BF16)


def side_kernel(x_ref, cot_ref, l_ref, r_ref, after_ref, side_ref):
    rows, cols = x_ref.shape[:2]
    cells = rows * cols
    bottom = lax.axis_index("space")
    for i in range(2):
        row = (1 - bottom) * (rows - 2) + i
        base = i * (cols + 4)
        side_ref[base : base + 2] = l_ref[pl.ds(row * cols + cols - 2, 2)]
        side_ref[base + 2 : base + 2 + cols] = x_ref[row]
        side_ref[base + 2 + cols : base + 4 + cols] = r_ref[pl.ds(row * cols, 2)]
    row = (1 - bottom) * (rows - 1)
    base = 2 * (cols + 4)
    side_ref[base] = l_ref[cells + row]
    side_ref[base + 1 : base + 1 + cols] = cot_ref[row]
    side_ref[base + 1 + cols] = r_ref[cells + row]


def conv_back(hg_ref, w_ref, rows, cols):
    channels = w_ref.shape[-1]
    conv = None
    for u in range(3):
        for v in range(3):
            piece = hg_ref[2 - u : 2 - u + rows, 2 - v : 2 - v + cols]
            term = dot_back(piece.reshape(-1, channels), w_ref[3 * u + v])
            conv = term if conv is None else conv + term
    return conv


def window_grad(window, slope_ref, tw_ref, hg_ref, frames):
    act = dot_back(window, tw_ref[0])
    for lag in (1, 2):
        act = act + frame_shift(dot_back(window, tw_ref[lag]), lag, frames)
    hg_ref[...] = (act * slope_ref[...]).astype(BF16).reshape(hg_ref.shape)


def send_on(out_ref, own, conv, cot_ref):
    first = lax.axis_index("pipe") == 0

    @pl.when(first)
    def _():
        out_ref[...] = cot_ref[...]

    @pl.when(jnp.logical_not(first))
    def _():
        out_ref[...] = (own.astype(F32) + conv).astype(BF16).reshape(out_ref.shape)


def first_kernel(
    frames, x_ref, cot_ref, l_ref, r_ref, side_ref, w_ref, tw_ref,
    slope_ref, out_ref, xw_ref, cw_ref, hg_ref,
):
    rows, cols, steps, channels = x_ref.shape
    cells = rows * cols
    bottom = lax.axis_index("space")
    xw_ref[2 : 2 + rows, 2 : 2 + cols] = x_ref[...]
    cw_ref[1 : 1 + rows, 1 : 1 + cols] = cot_ref[...]
    for r in range(rows):
        xw_ref[2 + r, 0:2] = l_ref[r * cols + cols - 2 : r * cols + cols]
        xw_ref[2 + r, cols + 2 : cols + 4] = r_ref[r * cols : r * cols + 2]
        cw_ref[1 + r, 0] = l_ref[cells + r]
        cw_ref[1 + r, cols + 1] = r_ref[cells + r]
    near = (1 - bottom) * (rows + 2)
    far = bottom * (rows + 2)
    for i in range(2):
        xw_ref[near + i] = side_ref[i * (cols + 4) : (i + 1) * (cols + 4)]
        xw_ref[far + i] = jnp.zeros(xw_ref.shape[1:], BF16)
    near = (1 - bottom) * (rows + 1)
    far = bottom * (rows + 1)
    cw_ref[near] = side_ref[2 * (cols + 4) :]
    cw_ref[far] = jnp.zeros(cw_ref.shape[1:], BF16)
    hidden = None
    for u in range(3):
        for v in range(3):
            piece = xw_ref[u : u + rows + 2, v : v + cols + 2]
            term = dot(piece.reshape(-1, channels), w_ref[3 * u + v])
            hidden = term if hidden is None else hidden + term
    slope_ref[...] = slope_of(hidden)
    window_grad(cw_ref[...].reshape(-1, channels), slope_ref, tw_ref, hg_ref, frames)
    conv = conv_back(hg_ref, w_ref, rows, cols)
    send_on(out_ref, cot_ref[...].reshape(-1, channels), conv, cot_ref)


def collect_kernel(wrapped, extra, *refs):
    pieces, out_ref = refs[: -1 - extra], refs[-1]
    chan = len(pieces) - wrapped
    rows, cols, steps, channels = pieces[0].shape
    me = lax.axis_index("chan")

    def put(d, piece):
        place = lax.rem(me - d + chan, chan) * cols
        for r in range(rows):
            out_ref[r, pl.ds(place, cols)] = (
                piece[r] if piece.ndim == 4 else piece[r * cols : (r + 1) * cols]
            )

    for d in range(chan):
        if not wrapped or d not in (1, chan - 1):
            put(d, pieces[d])
    if wrapped:
        edge = pieces[chan]
        for d, at in ((1, 0), (chan - 1, chan - 1)):
            pl.when(me == at)(functools.partial(put, d, edge))
            pl.when(me != at)(functools.partial(put, d, pieces[d]))


def fill_padded(padded, own, other):
    rows_all, cols_all, steps, channels = padded.shape
    zero_row = jnp.zeros((1, cols_all, steps, channels), padded.dtype)
    padded[0:1] = zero_row
    padded[rows_all - 1 :] = zero_row
    for r in range(1, rows_all - 1):
        for c in (0, cols_all - 1):
            padded[r, c] = jnp.zeros((steps, channels), padded.dtype)
    rows = own.shape[0]
    bottom = lax.axis_index("space")
    for half, top in ((own, bottom * rows), (other, (1 - bottom) * rows)):
        padded[pl.ds(1 + top, rows), 1 : cols_all - 1] = half[...]


def own_window(gp_ref, slope_ref, w_ref, tw_ref, hg_ref, frames, rows, cols):
    channels = w_ref.shape[-1]
    r0 = lax.axis_index("space") * rows
    c0 = lax.axis_index("chan") * cols
    window = gp_ref[pl.ds(r0, rows + 2), pl.ds(c0, cols + 2)].reshape(-1, channels)
    window_grad(window, slope_ref, tw_ref, hg_ref, frames)
    own = gp_ref[pl.ds(r0 + 1, rows), pl.ds(c0 + 1, cols)].reshape(-1, channels)
    return own, conv_back(hg_ref, w_ref, rows, cols)


def tick_kernel(
    frames, g_ref, other_ref, cot_ref, slope_ref, w_ref, tw_ref, out_ref, gp_ref, hg_ref
):
    rows, cols = cot_ref.shape[:2]
    fill_padded(gp_ref, g_ref, other_ref)
    own, conv = own_window(gp_ref, slope_ref, w_ref, tw_ref, hg_ref, frames, rows, cols)
    send_on(out_ref, own, conv, cot_ref)


def tile_kernel(share, x_ref, other_ref, w_ref, after_ref, act_ref, xt_ref, slope_ref, xp_ref):
    rows, width, steps, channels = x_ref.shape
    fill_padded(xp_ref, x_ref, other_ref)
    span = width * steps
    turn = lax.rem(channels - lax.axis_index("chan") * share, channels)
    for i in range(2 * rows):
        hidden = None
        for u in range(3):
            for v in range(3):
                piece = xp_ref[i + u, v : v + width].reshape(-1, channels)
                term = dot(piece, w_ref[3 * u + v])
                hidden = term if hidden is None else hidden + term
        active = (hidden * jax.nn.sigmoid(hidden)).astype(BF16)
        act_ref[:, i * span : (i + 1) * span] = active.T
        slope_ref[i * span : (i + 1) * span, :] = slope_of(pltpu.roll(hidden, turn, 1)[:, :share])
        xt_ref[:, i * span : (i + 1) * span] = xp_ref[i + 1, 1 : 1 + width].reshape(-1, channels).T


def final_kernel(
    frames, g_ref, other_ref, slope_w_ref, slope_s_ref, act_ref, xt_ref, w_ref, tw_ref, pick_ref,
    out_ref, space_ref, time_ref, gp_ref, hg_ref, hs_ref, hcols_ref, gcols_ref,
):
    rows, width, steps, channels = g_ref.shape
    clips, _, _, cols, _ = out_ref.shape
    share = slope_s_ref.shape[1]
    height = 2 * rows
    span = width * steps
    fill_padded(gp_ref, g_ref, other_ref)
    hs_ref[...] = jnp.zeros(hs_ref.shape, BF16)
    for i in range(height):
        block = gp_ref[i + 1, 1 : 1 + width].reshape(-1, channels)
        mixed = dot_back(block, pick_ref[...])
        act = mixed[:, :share]
        for lag in (1, 2):
            act = act + frame_shift(mixed[:, lag * share : (lag + 1) * share], lag, frames)
        grad = (act * slope_s_ref[i * span : (i + 1) * span, :]).astype(BF16)
        hs_ref[i + 1, 1 : 1 + width] = grad.reshape(width, steps, share)
        own = mixed[:, 3 * share :]
        for lag in range(3):
            shifted = own if lag == 0 else frame_shift(own, lag, frames)
            gcols_ref[i * span : (i + 1) * span, lag * share : (lag + 1) * share] = shifted.astype(
                BF16
            )
    for u in range(3):
        for v in range(3):
            tap = 3 * u + v
            for i in range(height):
                hcols_ref[i * span : (i + 1) * span, tap * share : (tap + 1) * share] = hs_ref[
                    i + 2 - u, 2 - v : 2 - v + width
                ].reshape(-1, share)
    time_ref[...] = dot(act_ref[...], gcols_ref[...]).T.reshape(time_ref.shape)
    space_ref[...] = dot(xt_ref[...], hcols_ref[...]).T.reshape(space_ref.shape)
    own, conv = own_window(gp_ref, slope_w_ref, w_ref, tw_ref, hg_ref, frames, rows, cols)
    grads = (own.astype(F32) + conv).astype(BF16).reshape(rows, cols, steps, channels)
    for r in range(rows):
        out_ref[:, :, r] = jnp.swapaxes(grads[r], 0, 1).reshape(clips, frames, cols, channels)


VM = pltpu.VMEM


def call(kernel, outs, scratch, limit, flops, moved, *operands, places=None):
    places = places or [VM] * len(operands)
    return pl.pallas_call(
        kernel,
        out_shape=outs,
        in_specs=[pl.BlockSpec(memory_space=place) for place in places],
        scratch_shapes=scratch,
        compiler_params=pltpu.CompilerParams(vmem_limit_bytes=limit * MIB),
        cost_estimate=pl.CostEstimate(flops=flops, bytes_accessed=moved, transcendentals=0),
    )(*operands)


def per_device(activations, cotangent, space_weight, time_weight):
    clips, frames, rows, cols, channels = activations.shape[1:]
    steps = clips * frames
    chan, depth = lax.axis_size("chan"), lax.axis_size("pipe")
    share = channels // chan
    height, width = 2 * rows, chan * cols
    count = height * width * steps
    win = (rows + 2) * (cols + 2) * steps
    large = 24 if chan <= 4 else 56
    cell = (steps, channels)

    def bf16(*shape):
        return jax.ShapeDtypeStruct(shape + cell, BF16)

    beside = rows * cols + rows
    x_own, cot_own, to_right, to_left = call(
        pack_kernel,
        (bf16(rows, cols), bf16(rows, cols), bf16(beside), bf16(beside)),
        [],
        16,
        1_000_000,
        1_000_000,
        jnp.stack([activations[0], cotangent]),
    )
    w, tw, pick = call(
        functools.partial(weights_kernel, share),
        (
            jax.ShapeDtypeStruct((9, channels, channels), BF16),
            jax.ShapeDtypeStruct((3, channels, channels), BF16),
            jax.ShapeDtypeStruct((4 * share, channels), BF16),
        ),
        [],
        16,
        1_000_000,
        3_000_000,
        space_weight[0].reshape(9, channels, channels),
        time_weight[0],
        x_own,
        places=[VM, VM, pl.ANY],
    )

    def along(message, by):
        return lax.ppermute(
            message, "chan", [(c, c + by) for c in range(chan) if 0 <= c + by < chan]
        )

    from_left = along(to_right, 1)
    from_right = along(to_left, -1)
    pieces = [x_own, from_left]
    for d in range(2, chan - 1):
        pieces.append(lax.ppermute(x_own, "chan", [(i, (i + d) % chan) for i in range(chan)]))
    pieces.append(from_right)
    pieces.append(lax.ppermute(x_own, "chan", [(0, chan - 1), (chan - 1, 0)]))
    to_side = call(
        side_kernel,
        bf16(2 * (cols + 4) + cols + 2),
        [],
        16,
        1_000_000,
        1_000_000,
        x_own, cot_own, from_left, from_right, pick,
        places=[VM] * 4 + [pl.ANY],
    )
    from_side = lax.ppermute(to_side, "space", [(0, 1), (1, 0)])

    def gathered(wrapped, parts, after=()):
        half = call(
            functools.partial(collect_kernel, wrapped, len(after)),
            bf16(rows, width),
            [],
            16,
            1_000_000,
            1_000_000,
            *parts,
            *after,
            places=[VM] * len(parts) + [pl.ANY] * len(after),
        )
        return half, lax.ppermute(half, "space", [(0, 1), (1, 0)])

    slope_w, payload = call(
        functools.partial(first_kernel, frames),
        (jax.ShapeDtypeStruct((win, channels), F32), bf16(rows, cols)),
        [
            pltpu.VMEM((rows + 4, cols + 4) + cell, BF16),
            pltpu.VMEM((rows + 2, cols + 2) + cell, BF16),
            pltpu.VMEM((rows + 2, cols + 2) + cell, BF16),
        ],
        20,
        2 * win * 18 * channels * channels,
        4_000_000,
        x_own, cot_own, from_left, from_right, from_side, w, tw,
    )

    padded = pltpu.VMEM((height + 2, width + 2) + cell, BF16)
    hg_win = pltpu.VMEM((rows + 2, cols + 2) + cell, BF16)
    for tick in range(depth - 1):
        if tick:
            payload = call(
                functools.partial(tick_kernel, frames),
                bf16(rows, cols),
                [padded, hg_win],
                large,
                2 * win * 12 * channels * channels,
                4_000_000,
                *g_all, cot_own, slope_w, w, tw,
            )
        arrived = []
        for d in range(chan):
            pairs = [
                (c * depth + p, (c + d) % chan * depth + (p - 1) % depth)
                for p in range(depth)
                for c in range(chan)
            ]
            arrived.append(lax.ppermute(payload, ("chan", "pipe"), pairs))
        if not tick:
            x_all = gathered(1, pieces, (payload,))
            act_t, x_t, slope_s = call(
                functools.partial(tile_kernel, share),
                (
                    jax.ShapeDtypeStruct((channels, count), BF16),
                    jax.ShapeDtypeStruct((channels, count), BF16),
                    jax.ShapeDtypeStruct((count, share), F32),
                ),
                [padded],
                large,
                2 * count * 9 * channels * channels,
                6_000_000,
                *x_all,
                w,
                arrived[0],
                places=[VM, VM, VM, pl.ANY],
            )
        g_all = gathered(0, arrived, () if tick else (slope_s,))
    grads, space_grad, time_grad = call(
        functools.partial(final_kernel, frames),
        (
            jax.ShapeDtypeStruct((clips, frames, rows, cols, channels), BF16),
            jax.ShapeDtypeStruct((9, share, channels), F32),
            jax.ShapeDtypeStruct((3, share, channels), F32),
        ),
        [
            padded,
            hg_win,
            pltpu.VMEM((height + 2, width + 2, steps, share), BF16),
            pltpu.VMEM((count, 9 * share), BF16),
            pltpu.VMEM((count, 3 * share), BF16),
        ],
        large,
        4 * win * 9 * channels * channels,
        8_000_000,
        *g_all, slope_w, slope_s, act_t, x_t, w, tw, pick,
    )
    return (
        grads[None],
        jnp.swapaxes(space_grad, 1, 2).reshape(3, 3, channels, share)[None],
        jnp.swapaxes(time_grad, 1, 2)[None],
    )


def solution(mesh):
    return jax.shard_map(
        per_device,
        mesh=mesh,
        in_specs=(
            P("pipe", "groups", None, "space", "chan", None),
            P("groups", None, "space", "chan", None),
            P("pipe", None, None, None, None),
            P("pipe", None, None, None),
        ),
        out_specs=(
            P("pipe", "groups", None, "space", "chan", None),
            P("pipe", "groups", None, None, "chan"),
            P("pipe", "groups", None, "chan"),
        ),
        check_vma=False,
    )
```

```python
import functools

import jax
import jax.numpy as jnp
from jax import lax
from jax.experimental import pallas as pl
from jax.experimental.pallas import tpu as pltpu
from jax.sharding import PartitionSpec as P

F32 = jnp.float32
BF16 = jnp.bfloat16
MIB = 1024 * 1024
ROWS_IN = (((1,), (1,)), ((), ()))


def dot(left, right):
    return jnp.dot(left, right, preferred_element_type=F32)


def dot_back(left, right):
    return lax.dot_general(left, right, ROWS_IN, preferred_element_type=F32)


def frame_shift(term, lag, frames):
    rows = term.shape[0]
    moved = pltpu.roll(term, rows - lag, 0)
    frame = lax.broadcasted_iota(jnp.int32, term.shape, 0) % frames
    return jnp.where(frame < frames - lag, moved, 0.0)


def slope_of(hidden):
    sig = jax.nn.sigmoid(hidden)
    return sig * (1.0 + hidden * (1.0 - sig))


def pack_kernel(both_ref, xc_ref, cc_ref, right_ref, left_ref):
    rows, cols, steps, channels = xc_ref.shape
    for n, dst in enumerate((xc_ref, cc_ref)):
        for r in range(rows):
            dst[r] = jnp.swapaxes(both_ref[n, :, :, r].reshape(steps, cols, channels), 0, 1)
    cells = rows * cols
    for msg, col in ((right_ref, cols - 1), (left_ref, 0)):
        msg[:cells] = xc_ref[...].reshape(cells, steps, channels)
        for r in range(rows):
            msg[cells + r] = cc_ref[r, col]


def weights_kernel(share, w_in, tw_in, after_ref, w_ref, tw_ref, pick_ref):
    channels = w_ref.shape[-1]
    w_ref[...] = w_in[...]
    tw_ref[...] = tw_in[...]
    first = pl.multiple_of(lax.axis_index("chan") * share, share)
    for lag in range(3):
        pick_ref[lag * share : (lag + 1) * share, :] = tw_in[lag, pl.ds(first, share), :]
    at = lax.broadcasted_iota(jnp.int32, (share, channels), 1) - first
    chosen = at == lax.broadcasted_iota(jnp.int32, (share, channels), 0)
    pick_ref[3 * share :, :] = jnp.where(chosen, 1.0, 0.0).astype(BF16)


def side_kernel(*refs):
    pieces, (cot_ref, _, side_ref) = refs[:-3], refs[-3:]
    rows, cols, steps, channels = pieces[0].shape
    cells = rows * cols
    for d, piece in enumerate(pieces):
        block = piece[...].reshape(cells, steps, channels) if d == 0 else piece[:cells]
        side_ref[d * cells : (d + 1) * cells] = block
    row = (1 - lax.axis_index("space")) * (rows - 1)
    base = len(pieces) * cells
    side_ref[base] = pieces[1][cells + row]
    side_ref[base + 1 : base + 1 + cols] = cot_ref[row]
    side_ref[base + 1 + cols] = pieces[-1][cells + row]


def conv_back(hg_ref, w_ref, rows, cols):
    channels = w_ref.shape[-1]
    conv = None
    for u in range(3):
        for v in range(3):
            piece = hg_ref[2 - u : 2 - u + rows, 2 - v : 2 - v + cols]
            term = dot_back(piece.reshape(-1, channels), w_ref[3 * u + v])
            conv = term if conv is None else conv + term
    return conv


def window_grad(window, slope_ref, tw_ref, hg_ref, frames):
    act = dot_back(window, tw_ref[0])
    for lag in (1, 2):
        act = act + frame_shift(dot_back(window, tw_ref[lag]), lag, frames)
    hg_ref[...] = (act * slope_ref[...]).astype(BF16).reshape(hg_ref.shape)


def send_on(out_ref, own, conv, cot_ref):
    first = lax.axis_index("pipe") == 0

    @pl.when(first)
    def _():
        out_ref[...] = cot_ref[...]

    @pl.when(jnp.logical_not(first))
    def _():
        out_ref[...] = (own.astype(F32) + conv).astype(BF16).reshape(out_ref.shape)


def first_kernel(
    frames, x_ref, cot_ref, l_ref, r_ref, side_ref, w_ref, tw_ref,
    slope_ref, out_ref, xw_ref, cw_ref, hg_ref,
):
    rows, cols, steps, channels = x_ref.shape
    cells = rows * cols
    chan = side_ref.shape[0] // cells
    bottom = lax.axis_index("space")
    xw_ref[2 : 2 + rows, 2 : 2 + cols] = x_ref[...]
    cw_ref[1 : 1 + rows, 1 : 1 + cols] = cot_ref[...]
    for r in range(rows):
        xw_ref[2 + r, 0:2] = l_ref[r * cols + cols - 2 : r * cols + cols]
        xw_ref[2 + r, cols + 2 : cols + 4] = r_ref[r * cols : r * cols + 2]
        cw_ref[1 + r, 0] = l_ref[cells + r]
        cw_ref[1 + r, cols + 1] = r_ref[cells + r]
    near = (1 - bottom) * (rows + 2)
    far = bottom * (rows + 2)
    for i in range(2):
        at = (bottom * (rows - 2) + i) * cols
        xw_ref[near + i, 2 : 2 + cols] = side_ref[pl.ds(at, cols)]
        xw_ref[near + i, 0:2] = side_ref[pl.ds(cells + at + cols - 2, 2)]
        xw_ref[near + i, cols + 2 : cols + 4] = side_ref[pl.ds((chan - 1) * cells + at, 2)]
        xw_ref[far + i] = jnp.zeros(xw_ref.shape[1:], BF16)
    near = (1 - bottom) * (rows + 1)
    far = bottom * (rows + 1)
    cw_ref[near] = side_ref[chan * cells :]
    cw_ref[far] = jnp.zeros(cw_ref.shape[1:], BF16)
    me = lax.axis_index("chan")
    for end, c in ((0, 0), (chan - 1, cols + 2)):

        @pl.when(me == end)
        def _(c=c):
            xw_ref[:, c : c + 2] = jnp.zeros((rows + 4, 2, steps, channels), BF16)
            edge = min(c, cols + 1)
            cw_ref[:, edge : edge + 1] = jnp.zeros((rows + 2, 1, steps, channels), BF16)

    hidden = None
    for u in range(3):
        for v in range(3):
            piece = xw_ref[u : u + rows + 2, v : v + cols + 2]
            term = dot(piece.reshape(-1, channels), w_ref[3 * u + v])
            hidden = term if hidden is None else hidden + term
    slope_ref[...] = slope_of(hidden)
    window_grad(cw_ref[...].reshape(-1, channels), slope_ref, tw_ref, hg_ref, frames)
    conv = conv_back(hg_ref, w_ref, rows, cols)
    send_on(out_ref, cot_ref[...].reshape(-1, channels), conv, cot_ref)


def collect_kernel(extra, *refs):
    pieces, out_ref = refs[: -1 - extra], refs[-1]
    chan = len(pieces)
    rows, cols, steps, channels = pieces[0].shape
    me = lax.axis_index("chan")
    for d, piece in enumerate(pieces):
        out_ref[:, pl.ds(lax.rem(me - d + chan, chan) * cols, cols)] = piece[...]


def clear_rim(padded):
    rows_all, cols_all, steps, channels = padded.shape
    zero_row = jnp.zeros((1, cols_all, steps, channels), padded.dtype)
    padded[0:1] = zero_row
    padded[rows_all - 1 :] = zero_row
    for r in range(1, rows_all - 1):
        for c in (0, cols_all - 1):
            padded[r, c] = jnp.zeros((steps, channels), padded.dtype)


def fill_padded(padded, own, other):
    clear_rim(padded)
    rows, cols = own.shape[0], own.shape[1]
    bottom = lax.axis_index("space")
    for half, top in ((own, bottom * rows), (other, (1 - bottom) * rows)):
        padded[pl.ds(1 + top, rows), 1 : 1 + cols] = half[...]


def fill_from_pieces(padded, rows, cols, pieces, side):
    clear_rim(padded)
    chan, cells = len(pieces), rows * cols
    me = lax.axis_index("chan")
    bottom = lax.axis_index("space")
    for d, piece in enumerate(pieces):
        place = 1 + lax.rem(me - d + chan, chan) * cols
        for r in range(rows):
            near = piece[r] if d == 0 else piece[r * cols : (r + 1) * cols]
            padded[1 + bottom * rows + r, pl.ds(place, cols)] = near
            at = d * cells + r * cols
            padded[1 + (1 - bottom) * rows + r, pl.ds(place, cols)] = side[at : at + cols]


def own_window(gp_ref, slope_ref, w_ref, tw_ref, hg_ref, frames, rows, cols):
    channels = w_ref.shape[-1]
    r0 = lax.axis_index("space") * rows
    c0 = lax.axis_index("chan") * cols
    window = gp_ref[pl.ds(r0, rows + 2), pl.ds(c0, cols + 2)].reshape(-1, channels)
    window_grad(window, slope_ref, tw_ref, hg_ref, frames)
    own = gp_ref[pl.ds(r0 + 1, rows), pl.ds(c0 + 1, cols)].reshape(-1, channels)
    return own, conv_back(hg_ref, w_ref, rows, cols)


def tick_kernel(
    frames, g_ref, other_ref, cot_ref, slope_ref, w_ref, tw_ref, out_ref, gp_ref, hg_ref
):
    rows, cols = cot_ref.shape[:2]
    fill_padded(gp_ref, g_ref, other_ref)
    own, conv = own_window(gp_ref, slope_ref, w_ref, tw_ref, hg_ref, frames, rows, cols)
    send_on(out_ref, own, conv, cot_ref)


def tile_kernel(chan, *refs):
    pieces, (side, w_ref), (act_ref, xt_ref, slope_ref, xp_ref) = (
        refs[:chan],
        refs[chan : chan + 2],
        refs[-4:],
    )
    rows, cols, steps, channels = pieces[0].shape
    width = chan * cols
    share = channels // chan
    fill_from_pieces(xp_ref, rows, cols, pieces, side)
    span = width * steps
    turn = lax.rem(channels - lax.axis_index("chan") * share, channels)
    for i in range(2 * rows):
        hidden = None
        for u in range(3):
            for v in range(3):
                piece = xp_ref[i + u, v : v + width].reshape(-1, channels)
                term = dot(piece, w_ref[3 * u + v])
                hidden = term if hidden is None else hidden + term
        active = (hidden * jax.nn.sigmoid(hidden)).astype(BF16)
        act_ref[:, i * span : (i + 1) * span] = active.T
        slope_ref[i * span : (i + 1) * span, :] = slope_of(pltpu.roll(hidden, turn, 1)[:, :share])
        xt_ref[:, i * span : (i + 1) * span] = xp_ref[i + 1, 1 : 1 + width].reshape(-1, channels).T


def final_kernel(
    frames, g_ref, other_ref, slope_w_ref, slope_s_ref, act_ref, xt_ref, w_ref, tw_ref, pick_ref,
    out_ref, space_ref, time_ref, gp_ref, hg_ref, hs_ref, hcols_ref, gcols_ref,
):
    rows, width, steps, channels = g_ref.shape
    clips, _, _, cols, _ = out_ref.shape
    share = slope_s_ref.shape[1]
    height = 2 * rows
    span = width * steps
    fill_padded(gp_ref, g_ref, other_ref)
    hs_ref[...] = jnp.zeros(hs_ref.shape, BF16)
    for i in range(height):
        block = gp_ref[i + 1, 1 : 1 + width].reshape(-1, channels)
        mixed = dot_back(block, pick_ref[...])
        act = mixed[:, :share]
        for lag in (1, 2):
            act = act + frame_shift(mixed[:, lag * share : (lag + 1) * share], lag, frames)
        grad = (act * slope_s_ref[i * span : (i + 1) * span, :]).astype(BF16)
        hs_ref[i + 1, 1 : 1 + width] = grad.reshape(width, steps, share)
        own = mixed[:, 3 * share :]
        for lag in range(3):
            shifted = own if lag == 0 else frame_shift(own, lag, frames)
            gcols_ref[i * span : (i + 1) * span, lag * share : (lag + 1) * share] = shifted.astype(
                BF16
            )
    for u in range(3):
        for v in range(3):
            tap = 3 * u + v
            for i in range(height):
                hcols_ref[i * span : (i + 1) * span, tap * share : (tap + 1) * share] = hs_ref[
                    i + 2 - u, 2 - v : 2 - v + width
                ].reshape(-1, share)
    time_ref[...] = dot(act_ref[...], gcols_ref[...]).T.reshape(time_ref.shape)
    space_ref[...] = dot(xt_ref[...], hcols_ref[...]).T.reshape(space_ref.shape)
    own, conv = own_window(gp_ref, slope_w_ref, w_ref, tw_ref, hg_ref, frames, rows, cols)
    grads = (own.astype(F32) + conv).astype(BF16).reshape(rows, cols, steps, channels)
    for r in range(rows):
        out_ref[:, :, r] = jnp.swapaxes(grads[r], 0, 1).reshape(clips, frames, cols, channels)


VM = pltpu.VMEM


def call(kernel, outs, scratch, limit, flops, moved, *operands, places=None):
    places = places or [VM] * len(operands)
    return pl.pallas_call(
        kernel,
        out_shape=outs,
        in_specs=[pl.BlockSpec(memory_space=place) for place in places],
        scratch_shapes=scratch,
        compiler_params=pltpu.CompilerParams(vmem_limit_bytes=limit * MIB),
        cost_estimate=pl.CostEstimate(flops=flops, bytes_accessed=moved, transcendentals=0),
    )(*operands)


def per_device(activations, cotangent, space_weight, time_weight):
    clips, frames, rows, cols, channels = activations.shape[1:]
    steps = clips * frames
    chan, depth = lax.axis_size("chan"), lax.axis_size("pipe")
    share = channels // chan
    height, width = 2 * rows, chan * cols
    count = height * width * steps
    win = (rows + 2) * (cols + 2) * steps
    large = 24 if chan <= 4 else 56
    cell = (steps, channels)

    def bf16(*shape):
        return jax.ShapeDtypeStruct(shape + cell, BF16)

    beside = rows * cols + rows
    x_own, cot_own, to_right, to_left = call(
        pack_kernel,
        (bf16(rows, cols), bf16(rows, cols), bf16(beside), bf16(beside)),
        [],
        16,
        1_000_000,
        1_000_000,
        jnp.stack([activations[0], cotangent]),
    )
    w, tw, pick = call(
        functools.partial(weights_kernel, share),
        (
            jax.ShapeDtypeStruct((9, channels, channels), BF16),
            jax.ShapeDtypeStruct((3, channels, channels), BF16),
            jax.ShapeDtypeStruct((4 * share, channels), BF16),
        ),
        [],
        16,
        1_000_000,
        3_000_000,
        space_weight[0].reshape(9, channels, channels),
        time_weight[0],
        x_own,
        places=[VM, VM, pl.ANY],
    )

    def turned(message, by):
        return lax.ppermute(message, "chan", [(i, (i + by) % chan) for i in range(chan)])

    x_flat = x_own.reshape((rows * cols,) + cell)
    pieces = [
        x_own,
        turned(to_right, 1),
        *[turned(x_flat, d) for d in range(2, chan - 1)],
        turned(to_left, chan - 1),
    ]
    swap = [(0, 1), (1, 0)]
    to_side = call(
        side_kernel,
        bf16(chan * rows * cols + cols + 2),
        [],
        16,
        1_000_000,
        1_000_000,
        *pieces, cot_own, pick,
        places=[VM] * (chan + 1) + [pl.ANY],
    )
    from_side = lax.ppermute(to_side, "space", swap)

    def gathered(parts, after=()):
        half = call(
            functools.partial(collect_kernel, len(after)),
            bf16(rows, width),
            [],
            16,
            1_000_000,
            1_000_000,
            *parts,
            *after,
            places=[VM] * len(parts) + [pl.ANY] * len(after),
        )
        return half, lax.ppermute(half, "space", swap)

    slope_w, payload = call(
        functools.partial(first_kernel, frames),
        (jax.ShapeDtypeStruct((win, channels), F32), bf16(rows, cols)),
        [
            pltpu.VMEM((rows + 4, cols + 4) + cell, BF16),
            pltpu.VMEM((rows + 2, cols + 2) + cell, BF16),
            pltpu.VMEM((rows + 2, cols + 2) + cell, BF16),
        ],
        20,
        2 * win * 18 * channels * channels,
        4_000_000,
        x_own, cot_own, pieces[1], pieces[-1], from_side, w, tw,
    )

    padded = pltpu.VMEM((height + 2, width + 2) + cell, BF16)
    hg_win = pltpu.VMEM((rows + 2, cols + 2) + cell, BF16)
    for tick in range(depth - 1):
        if tick:
            payload = call(
                functools.partial(tick_kernel, frames),
                bf16(rows, cols),
                [padded, hg_win],
                large,
                2 * win * 12 * channels * channels,
                4_000_000,
                *g_all, cot_own, slope_w, w, tw,
            )
        arrived = []
        for d in range(chan):
            pairs = [
                (c * depth + p, (c + d) % chan * depth + (p - 1) % depth)
                for p in range(depth)
                for c in range(chan)
            ]
            arrived.append(lax.ppermute(payload, ("chan", "pipe"), pairs))
        if not tick:
            operands = [*pieces, from_side, w]
            act_t, x_t, slope_s = call(
                functools.partial(tile_kernel, chan),
                (
                    jax.ShapeDtypeStruct((channels, count), BF16),
                    jax.ShapeDtypeStruct((channels, count), BF16),
                    jax.ShapeDtypeStruct((count, share), F32),
                ),
                [padded],
                large,
                2 * count * 9 * channels * channels,
                6_000_000,
                *operands,
                arrived[0],
                places=[VM] * len(operands) + [pl.ANY],
            )
        g_all = gathered(arrived, () if tick else (slope_s,))
    grads, space_grad, time_grad = call(
        functools.partial(final_kernel, frames),
        (
            jax.ShapeDtypeStruct((clips, frames, rows, cols, channels), BF16),
            jax.ShapeDtypeStruct((9, share, channels), F32),
            jax.ShapeDtypeStruct((3, share, channels), F32),
        ),
        [
            padded,
            hg_win,
            pltpu.VMEM((height + 2, width + 2, steps, share), BF16),
            pltpu.VMEM((count, 9 * share), BF16),
            pltpu.VMEM((count, 3 * share), BF16),
        ],
        large,
        4 * win * 9 * channels * channels,
        8_000_000,
        *g_all, slope_w, slope_s, act_t, x_t, w, tw, pick,
    )
    return (
        grads[None],
        jnp.swapaxes(space_grad, 1, 2).reshape(3, 3, channels, share)[None],
        jnp.swapaxes(time_grad, 1, 2)[None],
    )


def solution(mesh):
    return jax.shard_map(
        per_device,
        mesh=mesh,
        in_specs=(
            P("pipe", "groups", None, "space", "chan", None),
            P("groups", None, "space", "chan", None),
            P("pipe", None, None, None, None),
            P("pipe", None, None, None),
        ),
        out_specs=(
            P("pipe", "groups", None, "space", "chan", None),
            P("pipe", "groups", None, None, "chan"),
            P("pipe", "groups", None, "chan"),
        ),
        check_vma=False,
    )
```

```python
import functools

import jax
import jax.numpy as jnp
from jax import lax
from jax.experimental import pallas as pl
from jax.experimental.pallas import tpu as pltpu
from jax.sharding import PartitionSpec as P

F32 = jnp.float32
BF16 = jnp.bfloat16
MIB = 1024 * 1024
ROWS_IN = (((1,), (1,)), ((), ()))


def dot(left, right):
    return jnp.dot(left, right, preferred_element_type=F32)


def dot_back(left, right):
    return lax.dot_general(left, right, ROWS_IN, preferred_element_type=F32)


def frame_shift(term, lag, frames):
    rows = term.shape[0]
    moved = pltpu.roll(term, rows - lag, 0)
    frame = lax.broadcasted_iota(jnp.int32, term.shape, 0) % frames
    return jnp.where(frame < frames - lag, moved, 0.0)


def slope_of(hidden):
    sig = jax.nn.sigmoid(hidden)
    return sig * (1.0 + hidden * (1.0 - sig))


def pack_kernel(both_ref, xc_ref, cc_ref, right_ref, left_ref):
    rows, cols, steps, channels = xc_ref.shape
    for n, dst in enumerate((xc_ref, cc_ref)):
        for r in range(rows):
            dst[r] = jnp.swapaxes(both_ref[n, :, :, r].reshape(steps, cols, channels), 0, 1)
    cells = rows * cols
    for msg, col in ((right_ref, cols - 1), (left_ref, 0)):
        msg[:cells] = xc_ref[...].reshape(cells, steps, channels)
        for r in range(rows):
            msg[cells + r] = cc_ref[r, col]


def weights_kernel(share, w_in, tw_in, after_ref, w_ref, tw_ref, pick_ref):
    channels = w_ref.shape[-1]
    w_ref[...] = w_in[...]
    tw_ref[...] = tw_in[...]
    first = pl.multiple_of(lax.axis_index("chan") * share, share)
    for lag in range(3):
        pick_ref[lag * share : (lag + 1) * share, :] = tw_in[lag, pl.ds(first, share), :]
    at = lax.broadcasted_iota(jnp.int32, (share, channels), 1) - first
    chosen = at == lax.broadcasted_iota(jnp.int32, (share, channels), 0)
    pick_ref[3 * share :, :] = jnp.where(chosen, 1.0, 0.0).astype(BF16)


def side_kernel(x_ref, l_ref, r_ref, cot_ref, after_ref, *side_refs):
    rows, cols = x_ref.shape[:2]
    cells = rows * cols
    bottom = lax.axis_index("space")
    out = [side.at[i] for side in side_refs for i in range(side.shape[0])]
    for i in range(2):
        at = ((1 - bottom) * (rows - 2) + i) * cols
        line = out[i * (cols + 4) : (i + 1) * (cols + 4)]
        for c in range(cols):
            line[2 + c][...] = x_ref[(1 - bottom) * (rows - 2) + i, c]
        for c in range(2):
            line[c][...] = l_ref[at + cols - 2 + c]
            line[2 + cols + c][...] = r_ref[at + c]
    row = (1 - bottom) * (rows - 1)
    line = out[2 * (cols + 4) :]
    line[0][...] = l_ref[cells + row]
    line[1 + cols][...] = r_ref[cells + row]
    for c in range(cols):
        line[1 + c][...] = cot_ref[row, c]


def late_kernel(payload_ref, x_ref, *refs):
    pieces, (out_ref, late_ref) = refs[:-2], refs[-2:]
    out_ref[...] = payload_ref[...]
    rows, cols, steps, channels = x_ref.shape
    cells = rows * cols
    late_ref[:cells] = x_ref[...].reshape(cells, steps, channels)
    for n, piece in enumerate(pieces):
        late_ref[(n + 1) * cells : (n + 2) * cells] = piece[:cells]


def conv_back(hg_ref, w_ref, rows, cols):
    channels = w_ref.shape[-1]
    conv = None
    for u in range(3):
        for v in range(3):
            piece = hg_ref[2 - u : 2 - u + rows, 2 - v : 2 - v + cols]
            term = dot_back(piece.reshape(-1, channels), w_ref[3 * u + v])
            conv = term if conv is None else conv + term
    return conv


def window_grad(window, slope_ref, tw_ref, hg_ref, frames):
    act = dot_back(window, tw_ref[0])
    for lag in (1, 2):
        act = act + frame_shift(dot_back(window, tw_ref[lag]), lag, frames)
    hg_ref[...] = (act * slope_ref[...]).astype(BF16).reshape(hg_ref.shape)


def send_on(out_ref, own, conv, cot_ref):
    first = lax.axis_index("pipe") == 0

    @pl.when(first)
    def _():
        out_ref[...] = cot_ref[...]

    @pl.when(jnp.logical_not(first))
    def _():
        out_ref[...] = (own.astype(F32) + conv).astype(BF16).reshape(out_ref.shape)


def first_kernel(
    frames, x_ref, cot_ref, l_ref, r_ref, side_ref, side2_ref, w_ref, tw_ref,
    slope_ref, out_ref, xw_ref, cw_ref, hg_ref,
):
    rows, cols, steps, channels = x_ref.shape
    cells = rows * cols
    chan = lax.axis_size("chan")
    bottom = lax.axis_index("space")
    xw_ref[2 : 2 + rows, 2 : 2 + cols] = x_ref[...]
    cw_ref[1 : 1 + rows, 1 : 1 + cols] = cot_ref[...]
    for r in range(rows):
        xw_ref[2 + r, 0:2] = l_ref[r * cols + cols - 2 : r * cols + cols]
        xw_ref[2 + r, cols + 2 : cols + 4] = r_ref[r * cols : r * cols + 2]
        cw_ref[1 + r, 0] = l_ref[cells + r]
        cw_ref[1 + r, cols + 1] = r_ref[cells + r]
    near = (1 - bottom) * (rows + 2)
    far = bottom * (rows + 2)
    line = [side.at[i] for side in (side_ref, side2_ref) for i in range(side.shape[0])]
    for i in range(2):
        for c in range(cols + 4):
            xw_ref[near + i, c] = line[i * (cols + 4) + c][...]
        xw_ref[far + i] = jnp.zeros(xw_ref.shape[1:], BF16)
    near = (1 - bottom) * (rows + 1)
    far = bottom * (rows + 1)
    for c in range(cols + 2):
        cw_ref[near, c] = line[2 * (cols + 4) + c][...]
    cw_ref[far] = jnp.zeros(cw_ref.shape[1:], BF16)
    me = lax.axis_index("chan")
    for end, c in ((0, 0), (chan - 1, cols + 2)):

        @pl.when(me == end)
        def _(c=c):
            xw_ref[:, c : c + 2] = jnp.zeros((rows + 4, 2, steps, channels), BF16)
            edge = min(c, cols + 1)
            cw_ref[:, edge : edge + 1] = jnp.zeros((rows + 2, 1, steps, channels), BF16)

    hidden = None
    for u in range(3):
        for v in range(3):
            piece = xw_ref[u : u + rows + 2, v : v + cols + 2]
            term = dot(piece.reshape(-1, channels), w_ref[3 * u + v])
            hidden = term if hidden is None else hidden + term
    slope_ref[...] = slope_of(hidden)
    window_grad(cw_ref[...].reshape(-1, channels), slope_ref, tw_ref, hg_ref, frames)
    conv = conv_back(hg_ref, w_ref, rows, cols)
    send_on(out_ref, cot_ref[...].reshape(-1, channels), conv, cot_ref)


def collect_kernel(extra, *refs):
    pieces, out_ref = refs[: -1 - extra], refs[-1]
    chan = len(pieces)
    rows, cols, steps, channels = pieces[0].shape
    me = lax.axis_index("chan")
    for d, piece in enumerate(pieces):
        out_ref[:, pl.ds(lax.rem(me - d + chan, chan) * cols, cols)] = piece[...]


def clear_rim(padded):
    rows_all, cols_all, steps, channels = padded.shape
    zero_row = jnp.zeros((1, cols_all, steps, channels), padded.dtype)
    padded[0:1] = zero_row
    padded[rows_all - 1 :] = zero_row
    for r in range(1, rows_all - 1):
        for c in (0, cols_all - 1):
            padded[r, c] = jnp.zeros((steps, channels), padded.dtype)


def fill_padded(padded, own, other):
    clear_rim(padded)
    rows, cols = own.shape[0], own.shape[1]
    bottom = lax.axis_index("space")
    for half, top in ((own, bottom * rows), (other, (1 - bottom) * rows)):
        padded[pl.ds(1 + top, rows), 1 : 1 + cols] = half[...]


def fill_from_pieces(padded, rows, cols, pieces, late):
    clear_rim(padded)
    chan, cells = len(pieces), rows * cols
    me = lax.axis_index("chan")
    bottom = lax.axis_index("space")
    for d, piece in enumerate(pieces):
        place = 1 + lax.rem(me - d + chan, chan) * cols
        for r in range(rows):
            near = piece[r] if d == 0 else piece[r * cols : (r + 1) * cols]
            padded[1 + bottom * rows + r, pl.ds(place, cols)] = near
            at = d * cells + r * cols
            padded[1 + (1 - bottom) * rows + r, pl.ds(place, cols)] = late[at : at + cols]


def own_window(gp_ref, slope_ref, w_ref, tw_ref, hg_ref, frames, rows, cols):
    channels = w_ref.shape[-1]
    r0 = lax.axis_index("space") * rows
    c0 = lax.axis_index("chan") * cols
    window = gp_ref[pl.ds(r0, rows + 2), pl.ds(c0, cols + 2)].reshape(-1, channels)
    window_grad(window, slope_ref, tw_ref, hg_ref, frames)
    own = gp_ref[pl.ds(r0 + 1, rows), pl.ds(c0 + 1, cols)].reshape(-1, channels)
    return own, conv_back(hg_ref, w_ref, rows, cols)


def tick_kernel(
    frames, g_ref, other_ref, cot_ref, slope_ref, w_ref, tw_ref, out_ref, gp_ref, hg_ref
):
    rows, cols = cot_ref.shape[:2]
    fill_padded(gp_ref, g_ref, other_ref)
    own, conv = own_window(gp_ref, slope_ref, w_ref, tw_ref, hg_ref, frames, rows, cols)
    send_on(out_ref, own, conv, cot_ref)


def tile_kernel(chan, *refs):
    pieces, (late, w_ref) = refs[:chan], refs[chan : chan + 2]
    act_ref, xt_ref, slope_ref, xp_ref = refs[-4:]
    rows, cols, steps, channels = pieces[0].shape
    width = chan * cols
    share = channels // chan
    fill_from_pieces(xp_ref, rows, cols, pieces, late)
    span = width * steps
    turn = lax.rem(channels - lax.axis_index("chan") * share, channels)
    for i in range(2 * rows):
        hidden = None
        for u in range(3):
            for v in range(3):
                piece = xp_ref[i + u, v : v + width].reshape(-1, channels)
                term = dot(piece, w_ref[3 * u + v])
                hidden = term if hidden is None else hidden + term
        active = (hidden * jax.nn.sigmoid(hidden)).astype(BF16)
        act_ref[:, i * span : (i + 1) * span] = active.T
        slope_ref[i * span : (i + 1) * span, :] = slope_of(pltpu.roll(hidden, turn, 1)[:, :share])
        xt_ref[:, i * span : (i + 1) * span] = xp_ref[i + 1, 1 : 1 + width].reshape(-1, channels).T


def final_kernel(
    frames, g_ref, other_ref, slope_w_ref, slope_s_ref, act_ref, xt_ref, w_ref, tw_ref, pick_ref,
    out_ref, space_ref, time_ref, gp_ref, hg_ref, hs_ref, hcols_ref, gcols_ref,
):
    rows, width, steps, channels = g_ref.shape
    clips, _, _, cols, _ = out_ref.shape
    share = slope_s_ref.shape[1]
    height = 2 * rows
    span = width * steps
    fill_padded(gp_ref, g_ref, other_ref)
    hs_ref[...] = jnp.zeros(hs_ref.shape, BF16)
    for i in range(height):
        block = gp_ref[i + 1, 1 : 1 + width].reshape(-1, channels)
        mixed = dot_back(block, pick_ref[...])
        act = mixed[:, :share]
        for lag in (1, 2):
            act = act + frame_shift(mixed[:, lag * share : (lag + 1) * share], lag, frames)
        grad = (act * slope_s_ref[i * span : (i + 1) * span, :]).astype(BF16)
        hs_ref[i + 1, 1 : 1 + width] = grad.reshape(width, steps, share)
        own = mixed[:, 3 * share :]
        for lag in range(3):
            shifted = own if lag == 0 else frame_shift(own, lag, frames)
            gcols_ref[i * span : (i + 1) * span, lag * share : (lag + 1) * share] = shifted.astype(
                BF16
            )
    for u in range(3):
        for v in range(3):
            tap = 3 * u + v
            for i in range(height):
                hcols_ref[i * span : (i + 1) * span, tap * share : (tap + 1) * share] = hs_ref[
                    i + 2 - u, 2 - v : 2 - v + width
                ].reshape(-1, share)
    time_ref[...] = dot(act_ref[...], gcols_ref[...]).T.reshape(time_ref.shape)
    space_ref[...] = dot(xt_ref[...], hcols_ref[...]).T.reshape(space_ref.shape)
    own, conv = own_window(gp_ref, slope_w_ref, w_ref, tw_ref, hg_ref, frames, rows, cols)
    grads = (own.astype(F32) + conv).astype(BF16).reshape(rows, cols, steps, channels)
    for r in range(rows):
        out_ref[:, :, r] = jnp.swapaxes(grads[r], 0, 1).reshape(clips, frames, cols, channels)


VM = pltpu.VMEM


def call(kernel, outs, scratch, limit, flops, moved, *operands, places=None):
    places = places or [VM] * len(operands)
    return pl.pallas_call(
        kernel,
        out_shape=outs,
        in_specs=[pl.BlockSpec(memory_space=place) for place in places],
        scratch_shapes=scratch,
        compiler_params=pltpu.CompilerParams(vmem_limit_bytes=limit * MIB),
        cost_estimate=pl.CostEstimate(flops=flops, bytes_accessed=moved, transcendentals=0),
    )(*operands)


def per_device(activations, cotangent, space_weight, time_weight):
    clips, frames, rows, cols, channels = activations.shape[1:]
    steps = clips * frames
    chan, depth = lax.axis_size("chan"), lax.axis_size("pipe")
    share = channels // chan
    height, width = 2 * rows, chan * cols
    count = height * width * steps
    win = (rows + 2) * (cols + 2) * steps
    large = 24 if chan <= 4 else 56
    cell = (steps, channels)

    def bf16(*shape):
        return jax.ShapeDtypeStruct(shape + cell, BF16)

    beside = rows * cols + rows
    x_own, cot_own, to_right, to_left = call(
        pack_kernel,
        (bf16(rows, cols), bf16(rows, cols), bf16(beside), bf16(beside)),
        [],
        16,
        1_000_000,
        1_000_000,
        jnp.stack([activations[0], cotangent]),
    )
    w, tw, pick = call(
        functools.partial(weights_kernel, share),
        (
            jax.ShapeDtypeStruct((9, channels, channels), BF16),
            jax.ShapeDtypeStruct((3, channels, channels), BF16),
            jax.ShapeDtypeStruct((4 * share, channels), BF16),
        ),
        [],
        16,
        1_000_000,
        3_000_000,
        space_weight[0].reshape(9, channels, channels),
        time_weight[0],
        x_own,
        places=[VM, VM, pl.ANY],
    )

    def turned(message, by):
        return lax.ppermute(message, "chan", [(i, (i + by) % chan) for i in range(chan)])

    x_flat = x_own.reshape((rows * cols,) + cell)
    pieces = [
        x_own,
        turned(to_right, 1),
        *[turned(x_flat, d) for d in range(2, chan - 1)],
        turned(to_left, chan - 1),
    ]
    swap = [(0, 1), (1, 0)]
    half_side = (2 * (cols + 4) + cols + 2) // 2
    to_side = call(
        side_kernel,
        (bf16(half_side), bf16(2 * (cols + 4) + cols + 2 - half_side)),
        [],
        16,
        1_000_000,
        1_000_000,
        x_own, pieces[1], pieces[-1], cot_own, pick,
        places=[VM] * 4 + [pl.ANY],
    )
    from_side = [lax.ppermute(part, "space", swap) for part in to_side]

    def gathered(parts, after=()):
        half = call(
            functools.partial(collect_kernel, len(after)),
            bf16(rows, width),
            [],
            16,
            1_000_000,
            1_000_000,
            *parts,
            *after,
            places=[VM] * len(parts) + [pl.ANY] * len(after),
        )
        return half, lax.ppermute(half, "space", swap)

    slope_w, payload = call(
        functools.partial(first_kernel, frames),
        (jax.ShapeDtypeStruct((win, channels), F32), bf16(rows, cols)),
        [
            pltpu.VMEM((rows + 4, cols + 4) + cell, BF16),
            pltpu.VMEM((rows + 2, cols + 2) + cell, BF16),
            pltpu.VMEM((rows + 2, cols + 2) + cell, BF16),
        ],
        20,
        1,
        1,
        x_own, cot_own, pieces[1], pieces[-1], *from_side, w, tw,
    )

    padded = pltpu.VMEM((height + 2, width + 2) + cell, BF16)
    hg_win = pltpu.VMEM((rows + 2, cols + 2) + cell, BF16)
    for tick in range(depth - 1):
        if tick:
            payload = call(
                functools.partial(tick_kernel, frames),
                bf16(rows, cols),
                [padded, hg_win],
                large,
                2 * win * 12 * channels * channels,
                4_000_000,
                *g_all, cot_own, slope_w, w, tw,
            )
        if not tick:
            payload, to_late = call(
                late_kernel,
                (bf16(rows, cols), bf16(chan * rows * cols)),
                [],
                16,
                1_000_000,
                1_000_000,
                payload,
                *pieces,
            )
            from_late = lax.ppermute(to_late, "space", swap)
        arrived = []
        for d in range(chan):
            pairs = [
                (c * depth + p, (c + d) % chan * depth + (p - 1) % depth)
                for p in range(depth)
                for c in range(chan)
            ]
            arrived.append(lax.ppermute(payload, ("chan", "pipe"), pairs))
        if not tick:
            operands = [*pieces, from_late, w]
            act_t, x_t, slope_s = call(
                functools.partial(tile_kernel, chan),
                (
                    jax.ShapeDtypeStruct((channels, count), BF16),
                    jax.ShapeDtypeStruct((channels, count), BF16),
                    jax.ShapeDtypeStruct((count, share), F32),
                ),
                [padded],
                large,
                2 * count * 9 * channels * channels,
                6_000_000,
                *operands,
                arrived[0],
                places=[VM] * len(operands) + [pl.ANY],
            )
        g_all = gathered(arrived, () if tick else (slope_s,))
    grads, space_grad, time_grad = call(
        functools.partial(final_kernel, frames),
        (
            jax.ShapeDtypeStruct((clips, frames, rows, cols, channels), BF16),
            jax.ShapeDtypeStruct((9, share, channels), F32),
            jax.ShapeDtypeStruct((3, share, channels), F32),
        ),
        [
            padded,
            hg_win,
            pltpu.VMEM((height + 2, width + 2, steps, share), BF16),
            pltpu.VMEM((count, 9 * share), BF16),
            pltpu.VMEM((count, 3 * share), BF16),
        ],
        large,
        4 * win * 9 * channels * channels,
        8_000_000,
        *g_all, slope_w, slope_s, act_t, x_t, w, tw, pick,
    )
    return (
        grads[None],
        jnp.swapaxes(space_grad, 1, 2).reshape(3, 3, channels, share)[None],
        jnp.swapaxes(time_grad, 1, 2)[None],
    )


def solution(mesh):
    return jax.shard_map(
        per_device,
        mesh=mesh,
        in_specs=(
            P("pipe", "groups", None, "space", "chan", None),
            P("groups", None, "space", "chan", None),
            P("pipe", None, None, None, None),
            P("pipe", None, None, None),
        ),
        out_specs=(
            P("pipe", "groups", None, "space", "chan", None),
            P("pipe", "groups", None, None, "chan"),
            P("pipe", "groups", None, "chan"),
        ),
        check_vma=False,
    )
```

```python
import functools

import jax
import jax.numpy as jnp
from jax import lax
from jax.experimental import pallas as pl
from jax.experimental.pallas import tpu as pltpu
from jax.sharding import PartitionSpec as P

F32 = jnp.float32
BF16 = jnp.bfloat16
MIB = 1024 * 1024
ROWS_IN = (((1,), (1,)), ((), ()))


def dot(left, right):
    return jnp.dot(left, right, preferred_element_type=F32)


def dot_back(left, right):
    return lax.dot_general(left, right, ROWS_IN, preferred_element_type=F32)


def frame_shift(term, lag, frames):
    rows = term.shape[0]
    moved = pltpu.roll(term, rows - lag, 0)
    frame = lax.broadcasted_iota(jnp.int32, term.shape, 0) % frames
    return jnp.where(frame < frames - lag, moved, 0.0)


def slope_of(hidden):
    sig = jax.nn.sigmoid(hidden)
    return sig * (1.0 + hidden * (1.0 - sig))


def pack_kernel(both_ref, xc_ref, cc_ref, right_ref, left_ref):
    rows, cols, steps, channels = xc_ref.shape
    for n, dst in enumerate((xc_ref, cc_ref)):
        for r in range(rows):
            dst[r] = jnp.swapaxes(both_ref[n, :, :, r].reshape(steps, cols, channels), 0, 1)
    cells = rows * cols
    for msg, col in ((right_ref, cols - 1), (left_ref, 0)):
        msg[:cells] = xc_ref[...].reshape(cells, steps, channels)
        for r in range(rows):
            msg[cells + r] = cc_ref[r, col]


def weights_kernel(share, w_in, tw_in, after_ref, w_ref, tw_ref, pick_ref):
    channels = w_ref.shape[-1]
    w_ref[...] = w_in[...]
    tw_ref[...] = tw_in[...]
    first = pl.multiple_of(lax.axis_index("chan") * share, share)
    for lag in range(3):
        pick_ref[lag * share : (lag + 1) * share, :] = tw_in[lag, pl.ds(first, share), :]
    at = lax.broadcasted_iota(jnp.int32, (share, channels), 1) - first
    chosen = at == lax.broadcasted_iota(jnp.int32, (share, channels), 0)
    pick_ref[3 * share :, :] = jnp.where(chosen, 1.0, 0.0).astype(BF16)


def side_kernel(x_ref, l_ref, r_ref, cot_ref, after_ref, side_ref):
    rows, cols, steps, channels = x_ref.shape
    cells = rows * cols
    side_ref[:cells] = x_ref[...].reshape(cells, steps, channels)
    side_ref[cells : 2 * cells] = l_ref[:cells]
    side_ref[2 * cells : 3 * cells] = r_ref[:cells]
    row = (1 - lax.axis_index("space")) * (rows - 1)
    side_ref[3 * cells] = l_ref[cells + row]
    side_ref[3 * cells + 1 : 3 * cells + 1 + cols] = cot_ref[row]
    side_ref[3 * cells + 1 + cols] = r_ref[cells + row]


def late_kernel(count, *refs):
    pieces, late_ref = refs[:count], refs[-1]
    cells = pieces[0].shape[0]
    for n, piece in enumerate(pieces):
        late_ref[n * cells : (n + 1) * cells] = piece[...]


def conv_back(hg_ref, w_ref, rows, cols):
    channels = w_ref.shape[-1]
    conv = None
    for u in range(3):
        for v in range(3):
            piece = hg_ref[2 - u : 2 - u + rows, 2 - v : 2 - v + cols]
            term = dot_back(piece.reshape(-1, channels), w_ref[3 * u + v])
            conv = term if conv is None else conv + term
    return conv


def window_grad(window, slope_ref, tw_ref, hg_ref, frames):
    act = dot_back(window, tw_ref[0])
    for lag in (1, 2):
        act = act + frame_shift(dot_back(window, tw_ref[lag]), lag, frames)
    hg_ref[...] = (act * slope_ref[...]).astype(BF16).reshape(hg_ref.shape)


def send_on(out_ref, own, conv, cot_ref):
    first = lax.axis_index("pipe") == 0

    @pl.when(first)
    def _():
        out_ref[...] = cot_ref[...]

    @pl.when(jnp.logical_not(first))
    def _():
        out_ref[...] = (own.astype(F32) + conv).astype(BF16).reshape(out_ref.shape)


def first_kernel(
    frames, x_ref, cot_ref, l_ref, r_ref, side_ref, w_ref, tw_ref,
    slope_ref, out_ref, xw_ref, cw_ref, hg_ref,
):
    rows, cols, steps, channels = x_ref.shape
    cells = rows * cols
    chan = lax.axis_size("chan")
    bottom = lax.axis_index("space")
    xw_ref[2 : 2 + rows, 2 : 2 + cols] = x_ref[...]
    cw_ref[1 : 1 + rows, 1 : 1 + cols] = cot_ref[...]
    for r in range(rows):
        xw_ref[2 + r, 0:2] = l_ref[r * cols + cols - 2 : r * cols + cols]
        xw_ref[2 + r, cols + 2 : cols + 4] = r_ref[r * cols : r * cols + 2]
        cw_ref[1 + r, 0] = l_ref[cells + r]
        cw_ref[1 + r, cols + 1] = r_ref[cells + r]
    near = (1 - bottom) * (rows + 2)
    far = bottom * (rows + 2)
    for i in range(2):
        at = (bottom * (rows - 2) + i) * cols
        xw_ref[near + i, 2 : 2 + cols] = side_ref[pl.ds(at, cols)]
        xw_ref[near + i, 0:2] = side_ref[pl.ds(cells + at + cols - 2, 2)]
        xw_ref[near + i, cols + 2 : cols + 4] = side_ref[pl.ds(2 * cells + at, 2)]
        xw_ref[far + i] = jnp.zeros(xw_ref.shape[1:], BF16)
    near = (1 - bottom) * (rows + 1)
    far = bottom * (rows + 1)
    cw_ref[near] = side_ref[3 * cells :]
    cw_ref[far] = jnp.zeros(cw_ref.shape[1:], BF16)
    me = lax.axis_index("chan")
    for end, c in ((0, 0), (chan - 1, cols + 2)):

        @pl.when(me == end)
        def _(c=c):
            xw_ref[:, c : c + 2] = jnp.zeros((rows + 4, 2, steps, channels), BF16)
            edge = min(c, cols + 1)
            cw_ref[:, edge : edge + 1] = jnp.zeros((rows + 2, 1, steps, channels), BF16)

    hidden = None
    for u in range(3):
        for v in range(3):
            piece = xw_ref[u : u + rows + 2, v : v + cols + 2]
            term = dot(piece.reshape(-1, channels), w_ref[3 * u + v])
            hidden = term if hidden is None else hidden + term
    slope_ref[...] = slope_of(hidden)
    window_grad(cw_ref[...].reshape(-1, channels), slope_ref, tw_ref, hg_ref, frames)
    conv = conv_back(hg_ref, w_ref, rows, cols)
    send_on(out_ref, cot_ref[...].reshape(-1, channels), conv, cot_ref)


def collect_kernel(extra, *refs):
    pieces, out_ref = refs[: -1 - extra], refs[-1]
    chan = len(pieces)
    rows, cols, steps, channels = pieces[0].shape
    me = lax.axis_index("chan")
    for d, piece in enumerate(pieces):
        out_ref[:, pl.ds(lax.rem(me - d + chan, chan) * cols, cols)] = piece[...]


def clear_rim(padded):
    rows_all, cols_all, steps, channels = padded.shape
    zero_row = jnp.zeros((1, cols_all, steps, channels), padded.dtype)
    padded[0:1] = zero_row
    padded[rows_all - 1 :] = zero_row
    for r in range(1, rows_all - 1):
        for c in (0, cols_all - 1):
            padded[r, c] = jnp.zeros((steps, channels), padded.dtype)


def fill_padded(padded, own, other):
    clear_rim(padded)
    rows, cols = own.shape[0], own.shape[1]
    bottom = lax.axis_index("space")
    for half, top in ((own, bottom * rows), (other, (1 - bottom) * rows)):
        padded[pl.ds(1 + top, rows), 1 : 1 + cols] = half[...]


def fill_from_pieces(padded, rows, cols, pieces, side, late):
    clear_rim(padded)
    chan, cells = len(pieces), rows * cols
    me = lax.axis_index("chan")
    bottom = lax.axis_index("space")
    for d, piece in enumerate(pieces):
        place = 1 + lax.rem(me - d + chan, chan) * cols
        for r in range(rows):
            near = piece[r] if d == 0 else piece[r * cols : (r + 1) * cols]
            padded[1 + bottom * rows + r, pl.ds(place, cols)] = near
            source, n = (late, d - 2) if 1 < d < chan - 1 else (side, min(d, 2))
            at = n * cells + r * cols
            far = 1 + (1 - bottom) * rows + r
            if source is late:
                padded[far, pl.ds(place, cols)] = late[1 - bottom, at : at + cols]
            else:
                padded[far, pl.ds(place, cols)] = side[at : at + cols]


def own_window(gp_ref, slope_ref, w_ref, tw_ref, hg_ref, frames, rows, cols):
    channels = w_ref.shape[-1]
    r0 = lax.axis_index("space") * rows
    c0 = lax.axis_index("chan") * cols
    window = gp_ref[pl.ds(r0, rows + 2), pl.ds(c0, cols + 2)].reshape(-1, channels)
    window_grad(window, slope_ref, tw_ref, hg_ref, frames)
    own = gp_ref[pl.ds(r0 + 1, rows), pl.ds(c0 + 1, cols)].reshape(-1, channels)
    return own, conv_back(hg_ref, w_ref, rows, cols)


def tick_kernel(
    frames, g_ref, other_ref, cot_ref, slope_ref, w_ref, tw_ref, out_ref, gp_ref, hg_ref
):
    rows, cols = cot_ref.shape[:2]
    fill_padded(gp_ref, g_ref, other_ref)
    own, conv = own_window(gp_ref, slope_ref, w_ref, tw_ref, hg_ref, frames, rows, cols)
    send_on(out_ref, own, conv, cot_ref)


def tile_kernel(chan, *refs):
    pieces, (side, late, w_ref) = refs[:chan], refs[chan : chan + 3]
    act_ref, xt_ref, slope_ref, xp_ref = refs[-4:]
    rows, cols, steps, channels = pieces[0].shape
    width = chan * cols
    share = channels // chan
    fill_from_pieces(xp_ref, rows, cols, pieces, side, late)
    span = width * steps
    turn = lax.rem(channels - lax.axis_index("chan") * share, channels)
    for i in range(2 * rows):
        hidden = None
        for u in range(3):
            for v in range(3):
                piece = xp_ref[i + u, v : v + width].reshape(-1, channels)
                term = dot(piece, w_ref[3 * u + v])
                hidden = term if hidden is None else hidden + term
        active = (hidden * jax.nn.sigmoid(hidden)).astype(BF16)
        act_ref[:, i * span : (i + 1) * span] = active.T
        slope_ref[i * span : (i + 1) * span, :] = slope_of(pltpu.roll(hidden, turn, 1)[:, :share])
        xt_ref[:, i * span : (i + 1) * span] = xp_ref[i + 1, 1 : 1 + width].reshape(-1, channels).T


def final_kernel(
    frames, g_ref, other_ref, slope_w_ref, slope_s_ref, act_ref, xt_ref, w_ref, tw_ref, pick_ref,
    out_ref, space_ref, time_ref, gp_ref, hg_ref, hs_ref, hcols_ref, gcols_ref,
):
    rows, width, steps, channels = g_ref.shape
    clips, _, _, cols, _ = out_ref.shape
    share = slope_s_ref.shape[1]
    height = 2 * rows
    span = width * steps
    fill_padded(gp_ref, g_ref, other_ref)
    hs_ref[...] = jnp.zeros(hs_ref.shape, BF16)
    for i in range(height):
        block = gp_ref[i + 1, 1 : 1 + width].reshape(-1, channels)
        mixed = dot_back(block, pick_ref[...])
        act = mixed[:, :share]
        for lag in (1, 2):
            act = act + frame_shift(mixed[:, lag * share : (lag + 1) * share], lag, frames)
        grad = (act * slope_s_ref[i * span : (i + 1) * span, :]).astype(BF16)
        hs_ref[i + 1, 1 : 1 + width] = grad.reshape(width, steps, share)
        own = mixed[:, 3 * share :]
        for lag in range(3):
            shifted = own if lag == 0 else frame_shift(own, lag, frames)
            gcols_ref[i * span : (i + 1) * span, lag * share : (lag + 1) * share] = shifted.astype(
                BF16
            )
    for u in range(3):
        for v in range(3):
            tap = 3 * u + v
            for i in range(height):
                hcols_ref[i * span : (i + 1) * span, tap * share : (tap + 1) * share] = hs_ref[
                    i + 2 - u, 2 - v : 2 - v + width
                ].reshape(-1, share)
    time_ref[...] = dot(act_ref[...], gcols_ref[...]).T.reshape(time_ref.shape)
    space_ref[...] = dot(xt_ref[...], hcols_ref[...]).T.reshape(space_ref.shape)
    own, conv = own_window(gp_ref, slope_w_ref, w_ref, tw_ref, hg_ref, frames, rows, cols)
    grads = (own.astype(F32) + conv).astype(BF16).reshape(rows, cols, steps, channels)
    for r in range(rows):
        out_ref[:, :, r] = jnp.swapaxes(grads[r], 0, 1).reshape(clips, frames, cols, channels)


VM = pltpu.VMEM


def call(kernel, outs, scratch, limit, flops, moved, *operands, places=None):
    places = places or [VM] * len(operands)
    return pl.pallas_call(
        kernel,
        out_shape=outs,
        in_specs=[pl.BlockSpec(memory_space=place) for place in places],
        scratch_shapes=scratch,
        compiler_params=pltpu.CompilerParams(vmem_limit_bytes=limit * MIB),
        cost_estimate=pl.CostEstimate(flops=flops, bytes_accessed=moved, transcendentals=0),
    )(*operands)


def per_device(activations, cotangent, space_weight, time_weight):
    clips, frames, rows, cols, channels = activations.shape[1:]
    steps = clips * frames
    chan, depth = lax.axis_size("chan"), lax.axis_size("pipe")
    share = channels // chan
    height, width = 2 * rows, chan * cols
    count = height * width * steps
    win = (rows + 2) * (cols + 2) * steps
    large = 24 if chan <= 4 else 56
    cell = (steps, channels)

    def bf16(*shape):
        return jax.ShapeDtypeStruct(shape + cell, BF16)

    beside = rows * cols + rows
    x_own, cot_own, to_right, to_left = call(
        pack_kernel,
        (bf16(rows, cols), bf16(rows, cols), bf16(beside), bf16(beside)),
        [],
        16,
        1_000_000,
        1_000_000,
        jnp.stack([activations[0], cotangent]),
    )
    w, tw, pick = call(
        functools.partial(weights_kernel, share),
        (
            jax.ShapeDtypeStruct((9, channels, channels), BF16),
            jax.ShapeDtypeStruct((3, channels, channels), BF16),
            jax.ShapeDtypeStruct((4 * share, channels), BF16),
        ),
        [],
        16,
        1_000_000,
        3_000_000,
        space_weight[0].reshape(9, channels, channels),
        time_weight[0],
        x_own,
        places=[VM, VM, pl.ANY],
    )

    def turned(message, by):
        return lax.ppermute(message, "chan", [(i, (i + by) % chan) for i in range(chan)])

    x_flat = x_own.reshape((rows * cols,) + cell)
    pieces = [
        x_own,
        turned(to_right, 1),
        *[turned(x_flat, d) for d in range(2, chan - 1)],
        turned(to_left, chan - 1),
    ]
    swap = [(0, 1), (1, 0)]
    to_side = call(
        side_kernel,
        bf16(3 * rows * cols + cols + 2),
        [],
        16,
        1_000_000,
        1_000_000,
        x_own, pieces[1], pieces[-1], cot_own, pick,
        places=[VM] * 4 + [pl.ANY],
    )
    from_side = lax.ppermute(to_side, "space", swap)

    def gathered(parts, after=()):
        half = call(
            functools.partial(collect_kernel, len(after)),
            bf16(rows, width),
            [],
            16,
            1_000_000,
            1_000_000,
            *parts,
            *after,
            places=[VM] * len(parts) + [pl.ANY] * len(after),
        )
        return half, lax.ppermute(half, "space", swap)

    slope_w, payload = call(
        functools.partial(first_kernel, frames),
        (jax.ShapeDtypeStruct((win, channels), F32), bf16(rows, cols)),
        [
            pltpu.VMEM((rows + 4, cols + 4) + cell, BF16),
            pltpu.VMEM((rows + 2, cols + 2) + cell, BF16),
            pltpu.VMEM((rows + 2, cols + 2) + cell, BF16),
        ],
        20,
        1,
        1,
        x_own, cot_own, pieces[1], pieces[-1], from_side, w, tw,
    )

    padded = pltpu.VMEM((height + 2, width + 2) + cell, BF16)
    hg_win = pltpu.VMEM((rows + 2, cols + 2) + cell, BF16)
    for tick in range(depth - 1):
        if tick:
            payload = call(
                functools.partial(tick_kernel, frames),
                bf16(rows, cols),
                [padded, hg_win],
                large,
                2 * win * 12 * channels * channels,
                4_000_000,
                *g_all, cot_own, slope_w, w, tw,
            )
        if not tick:
            far = pieces[2:-1]
            to_late = call(
                functools.partial(late_kernel, len(far)),
                bf16(len(far) * rows * cols),
                [],
                16,
                1,
                1,
                *far,
                payload,
                places=[VM] * len(far) + [pl.ANY],
            )
            from_late = lax.all_gather(to_late, "space", axis=0, tiled=False)
        arrived = []
        for d in range(chan):
            pairs = [
                (c * depth + p, (c + d) % chan * depth + (p - 1) % depth)
                for p in range(depth)
                for c in range(chan)
            ]
            arrived.append(lax.ppermute(payload, ("chan", "pipe"), pairs))
        if not tick:
            operands = [*pieces, from_side, from_late, w]
            act_t, x_t, slope_s = call(
                functools.partial(tile_kernel, chan),
                (
                    jax.ShapeDtypeStruct((channels, count), BF16),
                    jax.ShapeDtypeStruct((channels, count), BF16),
                    jax.ShapeDtypeStruct((count, share), F32),
                ),
                [padded],
                large,
                1,
                1,
                *operands,
                arrived[0],
                places=[VM] * len(operands) + [pl.ANY],
            )
        g_all = gathered(arrived, () if tick else (slope_s,))
    grads, space_grad, time_grad = call(
        functools.partial(final_kernel, frames),
        (
            jax.ShapeDtypeStruct((clips, frames, rows, cols, channels), BF16),
            jax.ShapeDtypeStruct((9, share, channels), F32),
            jax.ShapeDtypeStruct((3, share, channels), F32),
        ),
        [
            padded,
            hg_win,
            pltpu.VMEM((height + 2, width + 2, steps, share), BF16),
            pltpu.VMEM((count, 9 * share), BF16),
            pltpu.VMEM((count, 3 * share), BF16),
        ],
        large,
        4 * win * 9 * channels * channels,
        8_000_000,
        *g_all, slope_w, slope_s, act_t, x_t, w, tw, pick,
    )
    return (
        grads[None],
        jnp.swapaxes(space_grad, 1, 2).reshape(3, 3, channels, share)[None],
        jnp.swapaxes(time_grad, 1, 2)[None],
    )


def solution(mesh):
    return jax.shard_map(
        per_device,
        mesh=mesh,
        in_specs=(
            P("pipe", "groups", None, "space", "chan", None),
            P("groups", None, "space", "chan", None),
            P("pipe", None, None, None, None),
            P("pipe", None, None, None),
        ),
        out_specs=(
            P("pipe", "groups", None, "space", "chan", None),
            P("pipe", "groups", None, None, "chan"),
            P("pipe", "groups", None, "chan"),
        ),
        check_vma=False,
    )
```

```python
import functools

import jax
import jax.numpy as jnp
from jax import lax
from jax.experimental import pallas as pl
from jax.experimental.pallas import tpu as pltpu
from jax.sharding import PartitionSpec as P

F32 = jnp.float32
BF16 = jnp.bfloat16
MIB = 1024 * 1024
ROWS_IN = (((1,), (1,)), ((), ()))


def dot(left, right):
    return jnp.dot(left, right, preferred_element_type=F32)


def dot_back(left, right):
    return lax.dot_general(left, right, ROWS_IN, preferred_element_type=F32)


def frame_shift(term, lag, frames):
    rows = term.shape[0]
    moved = pltpu.roll(term, rows - lag, 0)
    frame = lax.broadcasted_iota(jnp.int32, term.shape, 0) % frames
    return jnp.where(frame < frames - lag, moved, 0.0)


def slope_of(hidden):
    sig = jax.nn.sigmoid(hidden)
    return sig * (1.0 + hidden * (1.0 - sig))


def pack_kernel(both_ref, xc_ref, cc_ref, right_ref, left_ref):
    rows, cols, steps, channels = xc_ref.shape
    for n, dst in enumerate((xc_ref, cc_ref)):
        for r in range(rows):
            dst[r] = jnp.swapaxes(both_ref[n, :, :, r].reshape(steps, cols, channels), 0, 1)
    cells = rows * cols
    for msg, col in ((right_ref, cols - 1), (left_ref, 0)):
        msg[:cells] = xc_ref[...].reshape(cells, steps, channels)
        for r in range(rows):
            msg[cells + r] = cc_ref[r, col]


def weights_kernel(share, w_in, tw_in, after_ref, w_ref, tw_ref, pick_ref):
    channels = w_ref.shape[-1]
    w_ref[...] = w_in[...]
    tw_ref[...] = tw_in[...]
    first = pl.multiple_of(lax.axis_index("chan") * share, share)
    for lag in range(3):
        pick_ref[lag * share : (lag + 1) * share, :] = tw_in[lag, pl.ds(first, share), :]
    at = lax.broadcasted_iota(jnp.int32, (share, channels), 1) - first
    chosen = at == lax.broadcasted_iota(jnp.int32, (share, channels), 0)
    pick_ref[3 * share :, :] = jnp.where(chosen, 1.0, 0.0).astype(BF16)


def side_kernel(x_ref, l_ref, r_ref, cot_ref, after_ref, side_ref):
    rows, cols, steps, channels = x_ref.shape
    cells = rows * cols
    side_ref[:cells] = x_ref[...].reshape(cells, steps, channels)
    side_ref[cells : 2 * cells] = l_ref[:cells]
    side_ref[2 * cells : 3 * cells] = r_ref[:cells]
    row = (1 - lax.axis_index("space")) * (rows - 1)
    side_ref[3 * cells] = l_ref[cells + row]
    side_ref[3 * cells + 1 : 3 * cells + 1 + cols] = cot_ref[row]
    side_ref[3 * cells + 1 + cols] = r_ref[cells + row]


def late_kernel(count, *refs):
    pieces, late_ref = refs[:count], refs[-1]
    cells = pieces[0].shape[0]
    for n, piece in enumerate(pieces):
        late_ref[n * cells : (n + 1) * cells] = piece[...]


def conv_back(hg_ref, w_ref, rows, cols):
    channels = w_ref.shape[-1]
    conv = None
    for u in range(3):
        for v in range(3):
            piece = hg_ref[2 - u : 2 - u + rows, 2 - v : 2 - v + cols]
            term = dot_back(piece.reshape(-1, channels), w_ref[3 * u + v])
            conv = term if conv is None else conv + term
    return conv


def window_grad(window, slope_ref, tw_ref, hg_ref, frames):
    act = dot_back(window, tw_ref[0])
    for lag in (1, 2):
        act = act + frame_shift(dot_back(window, tw_ref[lag]), lag, frames)
    hg_ref[...] = (act * slope_ref[...]).astype(BF16).reshape(hg_ref.shape)


def send_on(out_ref, own, conv, cot_ref):
    first = lax.axis_index("pipe") == 0

    @pl.when(first)
    def _():
        out_ref[...] = cot_ref[...]

    @pl.when(jnp.logical_not(first))
    def _():
        out_ref[...] = (own.astype(F32) + conv).astype(BF16).reshape(out_ref.shape)


def first_kernel(
    frames, x_ref, cot_ref, l_ref, r_ref, side_ref, w_ref, tw_ref,
    slope_ref, out_ref, xw_ref, cw_ref, hg_ref,
):
    rows, cols, steps, channels = x_ref.shape
    cells = rows * cols
    bottom = lax.axis_index("space")
    xw_ref[2 : 2 + rows, 2 : 2 + cols] = x_ref[...]
    cw_ref[1 : 1 + rows, 1 : 1 + cols] = cot_ref[...]
    for r in range(rows):
        xw_ref[2 + r, 0:2] = l_ref[r * cols + cols - 2 : r * cols + cols]
        xw_ref[2 + r, cols + 2 : cols + 4] = r_ref[r * cols : r * cols + 2]
        cw_ref[1 + r, 0] = l_ref[cells + r]
        cw_ref[1 + r, cols + 1] = r_ref[cells + r]
    near = (1 - bottom) * (rows + 2)
    far = bottom * (rows + 2)
    for i in range(2):
        at = (bottom * (rows - 2) + i) * cols
        xw_ref[near + i, 2 : 2 + cols] = side_ref[pl.ds(at, cols)]
        xw_ref[near + i, 0:2] = side_ref[pl.ds(cells + at + cols - 2, 2)]
        xw_ref[near + i, cols + 2 : cols + 4] = side_ref[pl.ds(2 * cells + at, 2)]
        xw_ref[far + i] = jnp.zeros(xw_ref.shape[1:], BF16)
    near = (1 - bottom) * (rows + 1)
    far = bottom * (rows + 1)
    cw_ref[near] = side_ref[3 * cells :]
    cw_ref[far] = jnp.zeros(cw_ref.shape[1:], BF16)
    hidden = None
    for u in range(3):
        for v in range(3):
            piece = xw_ref[u : u + rows + 2, v : v + cols + 2]
            term = dot(piece.reshape(-1, channels), w_ref[3 * u + v])
            hidden = term if hidden is None else hidden + term
    slope_ref[...] = slope_of(hidden)
    window_grad(cw_ref[...].reshape(-1, channels), slope_ref, tw_ref, hg_ref, frames)
    conv = conv_back(hg_ref, w_ref, rows, cols)
    send_on(out_ref, cot_ref[...].reshape(-1, channels), conv, cot_ref)


def collect_kernel(extra, *refs):
    pieces, out_ref = refs[: -1 - extra], refs[-1]
    chan = len(pieces)
    rows, cols, steps, channels = pieces[0].shape
    me = lax.axis_index("chan")
    for d, piece in enumerate(pieces):
        out_ref[:, pl.ds(lax.rem(me - d + chan, chan) * cols, cols)] = piece[...]


def clear_rim(padded):
    rows_all, cols_all, steps, channels = padded.shape
    zero_row = jnp.zeros((1, cols_all, steps, channels), padded.dtype)
    padded[0:1] = zero_row
    padded[rows_all - 1 :] = zero_row
    for r in range(1, rows_all - 1):
        for c in (0, cols_all - 1):
            padded[r, c] = jnp.zeros((steps, channels), padded.dtype)


def fill_padded(padded, own, other):
    clear_rim(padded)
    rows, cols = own.shape[0], own.shape[1]
    bottom = lax.axis_index("space")
    for half, top in ((own, bottom * rows), (other, (1 - bottom) * rows)):
        padded[pl.ds(1 + top, rows), 1 : 1 + cols] = half[...]


def fill_from_pieces(padded, rows, cols, pieces, wrap, side, late):
    clear_rim(padded)
    chan, cells = len(pieces), rows * cols
    me = lax.axis_index("chan")
    bottom = lax.axis_index("space")

    def put(d, near, far, n):
        place = 1 + lax.rem(me - d + chan, chan) * cols
        for r in range(rows):
            padded[1 + bottom * rows + r, pl.ds(place, cols)] = (
                near[r] if d == 0 else near[r * cols : (r + 1) * cols]
            )
            at = n * cells + r * cols
            padded[1 + (1 - bottom) * rows + r, pl.ds(place, cols)] = far[at : at + cols]

    other = late.at[1 - bottom]
    put(0, pieces[0], side, 0)
    for d in range(2, chan - 1):
        put(d, pieces[d], other, d - 2)
    for d, end, n in ((1, 0, 1), (chan - 1, chan - 1, 2)):

        @pl.when(me == end)
        def _(d=d):
            put(d, wrap, other, chan - 3)

        @pl.when(me != end)
        def _(d=d, n=n):
            put(d, pieces[d], side, n)


def own_window(gp_ref, slope_ref, w_ref, tw_ref, hg_ref, frames, rows, cols):
    channels = w_ref.shape[-1]
    r0 = lax.axis_index("space") * rows
    c0 = lax.axis_index("chan") * cols
    window = gp_ref[pl.ds(r0, rows + 2), pl.ds(c0, cols + 2)].reshape(-1, channels)
    window_grad(window, slope_ref, tw_ref, hg_ref, frames)
    own = gp_ref[pl.ds(r0 + 1, rows), pl.ds(c0 + 1, cols)].reshape(-1, channels)
    return own, conv_back(hg_ref, w_ref, rows, cols)


def tick_kernel(
    frames, g_ref, other_ref, cot_ref, slope_ref, w_ref, tw_ref, out_ref, gp_ref, hg_ref
):
    rows, cols = cot_ref.shape[:2]
    fill_padded(gp_ref, g_ref, other_ref)
    own, conv = own_window(gp_ref, slope_ref, w_ref, tw_ref, hg_ref, frames, rows, cols)
    send_on(out_ref, own, conv, cot_ref)


def tile_kernel(chan, *refs):
    pieces, (wrap, side, late, w_ref) = refs[:chan], refs[chan : chan + 4]
    act_ref, xt_ref, slope_ref, xp_ref = refs[-4:]
    rows, cols, steps, channels = pieces[0].shape
    width = chan * cols
    share = channels // chan
    fill_from_pieces(xp_ref, rows, cols, pieces, wrap, side, late)
    span = width * steps
    turn = lax.rem(channels - lax.axis_index("chan") * share, channels)
    for i in range(2 * rows):
        hidden = None
        for u in range(3):
            for v in range(3):
                piece = xp_ref[i + u, v : v + width].reshape(-1, channels)
                term = dot(piece, w_ref[3 * u + v])
                hidden = term if hidden is None else hidden + term
        active = (hidden * jax.nn.sigmoid(hidden)).astype(BF16)
        act_ref[:, i * span : (i + 1) * span] = active.T
        slope_ref[i * span : (i + 1) * span, :] = slope_of(pltpu.roll(hidden, turn, 1)[:, :share])
        xt_ref[:, i * span : (i + 1) * span] = xp_ref[i + 1, 1 : 1 + width].reshape(-1, channels).T


def final_kernel(
    frames, g_ref, other_ref, slope_w_ref, slope_s_ref, act_ref, xt_ref, w_ref, tw_ref, pick_ref,
    out_ref, space_ref, time_ref, gp_ref, hg_ref, hs_ref, hcols_ref, gcols_ref,
):
    rows, width, steps, channels = g_ref.shape
    clips, _, _, cols, _ = out_ref.shape
    share = slope_s_ref.shape[1]
    height = 2 * rows
    span = width * steps
    fill_padded(gp_ref, g_ref, other_ref)
    hs_ref[...] = jnp.zeros(hs_ref.shape, BF16)
    for i in range(height):
        block = gp_ref[i + 1, 1 : 1 + width].reshape(-1, channels)
        mixed = dot_back(block, pick_ref[...])
        act = mixed[:, :share]
        for lag in (1, 2):
            act = act + frame_shift(mixed[:, lag * share : (lag + 1) * share], lag, frames)
        grad = (act * slope_s_ref[i * span : (i + 1) * span, :]).astype(BF16)
        hs_ref[i + 1, 1 : 1 + width] = grad.reshape(width, steps, share)
        own = mixed[:, 3 * share :]
        for lag in range(3):
            shifted = own if lag == 0 else frame_shift(own, lag, frames)
            gcols_ref[i * span : (i + 1) * span, lag * share : (lag + 1) * share] = shifted.astype(
                BF16
            )
    for u in range(3):
        for v in range(3):
            tap = 3 * u + v
            for i in range(height):
                hcols_ref[i * span : (i + 1) * span, tap * share : (tap + 1) * share] = hs_ref[
                    i + 2 - u, 2 - v : 2 - v + width
                ].reshape(-1, share)
    time_ref[...] = dot(act_ref[...], gcols_ref[...]).T.reshape(time_ref.shape)
    space_ref[...] = dot(xt_ref[...], hcols_ref[...]).T.reshape(space_ref.shape)
    own, conv = own_window(gp_ref, slope_w_ref, w_ref, tw_ref, hg_ref, frames, rows, cols)
    grads = (own.astype(F32) + conv).astype(BF16).reshape(rows, cols, steps, channels)
    for r in range(rows):
        out_ref[:, :, r] = jnp.swapaxes(grads[r], 0, 1).reshape(clips, frames, cols, channels)


VM = pltpu.VMEM


def call(kernel, outs, scratch, limit, flops, moved, *operands, places=None):
    places = places or [VM] * len(operands)
    return pl.pallas_call(
        kernel,
        out_shape=outs,
        in_specs=[pl.BlockSpec(memory_space=place) for place in places],
        scratch_shapes=scratch,
        compiler_params=pltpu.CompilerParams(vmem_limit_bytes=limit * MIB),
        cost_estimate=pl.CostEstimate(flops=flops, bytes_accessed=moved, transcendentals=0),
    )(*operands)


def per_device(activations, cotangent, space_weight, time_weight):
    clips, frames, rows, cols, channels = activations.shape[1:]
    steps = clips * frames
    chan, depth = lax.axis_size("chan"), lax.axis_size("pipe")
    share = channels // chan
    height, width = 2 * rows, chan * cols
    count = height * width * steps
    win = (rows + 2) * (cols + 2) * steps
    large = 24 if chan <= 4 else 56
    cell = (steps, channels)

    def bf16(*shape):
        return jax.ShapeDtypeStruct(shape + cell, BF16)

    beside = rows * cols + rows
    x_own, cot_own, to_right, to_left = call(
        pack_kernel,
        (bf16(rows, cols), bf16(rows, cols), bf16(beside), bf16(beside)),
        [],
        16,
        1_000_000,
        1_000_000,
        jnp.stack([activations[0], cotangent]),
    )
    w, tw, pick = call(
        functools.partial(weights_kernel, share),
        (
            jax.ShapeDtypeStruct((9, channels, channels), BF16),
            jax.ShapeDtypeStruct((3, channels, channels), BF16),
            jax.ShapeDtypeStruct((4 * share, channels), BF16),
        ),
        [],
        16,
        1_000_000,
        3_000_000,
        space_weight[0].reshape(9, channels, channels),
        time_weight[0],
        x_own,
        places=[VM, VM, pl.ANY],
    )

    def turned(message, by):
        return lax.ppermute(message, "chan", [(i, (i + by) % chan) for i in range(chan)])

    x_flat = x_own.reshape((rows * cols,) + cell)
    pieces = [
        x_own,
        lax.ppermute(to_right, "chan", [(i, i + 1) for i in range(chan - 1)]),
        *[turned(x_flat, d) for d in range(2, chan - 1)],
        lax.ppermute(to_left, "chan", [(i + 1, i) for i in range(chan - 1)]),
    ]
    wrap = lax.ppermute(x_flat, "chan", [(0, chan - 1), (chan - 1, 0)])
    swap = [(0, 1), (1, 0)]
    to_side = call(
        side_kernel,
        bf16(3 * rows * cols + cols + 2),
        [],
        16,
        1_000_000,
        1_000_000,
        x_own, pieces[1], pieces[-1], cot_own, pick,
        places=[VM] * 4 + [pl.ANY],
    )
    from_side = lax.ppermute(to_side, "space", swap)

    def gathered(parts, after=()):
        half = call(
            functools.partial(collect_kernel, len(after)),
            bf16(rows, width),
            [],
            16,
            1_000_000,
            1_000_000,
            *parts,
            *after,
            places=[VM] * len(parts) + [pl.ANY] * len(after),
        )
        return half, lax.ppermute(half, "space", swap)

    slope_w, payload = call(
        functools.partial(first_kernel, frames),
        (jax.ShapeDtypeStruct((win, channels), F32), bf16(rows, cols)),
        [
            pltpu.VMEM((rows + 4, cols + 4) + cell, BF16),
            pltpu.VMEM((rows + 2, cols + 2) + cell, BF16),
            pltpu.VMEM((rows + 2, cols + 2) + cell, BF16),
        ],
        20,
        1,
        1,
        x_own, cot_own, pieces[1], pieces[-1], from_side, w, tw,
    )

    padded = pltpu.VMEM((height + 2, width + 2) + cell, BF16)
    hg_win = pltpu.VMEM((rows + 2, cols + 2) + cell, BF16)
    for tick in range(depth - 1):
        if tick:
            payload = call(
                functools.partial(tick_kernel, frames),
                bf16(rows, cols),
                [padded, hg_win],
                large,
                2 * win * 12 * channels * channels,
                4_000_000,
                *g_all, cot_own, slope_w, w, tw,
            )
        if not tick:
            far = [*pieces[2:-1], wrap]
            to_late = call(
                functools.partial(late_kernel, len(far)),
                bf16(len(far) * rows * cols),
                [],
                16,
                1,
                1,
                *far,
                payload,
                places=[VM] * len(far) + [pl.ANY],
            )
            from_late = lax.all_gather(to_late, "space", axis=0, tiled=False)
        arrived = []
        for d in range(chan):
            pairs = [
                (c * depth + p, (c + d) % chan * depth + (p - 1) % depth)
                for p in range(depth)
                for c in range(chan)
            ]
            arrived.append(lax.ppermute(payload, ("chan", "pipe"), pairs))
        if not tick:
            operands = [*pieces, wrap, from_side, from_late, w]
            act_t, x_t, slope_s = call(
                functools.partial(tile_kernel, chan),
                (
                    jax.ShapeDtypeStruct((channels, count), BF16),
                    jax.ShapeDtypeStruct((channels, count), BF16),
                    jax.ShapeDtypeStruct((count, share), F32),
                ),
                [padded],
                large,
                1,
                1,
                *operands,
                arrived[0],
                places=[VM] * len(operands) + [pl.ANY],
            )
        g_all = gathered(arrived, () if tick else (slope_s,))
    grads, space_grad, time_grad = call(
        functools.partial(final_kernel, frames),
        (
            jax.ShapeDtypeStruct((clips, frames, rows, cols, channels), BF16),
            jax.ShapeDtypeStruct((9, share, channels), F32),
            jax.ShapeDtypeStruct((3, share, channels), F32),
        ),
        [
            padded,
            hg_win,
            pltpu.VMEM((height + 2, width + 2, steps, share), BF16),
            pltpu.VMEM((count, 9 * share), BF16),
            pltpu.VMEM((count, 3 * share), BF16),
        ],
        large,
        4 * win * 9 * channels * channels,
        8_000_000,
        *g_all, slope_w, slope_s, act_t, x_t, w, tw, pick,
    )
    return (
        grads[None],
        jnp.swapaxes(space_grad, 1, 2).reshape(3, 3, channels, share)[None],
        jnp.swapaxes(time_grad, 1, 2)[None],
    )


def solution(mesh):
    return jax.shard_map(
        per_device,
        mesh=mesh,
        in_specs=(
            P("pipe", "groups", None, "space", "chan", None),
            P("groups", None, "space", "chan", None),
            P("pipe", None, None, None, None),
            P("pipe", None, None, None),
        ),
        out_specs=(
            P("pipe", "groups", None, "space", "chan", None),
            P("pipe", "groups", None, None, "chan"),
            P("pipe", "groups", None, "chan"),
        ),
        check_vma=False,
    )
```

```python
import functools

import jax
import jax.numpy as jnp
from jax import lax
from jax.experimental import pallas as pl
from jax.experimental.pallas import tpu as pltpu
from jax.sharding import PartitionSpec as P

F32 = jnp.float32
BF16 = jnp.bfloat16
MIB = 1024 * 1024
ROWS_IN = (((1,), (1,)), ((), ()))


def dot(left, right):
    return jnp.dot(left, right, preferred_element_type=F32)


def dot_back(left, right):
    return lax.dot_general(left, right, ROWS_IN, preferred_element_type=F32)


def frame_shift(term, lag, frames):
    rows = term.shape[0]
    moved = pltpu.roll(term, rows - lag, 0)
    frame = lax.broadcasted_iota(jnp.int32, term.shape, 0) % frames
    return jnp.where(frame < frames - lag, moved, 0.0)


def slope_of(hidden):
    sig = jax.nn.sigmoid(hidden)
    return sig * (1.0 + hidden * (1.0 - sig))


def pack_kernel(both_ref, xc_ref, cc_ref, one_ref, two_ref):
    rows, cols, steps, channels = xc_ref.shape
    for n, dst in enumerate((xc_ref, cc_ref)):
        for r in range(rows):
            dst[r] = jnp.swapaxes(both_ref[n, :, :, r].reshape(steps, cols, channels), 0, 1)
    cells = rows * cols
    odd = lax.rem(lax.axis_index("chan"), 2)
    for msg, col in ((one_ref, (1 - odd) * (cols - 1)), (two_ref, odd * (cols - 1))):
        msg[:cells] = xc_ref[...].reshape(cells, steps, channels)
        for r in range(rows):
            msg[cells + r] = cc_ref[r, col]


def weights_kernel(share, w_in, tw_in, after_ref, w_ref, tw_ref, pick_ref):
    channels = w_ref.shape[-1]
    w_ref[...] = w_in[...]
    tw_ref[...] = tw_in[...]
    first = pl.multiple_of(lax.axis_index("chan") * share, share)
    for lag in range(3):
        pick_ref[lag * share : (lag + 1) * share, :] = tw_in[lag, pl.ds(first, share), :]
    at = lax.broadcasted_iota(jnp.int32, (share, channels), 1) - first
    chosen = at == lax.broadcasted_iota(jnp.int32, (share, channels), 0)
    pick_ref[3 * share :, :] = jnp.where(chosen, 1.0, 0.0).astype(BF16)


def by_parity(body, one, two):
    odd = lax.rem(lax.axis_index("chan"), 2)
    pl.when(odd == 0)(functools.partial(body, two, one))
    pl.when(odd == 1)(functools.partial(body, one, two))


def side_kernel(x_ref, one_ref, two_ref, cot_ref, after_ref, side_ref):
    rows, cols, steps, channels = x_ref.shape
    cells = rows * cols
    side_ref[:cells] = x_ref[...].reshape(cells, steps, channels)
    side_ref[cells : 2 * cells] = one_ref[:cells]
    side_ref[2 * cells : 3 * cells] = two_ref[:cells]
    row = (1 - lax.axis_index("space")) * (rows - 1)
    side_ref[3 * cells + 1 : 3 * cells + 1 + cols] = cot_ref[row]

    def ends(left, right):
        side_ref[3 * cells] = left[cells + row]
        side_ref[3 * cells + 1 + cols] = right[cells + row]

    by_parity(ends, one_ref, two_ref)


def late_kernel(count, *refs):
    pieces, late_ref = refs[:count], refs[-1]
    cells = pieces[0].shape[0]
    for n, piece in enumerate(pieces):
        late_ref[n * cells : (n + 1) * cells] = piece[...]


def conv_back(hg_ref, w_ref, rows, cols):
    channels = w_ref.shape[-1]
    conv = None
    for u in range(3):
        for v in range(3):
            piece = hg_ref[2 - u : 2 - u + rows, 2 - v : 2 - v + cols]
            term = dot_back(piece.reshape(-1, channels), w_ref[3 * u + v])
            conv = term if conv is None else conv + term
    return conv


def window_grad(window, slope_ref, tw_ref, hg_ref, frames):
    act = dot_back(window, tw_ref[0])
    for lag in (1, 2):
        act = act + frame_shift(dot_back(window, tw_ref[lag]), lag, frames)
    hg_ref[...] = (act * slope_ref[...]).astype(BF16).reshape(hg_ref.shape)


def send_on(out_ref, own, conv, cot_ref):
    first = lax.axis_index("pipe") == 0

    @pl.when(first)
    def _():
        out_ref[...] = cot_ref[...]

    @pl.when(jnp.logical_not(first))
    def _():
        out_ref[...] = (own.astype(F32) + conv).astype(BF16).reshape(out_ref.shape)


def first_kernel(
    frames, x_ref, cot_ref, one_ref, two_ref, side_ref, w_ref, tw_ref,
    slope_ref, out_ref, xw_ref, cw_ref, hg_ref,
):
    rows, cols, steps, channels = x_ref.shape
    cells = rows * cols
    bottom = lax.axis_index("space")
    near = (1 - bottom) * (rows + 2)
    edge = (1 - bottom) * (rows + 1)
    xw_ref[2 : 2 + rows, 2 : 2 + cols] = x_ref[...]
    cw_ref[1 : 1 + rows, 1 : 1 + cols] = cot_ref[...]

    def beside(left, right):
        for r in range(rows):
            xw_ref[2 + r, 0:2] = left[r * cols + cols - 2 : r * cols + cols]
            xw_ref[2 + r, cols + 2 : cols + 4] = right[r * cols : r * cols + 2]
            cw_ref[1 + r, 0] = left[cells + r]
            cw_ref[1 + r, cols + 1] = right[cells + r]

    def corners(left, right):
        for i in range(2):
            at = (bottom * (rows - 2) + i) * cols
            xw_ref[near + i, 0:2] = side_ref[pl.ds(left * cells + at + cols - 2, 2)]
            xw_ref[near + i, cols + 2 : cols + 4] = side_ref[pl.ds(right * cells + at, 2)]

    by_parity(beside, one_ref, two_ref)
    by_parity(corners, 1, 2)
    for i in range(2):
        at = (bottom * (rows - 2) + i) * cols
        xw_ref[near + i, 2 : 2 + cols] = side_ref[pl.ds(at, cols)]
        xw_ref[bottom * (rows + 2) + i] = jnp.zeros(xw_ref.shape[1:], BF16)
    cw_ref[edge] = side_ref[3 * cells :]
    cw_ref[bottom * (rows + 1)] = jnp.zeros(cw_ref.shape[1:], BF16)
    me = lax.axis_index("chan")
    for end, c in ((0, 0), (lax.axis_size("chan") - 1, cols + 2)):

        @pl.when(me == end)
        def _(c=c):
            xw_ref[:, c : c + 2] = jnp.zeros((rows + 4, 2, steps, channels), BF16)
            last = min(c, cols + 1)
            cw_ref[:, last : last + 1] = jnp.zeros((rows + 2, 1, steps, channels), BF16)

    hidden = None
    for u in range(3):
        for v in range(3):
            piece = xw_ref[u : u + rows + 2, v : v + cols + 2]
            term = dot(piece.reshape(-1, channels), w_ref[3 * u + v])
            hidden = term if hidden is None else hidden + term
    slope_ref[...] = slope_of(hidden)
    window_grad(cw_ref[...].reshape(-1, channels), slope_ref, tw_ref, hg_ref, frames)
    conv = conv_back(hg_ref, w_ref, rows, cols)
    send_on(out_ref, cot_ref[...].reshape(-1, channels), conv, cot_ref)


def collect_kernel(extra, *refs):
    pieces, out_ref = refs[: -1 - extra], refs[-1]
    chan = len(pieces)
    rows, cols, steps, channels = pieces[0].shape
    me = lax.axis_index("chan")
    for d, piece in enumerate(pieces):
        out_ref[:, pl.ds(lax.rem(me - d + chan, chan) * cols, cols)] = piece[...]


def clear_rim(padded):
    rows_all, cols_all, steps, channels = padded.shape
    zero_row = jnp.zeros((1, cols_all, steps, channels), padded.dtype)
    padded[0:1] = zero_row
    padded[rows_all - 1 :] = zero_row
    for r in range(1, rows_all - 1):
        for c in (0, cols_all - 1):
            padded[r, c] = jnp.zeros((steps, channels), padded.dtype)


def fill_padded(padded, own, other):
    clear_rim(padded)
    rows, cols = own.shape[0], own.shape[1]
    bottom = lax.axis_index("space")
    for half, top in ((own, bottom * rows), (other, (1 - bottom) * rows)):
        padded[pl.ds(1 + top, rows), 1 : 1 + cols] = half[...]


def fill_from_pieces(padded, rows, cols, pieces, side, late):
    clear_rim(padded)
    chan, cells = len(pieces), rows * cols
    me = lax.axis_index("chan")
    turn = 1 - 2 * lax.rem(me, 2)
    bottom = lax.axis_index("space")
    for n, piece in enumerate(pieces):
        place = 1 + lax.rem(me + (0, turn, -turn, *range(-2, 1 - chan, -1))[n] + chan, chan) * cols
        for r in range(rows):
            near = piece[r] if n == 0 else piece[r * cols : (r + 1) * cols]
            padded[1 + bottom * rows + r, pl.ds(place, cols)] = near
            at = r * cols + (n if n < 3 else n - 3) * cells
            span = pl.ds(at, cols)
            other = side[span] if n < 3 else late[1 - bottom, span]
            padded[1 + (1 - bottom) * rows + r, pl.ds(place, cols)] = other


def own_window(gp_ref, slope_ref, w_ref, tw_ref, hg_ref, frames, rows, cols):
    channels = w_ref.shape[-1]
    r0 = lax.axis_index("space") * rows
    c0 = lax.axis_index("chan") * cols
    window = gp_ref[pl.ds(r0, rows + 2), pl.ds(c0, cols + 2)].reshape(-1, channels)
    window_grad(window, slope_ref, tw_ref, hg_ref, frames)
    own = gp_ref[pl.ds(r0 + 1, rows), pl.ds(c0 + 1, cols)].reshape(-1, channels)
    return own, conv_back(hg_ref, w_ref, rows, cols)


def tick_kernel(
    frames, g_ref, other_ref, cot_ref, slope_ref, w_ref, tw_ref, out_ref, gp_ref, hg_ref
):
    rows, cols = cot_ref.shape[:2]
    fill_padded(gp_ref, g_ref, other_ref)
    own, conv = own_window(gp_ref, slope_ref, w_ref, tw_ref, hg_ref, frames, rows, cols)
    send_on(out_ref, own, conv, cot_ref)


def tile_kernel(chan, *refs):
    pieces, (side, late, w_ref) = refs[:chan], refs[chan : chan + 3]
    act_ref, xt_ref, slope_ref, xp_ref = refs[-4:]
    rows, cols, steps, channels = pieces[0].shape
    width = chan * cols
    share = channels // chan
    fill_from_pieces(xp_ref, rows, cols, pieces, side, late)
    span = width * steps
    turn = lax.rem(channels - lax.axis_index("chan") * share, channels)
    for i in range(2 * rows):
        hidden = None
        for u in range(3):
            for v in range(3):
                piece = xp_ref[i + u, v : v + width].reshape(-1, channels)
                term = dot(piece, w_ref[3 * u + v])
                hidden = term if hidden is None else hidden + term
        active = (hidden * jax.nn.sigmoid(hidden)).astype(BF16)
        act_ref[:, i * span : (i + 1) * span] = active.T
        slope_ref[i * span : (i + 1) * span, :] = slope_of(pltpu.roll(hidden, turn, 1)[:, :share])
        xt_ref[:, i * span : (i + 1) * span] = xp_ref[i + 1, 1 : 1 + width].reshape(-1, channels).T


def final_kernel(
    frames, g_ref, other_ref, slope_w_ref, slope_s_ref, act_ref, xt_ref, w_ref, tw_ref, pick_ref,
    out_ref, space_ref, time_ref, gp_ref, hg_ref, hs_ref, hcols_ref, gcols_ref,
):
    rows, width, steps, channels = g_ref.shape
    clips, _, _, cols, _ = out_ref.shape
    share = slope_s_ref.shape[1]
    height = 2 * rows
    span = width * steps
    fill_padded(gp_ref, g_ref, other_ref)
    hs_ref[...] = jnp.zeros(hs_ref.shape, BF16)
    for i in range(height):
        block = gp_ref[i + 1, 1 : 1 + width].reshape(-1, channels)
        mixed = dot_back(block, pick_ref[...])
        act = mixed[:, :share]
        for lag in (1, 2):
            act = act + frame_shift(mixed[:, lag * share : (lag + 1) * share], lag, frames)
        grad = (act * slope_s_ref[i * span : (i + 1) * span, :]).astype(BF16)
        hs_ref[i + 1, 1 : 1 + width] = grad.reshape(width, steps, share)
        own = mixed[:, 3 * share :]
        for lag in range(3):
            shifted = own if lag == 0 else frame_shift(own, lag, frames)
            gcols_ref[i * span : (i + 1) * span, lag * share : (lag + 1) * share] = shifted.astype(
                BF16
            )
    for u in range(3):
        for v in range(3):
            tap = 3 * u + v
            for i in range(height):
                hcols_ref[i * span : (i + 1) * span, tap * share : (tap + 1) * share] = hs_ref[
                    i + 2 - u, 2 - v : 2 - v + width
                ].reshape(-1, share)
    time_ref[...] = dot(act_ref[...], gcols_ref[...]).T.reshape(time_ref.shape)
    space_ref[...] = dot(xt_ref[...], hcols_ref[...]).T.reshape(space_ref.shape)
    own, conv = own_window(gp_ref, slope_w_ref, w_ref, tw_ref, hg_ref, frames, rows, cols)
    grads = (own.astype(F32) + conv).astype(BF16).reshape(rows, cols, steps, channels)
    for r in range(rows):
        out_ref[:, :, r] = jnp.swapaxes(grads[r], 0, 1).reshape(clips, frames, cols, channels)


VM = pltpu.VMEM


def call(kernel, outs, scratch, limit, flops, moved, *operands, places=None):
    places = places or [VM] * len(operands)
    return pl.pallas_call(
        kernel,
        out_shape=outs,
        in_specs=[pl.BlockSpec(memory_space=place) for place in places],
        scratch_shapes=scratch,
        compiler_params=pltpu.CompilerParams(vmem_limit_bytes=limit * MIB),
        cost_estimate=pl.CostEstimate(flops=flops, bytes_accessed=moved, transcendentals=0),
    )(*operands)


def per_device(activations, cotangent, space_weight, time_weight):
    clips, frames, rows, cols, channels = activations.shape[1:]
    steps = clips * frames
    chan, depth = lax.axis_size("chan"), lax.axis_size("pipe")
    share = channels // chan
    height, width = 2 * rows, chan * cols
    count = height * width * steps
    win = (rows + 2) * (cols + 2) * steps
    large = 24 if chan <= 4 else 56
    cell = (steps, channels)

    def bf16(*shape):
        return jax.ShapeDtypeStruct(shape + cell, BF16)

    beside = rows * cols + rows
    x_own, cot_own, first_msg, second_msg = call(
        pack_kernel,
        (bf16(rows, cols), bf16(rows, cols), bf16(beside), bf16(beside)),
        [],
        16,
        1_000_000,
        1_000_000,
        jnp.stack([activations[0], cotangent]),
    )
    w, tw, pick = call(
        functools.partial(weights_kernel, share),
        (
            jax.ShapeDtypeStruct((9, channels, channels), BF16),
            jax.ShapeDtypeStruct((3, channels, channels), BF16),
            jax.ShapeDtypeStruct((4 * share, channels), BF16),
        ),
        [],
        16,
        1_000_000,
        3_000_000,
        space_weight[0].reshape(9, channels, channels),
        time_weight[0],
        x_own,
        places=[VM, VM, pl.ANY],
    )

    def turned(message, by):
        return lax.ppermute(message, "chan", [(i, (i + by) % chan) for i in range(chan)])

    x_flat = x_own.reshape((rows * cols,) + cell)
    one = lax.ppermute(first_msg, "chan", [(i, i ^ 1) for i in range(chan)])
    two = lax.ppermute(second_msg, "chan", [(i, (i + 2 * (i % 2) - 1) % chan) for i in range(chan)])
    far = [turned(x_flat, d) for d in range(2, chan - 1)]
    pieces = [x_own, one, two, *far]
    swap = [(0, 1), (1, 0)]
    to_side = call(
        side_kernel,
        bf16(3 * rows * cols + cols + 2),
        [],
        16,
        1_000_000,
        1_000_000,
        x_own, one, two, cot_own, pick,
        places=[VM] * 4 + [pl.ANY],
    )
    from_side = lax.ppermute(to_side, "space", swap)

    def gathered(parts, after=()):
        half = call(
            functools.partial(collect_kernel, len(after)),
            bf16(rows, width),
            [],
            16,
            1_000_000,
            1_000_000,
            *parts,
            *after,
            places=[VM] * len(parts) + [pl.ANY] * len(after),
        )
        return half, lax.ppermute(half, "space", swap)

    slope_w, payload = call(
        functools.partial(first_kernel, frames),
        (jax.ShapeDtypeStruct((win, channels), F32), bf16(rows, cols)),
        [
            pltpu.VMEM((rows + 4, cols + 4) + cell, BF16),
            pltpu.VMEM((rows + 2, cols + 2) + cell, BF16),
            pltpu.VMEM((rows + 2, cols + 2) + cell, BF16),
        ],
        20,
        1,
        1,
        x_own, cot_own, one, two, from_side, w, tw,
    )

    padded = pltpu.VMEM((height + 2, width + 2) + cell, BF16)
    hg_win = pltpu.VMEM((rows + 2, cols + 2) + cell, BF16)
    for tick in range(depth - 1):
        if tick:
            payload = call(
                functools.partial(tick_kernel, frames),
                bf16(rows, cols),
                [padded, hg_win],
                large,
                2 * win * 12 * channels * channels,
                4_000_000,
                *g_all, cot_own, slope_w, w, tw,
            )
        if not tick:
            to_late = call(
                functools.partial(late_kernel, len(far)),
                bf16(len(far) * rows * cols),
                [],
                16,
                1,
                1,
                *far,
                payload,
                places=[VM] * len(far) + [pl.ANY],
            )
            from_late = lax.all_gather(to_late, "space", axis=0, tiled=False)
        arrived = []
        for d in range(chan):
            pairs = [
                (c * depth + p, (c + d) % chan * depth + (p - 1) % depth)
                for p in range(depth)
                for c in range(chan)
            ]
            arrived.append(lax.ppermute(payload, ("chan", "pipe"), pairs))
        if not tick:
            operands = [*pieces, from_side, from_late, w]
            act_t, x_t, slope_s = call(
                functools.partial(tile_kernel, chan),
                (
                    jax.ShapeDtypeStruct((channels, count), BF16),
                    jax.ShapeDtypeStruct((channels, count), BF16),
                    jax.ShapeDtypeStruct((count, share), F32),
                ),
                [padded],
                large,
                1,
                1,
                *operands,
                arrived[0],
                places=[VM] * len(operands) + [pl.ANY],
            )
        g_all = gathered(arrived, () if tick else (slope_s,))
    grads, space_grad, time_grad = call(
        functools.partial(final_kernel, frames),
        (
            jax.ShapeDtypeStruct((clips, frames, rows, cols, channels), BF16),
            jax.ShapeDtypeStruct((9, share, channels), F32),
            jax.ShapeDtypeStruct((3, share, channels), F32),
        ),
        [
            padded,
            hg_win,
            pltpu.VMEM((height + 2, width + 2, steps, share), BF16),
            pltpu.VMEM((count, 9 * share), BF16),
            pltpu.VMEM((count, 3 * share), BF16),
        ],
        large,
        4 * win * 9 * channels * channels,
        8_000_000,
        *g_all, slope_w, slope_s, act_t, x_t, w, tw, pick,
    )
    return (
        grads[None],
        jnp.swapaxes(space_grad, 1, 2).reshape(3, 3, channels, share)[None],
        jnp.swapaxes(time_grad, 1, 2)[None],
    )


def solution(mesh):
    return jax.shard_map(
        per_device,
        mesh=mesh,
        in_specs=(
            P("pipe", "groups", None, "space", "chan", None),
            P("groups", None, "space", "chan", None),
            P("pipe", None, None, None, None),
            P("pipe", None, None, None),
        ),
        out_specs=(
            P("pipe", "groups", None, "space", "chan", None),
            P("pipe", "groups", None, None, "chan"),
            P("pipe", "groups", None, "chan"),
        ),
        check_vma=False,
    )
```

```python
import functools

import jax
import jax.numpy as jnp
from jax import lax
from jax.experimental import pallas as pl
from jax.experimental.pallas import tpu as pltpu
from jax.sharding import PartitionSpec as P

F32 = jnp.float32
BF16 = jnp.bfloat16
MIB = 1024 * 1024
ROWS_IN = (((1,), (1,)), ((), ()))


def dot(left, right):
    return jnp.dot(left, right, preferred_element_type=F32)


def dot_back(left, right):
    return lax.dot_general(left, right, ROWS_IN, preferred_element_type=F32)


def frame_shift(term, lag, frames):
    rows = term.shape[0]
    moved = pltpu.roll(term, rows - lag, 0)
    frame = lax.broadcasted_iota(jnp.int32, term.shape, 0) % frames
    return jnp.where(frame < frames - lag, moved, 0.0)


def slope_of(hidden):
    sig = jax.nn.sigmoid(hidden)
    return sig * (1.0 + hidden * (1.0 - sig))


def pack_kernel(both_ref, xc_ref, cc_ref, right_ref, left_ref):
    rows, cols, steps, channels = xc_ref.shape
    for n, dst in enumerate((xc_ref, cc_ref)):
        for r in range(rows):
            dst[r] = jnp.swapaxes(both_ref[n, :, :, r].reshape(steps, cols, channels), 0, 1)
    cells = rows * cols
    for msg, col in ((right_ref, cols - 1), (left_ref, 0)):
        msg[:cells] = xc_ref[...].reshape(cells, steps, channels)
        for r in range(rows):
            msg[cells + r] = cc_ref[r, col]


def weights_kernel(share, w_in, tw_in, after_ref, w_ref, tw_ref, pick_ref):
    channels = w_ref.shape[-1]
    w_ref[...] = w_in[...]
    tw_ref[...] = tw_in[...]
    first = pl.multiple_of(lax.axis_index("chan") * share, share)
    for lag in range(3):
        pick_ref[lag * share : (lag + 1) * share, :] = tw_in[lag, pl.ds(first, share), :]
    at = lax.broadcasted_iota(jnp.int32, (share, channels), 1) - first
    chosen = at == lax.broadcasted_iota(jnp.int32, (share, channels), 0)
    pick_ref[3 * share :, :] = jnp.where(chosen, 1.0, 0.0).astype(BF16)


def side_kernel(x_ref, l_ref, r_ref, cot_ref, after_ref, side_ref):
    rows, cols, steps, channels = x_ref.shape
    cells = rows * cols
    side_ref[:cells] = x_ref[...].reshape(cells, steps, channels)
    side_ref[cells : 2 * cells] = l_ref[:cells]
    side_ref[2 * cells : 3 * cells] = r_ref[:cells]
    row = (1 - lax.axis_index("space")) * (rows - 1)
    side_ref[3 * cells] = l_ref[cells + row]
    side_ref[3 * cells + 1 : 3 * cells + 1 + cols] = cot_ref[row]
    side_ref[3 * cells + 1 + cols] = r_ref[cells + row]


def late_kernel(count, *refs):
    pieces, late_ref = refs[:count], refs[-1]
    cells = pieces[0].shape[0]
    for n, piece in enumerate(pieces):
        late_ref[n * cells : (n + 1) * cells] = piece[...]


def conv_back(hg_ref, w_ref, rows, cols):
    channels = w_ref.shape[-1]
    conv = None
    for u in range(3):
        for v in range(3):
            piece = hg_ref[2 - u : 2 - u + rows, 2 - v : 2 - v + cols]
            term = dot_back(piece.reshape(-1, channels), w_ref[3 * u + v])
            conv = term if conv is None else conv + term
    return conv


def window_grad(window, slope_ref, tw_ref, hg_ref, frames):
    act = dot_back(window, tw_ref[0])
    for lag in (1, 2):
        act = act + frame_shift(dot_back(window, tw_ref[lag]), lag, frames)
    hg_ref[...] = (act * slope_ref[...]).astype(BF16).reshape(hg_ref.shape)


def send_on(out_ref, own, conv, cot_ref):
    first = lax.axis_index("pipe") == 0

    @pl.when(first)
    def _():
        out_ref[...] = cot_ref[...]

    @pl.when(jnp.logical_not(first))
    def _():
        out_ref[...] = (own.astype(F32) + conv).astype(BF16).reshape(out_ref.shape)


def first_kernel(
    frames, x_ref, cot_ref, l_ref, r_ref, side_ref, w_ref, tw_ref,
    slope_ref, out_ref, xw_ref, cw_ref, hg_ref,
):
    rows, cols, steps, channels = x_ref.shape
    cells = rows * cols
    chan = lax.axis_size("chan")
    bottom = lax.axis_index("space")
    xw_ref[2 : 2 + rows, 2 : 2 + cols] = x_ref[...]
    cw_ref[1 : 1 + rows, 1 : 1 + cols] = cot_ref[...]
    for r in range(rows):
        xw_ref[2 + r, 0:2] = l_ref[r * cols + cols - 2 : r * cols + cols]
        xw_ref[2 + r, cols + 2 : cols + 4] = r_ref[r * cols : r * cols + 2]
        cw_ref[1 + r, 0] = l_ref[cells + r]
        cw_ref[1 + r, cols + 1] = r_ref[cells + r]
    near = (1 - bottom) * (rows + 2)
    far = bottom * (rows + 2)
    for i in range(2):
        at = (bottom * (rows - 2) + i) * cols
        xw_ref[near + i, 2 : 2 + cols] = side_ref[pl.ds(at, cols)]
        xw_ref[near + i, 0:2] = side_ref[pl.ds(cells + at + cols - 2, 2)]
        xw_ref[near + i, cols + 2 : cols + 4] = side_ref[pl.ds(2 * cells + at, 2)]
        xw_ref[far + i] = jnp.zeros(xw_ref.shape[1:], BF16)
    near = (1 - bottom) * (rows + 1)
    far = bottom * (rows + 1)
    cw_ref[near] = side_ref[3 * cells :]
    cw_ref[far] = jnp.zeros(cw_ref.shape[1:], BF16)
    me = lax.axis_index("chan")
    for end, c in ((0, 0), (chan - 1, cols + 2)):

        @pl.when(me == end)
        def _(c=c):
            xw_ref[:, c : c + 2] = jnp.zeros((rows + 4, 2, steps, channels), BF16)
            edge = min(c, cols + 1)
            cw_ref[:, edge : edge + 1] = jnp.zeros((rows + 2, 1, steps, channels), BF16)

    hidden = None
    for u in range(3):
        for v in range(3):
            piece = xw_ref[u : u + rows + 2, v : v + cols + 2]
            term = dot(piece.reshape(-1, channels), w_ref[3 * u + v])
            hidden = term if hidden is None else hidden + term
    slope_ref[...] = slope_of(hidden)
    window_grad(cw_ref[...].reshape(-1, channels), slope_ref, tw_ref, hg_ref, frames)
    conv = conv_back(hg_ref, w_ref, rows, cols)
    send_on(out_ref, cot_ref[...].reshape(-1, channels), conv, cot_ref)


def collect_kernel(extra, *refs):
    pieces, out_ref = refs[: -1 - extra], refs[-1]
    chan = len(pieces)
    rows, cols, steps, channels = pieces[0].shape
    me = lax.axis_index("chan")
    for d, piece in enumerate(pieces):
        out_ref[:, pl.ds((me ^ d) * cols, cols)] = piece[...]


def clear_rim(padded):
    rows_all, cols_all, steps, channels = padded.shape
    zero_row = jnp.zeros((1, cols_all, steps, channels), padded.dtype)
    padded[0:1] = zero_row
    padded[rows_all - 1 :] = zero_row
    for r in range(1, rows_all - 1):
        for c in (0, cols_all - 1):
            padded[r, c] = jnp.zeros((steps, channels), padded.dtype)


def fill_padded(padded, own, other):
    clear_rim(padded)
    rows, cols = own.shape[0], own.shape[1]
    bottom = lax.axis_index("space")
    for half, top in ((own, bottom * rows), (other, (1 - bottom) * rows)):
        padded[pl.ds(1 + top, rows), 1 : 1 + cols] = half[...]


def fill_from_pieces(padded, rows, cols, pieces, side, late):
    clear_rim(padded)
    chan, cells = len(pieces), rows * cols
    me = lax.axis_index("chan")
    bottom = lax.axis_index("space")
    for d, piece in enumerate(pieces):
        place = 1 + lax.rem(me - d + chan, chan) * cols
        for r in range(rows):
            near = piece[r] if d == 0 else piece[r * cols : (r + 1) * cols]
            padded[1 + bottom * rows + r, pl.ds(place, cols)] = near
            source, n = (late, d - 2) if 1 < d < chan - 1 else (side, min(d, 2))
            at = n * cells + r * cols
            far = 1 + (1 - bottom) * rows + r
            if source is late:
                padded[far, pl.ds(place, cols)] = late[1 - bottom, at : at + cols]
            else:
                padded[far, pl.ds(place, cols)] = side[at : at + cols]


def own_window(gp_ref, slope_ref, w_ref, tw_ref, hg_ref, frames, rows, cols):
    channels = w_ref.shape[-1]
    r0 = lax.axis_index("space") * rows
    c0 = lax.axis_index("chan") * cols
    window = gp_ref[pl.ds(r0, rows + 2), pl.ds(c0, cols + 2)].reshape(-1, channels)
    window_grad(window, slope_ref, tw_ref, hg_ref, frames)
    own = gp_ref[pl.ds(r0 + 1, rows), pl.ds(c0 + 1, cols)].reshape(-1, channels)
    return own, conv_back(hg_ref, w_ref, rows, cols)


def tick_kernel(
    frames, g_ref, other_ref, cot_ref, slope_ref, w_ref, tw_ref, out_ref, gp_ref, hg_ref
):
    rows, cols = cot_ref.shape[:2]
    fill_padded(gp_ref, g_ref, other_ref)
    own, conv = own_window(gp_ref, slope_ref, w_ref, tw_ref, hg_ref, frames, rows, cols)
    send_on(out_ref, own, conv, cot_ref)


def tile_kernel(chan, *refs):
    pieces, (side, late, w_ref) = refs[:chan], refs[chan : chan + 3]
    act_ref, xt_ref, slope_ref, xp_ref = refs[-4:]
    rows, cols, steps, channels = pieces[0].shape
    width = chan * cols
    share = channels // chan
    fill_from_pieces(xp_ref, rows, cols, pieces, side, late)
    span = width * steps
    turn = lax.rem(channels - lax.axis_index("chan") * share, channels)
    for i in range(2 * rows):
        hidden = None
        for u in range(3):
            for v in range(3):
                piece = xp_ref[i + u, v : v + width].reshape(-1, channels)
                term = dot(piece, w_ref[3 * u + v])
                hidden = term if hidden is None else hidden + term
        active = (hidden * jax.nn.sigmoid(hidden)).astype(BF16)
        act_ref[:, i * span : (i + 1) * span] = active.T
        slope_ref[i * span : (i + 1) * span, :] = slope_of(pltpu.roll(hidden, turn, 1)[:, :share])
        xt_ref[:, i * span : (i + 1) * span] = xp_ref[i + 1, 1 : 1 + width].reshape(-1, channels).T


def final_kernel(
    frames, g_ref, other_ref, slope_w_ref, slope_s_ref, act_ref, xt_ref, w_ref, tw_ref, pick_ref,
    out_ref, space_ref, time_ref, gp_ref, hg_ref, hs_ref, hcols_ref, gcols_ref,
):
    rows, width, steps, channels = g_ref.shape
    clips, _, _, cols, _ = out_ref.shape
    share = slope_s_ref.shape[1]
    height = 2 * rows
    span = width * steps
    fill_padded(gp_ref, g_ref, other_ref)
    hs_ref[...] = jnp.zeros(hs_ref.shape, BF16)
    for i in range(height):
        block = gp_ref[i + 1, 1 : 1 + width].reshape(-1, channels)
        mixed = dot_back(block, pick_ref[...])
        act = mixed[:, :share]
        for lag in (1, 2):
            act = act + frame_shift(mixed[:, lag * share : (lag + 1) * share], lag, frames)
        grad = (act * slope_s_ref[i * span : (i + 1) * span, :]).astype(BF16)
        hs_ref[i + 1, 1 : 1 + width] = grad.reshape(width, steps, share)
        own = mixed[:, 3 * share :]
        for lag in range(3):
            shifted = own if lag == 0 else frame_shift(own, lag, frames)
            gcols_ref[i * span : (i + 1) * span, lag * share : (lag + 1) * share] = shifted.astype(
                BF16
            )
    for u in range(3):
        for v in range(3):
            tap = 3 * u + v
            for i in range(height):
                hcols_ref[i * span : (i + 1) * span, tap * share : (tap + 1) * share] = hs_ref[
                    i + 2 - u, 2 - v : 2 - v + width
                ].reshape(-1, share)
    time_ref[...] = dot(act_ref[...], gcols_ref[...]).T.reshape(time_ref.shape)
    space_ref[...] = dot(xt_ref[...], hcols_ref[...]).T.reshape(space_ref.shape)
    own, conv = own_window(gp_ref, slope_w_ref, w_ref, tw_ref, hg_ref, frames, rows, cols)
    grads = (own.astype(F32) + conv).astype(BF16).reshape(rows, cols, steps, channels)
    for r in range(rows):
        out_ref[:, :, r] = jnp.swapaxes(grads[r], 0, 1).reshape(clips, frames, cols, channels)


VM = pltpu.VMEM


def call(kernel, outs, scratch, limit, flops, moved, *operands, places=None):
    places = places or [VM] * len(operands)
    return pl.pallas_call(
        kernel,
        out_shape=outs,
        in_specs=[pl.BlockSpec(memory_space=place) for place in places],
        scratch_shapes=scratch,
        compiler_params=pltpu.CompilerParams(vmem_limit_bytes=limit * MIB),
        cost_estimate=pl.CostEstimate(flops=flops, bytes_accessed=moved, transcendentals=0),
    )(*operands)


def per_device(activations, cotangent, space_weight, time_weight):
    clips, frames, rows, cols, channels = activations.shape[1:]
    steps = clips * frames
    chan, depth = lax.axis_size("chan"), lax.axis_size("pipe")
    share = channels // chan
    height, width = 2 * rows, chan * cols
    count = height * width * steps
    win = (rows + 2) * (cols + 2) * steps
    large = 24 if chan <= 4 else 56
    cell = (steps, channels)

    def bf16(*shape):
        return jax.ShapeDtypeStruct(shape + cell, BF16)

    beside = rows * cols + rows
    x_own, cot_own, to_right, to_left = call(
        pack_kernel,
        (bf16(rows, cols), bf16(rows, cols), bf16(beside), bf16(beside)),
        [],
        16,
        1_000_000,
        1_000_000,
        jnp.stack([activations[0], cotangent]),
    )
    w, tw, pick = call(
        functools.partial(weights_kernel, share),
        (
            jax.ShapeDtypeStruct((9, channels, channels), BF16),
            jax.ShapeDtypeStruct((3, channels, channels), BF16),
            jax.ShapeDtypeStruct((4 * share, channels), BF16),
        ),
        [],
        16,
        1_000_000,
        3_000_000,
        space_weight[0].reshape(9, channels, channels),
        time_weight[0],
        x_own,
        places=[VM, VM, pl.ANY],
    )

    def turned(message, by):
        return lax.ppermute(message, "chan", [(i, (i + by) % chan) for i in range(chan)])

    x_flat = x_own.reshape((rows * cols,) + cell)
    pieces = [
        x_own,
        turned(to_right, 1),
        *[turned(x_flat, d) for d in range(2, chan - 1)],
        turned(to_left, chan - 1),
    ]
    swap = [(0, 1), (1, 0)]
    to_side = call(
        side_kernel,
        bf16(3 * rows * cols + cols + 2),
        [],
        16,
        1_000_000,
        1_000_000,
        x_own, pieces[1], pieces[-1], cot_own, pick,
        places=[VM] * 4 + [pl.ANY],
    )
    from_side = lax.ppermute(to_side, "space", swap)

    def gathered(parts, after=()):
        half = call(
            functools.partial(collect_kernel, len(after)),
            bf16(rows, width),
            [],
            16,
            1_000_000,
            1_000_000,
            *parts,
            *after,
            places=[VM] * len(parts) + [pl.ANY] * len(after),
        )
        return half, lax.ppermute(half, "space", swap)

    slope_w, payload = call(
        functools.partial(first_kernel, frames),
        (jax.ShapeDtypeStruct((win, channels), F32), bf16(rows, cols)),
        [
            pltpu.VMEM((rows + 4, cols + 4) + cell, BF16),
            pltpu.VMEM((rows + 2, cols + 2) + cell, BF16),
            pltpu.VMEM((rows + 2, cols + 2) + cell, BF16),
        ],
        20,
        1,
        1,
        x_own, cot_own, pieces[1], pieces[-1], from_side, w, tw,
    )

    padded = pltpu.VMEM((height + 2, width + 2) + cell, BF16)
    hg_win = pltpu.VMEM((rows + 2, cols + 2) + cell, BF16)
    for tick in range(depth - 1):
        if tick:
            payload = call(
                functools.partial(tick_kernel, frames),
                bf16(rows, cols),
                [padded, hg_win],
                large,
                2 * win * 12 * channels * channels,
                4_000_000,
                *g_all, cot_own, slope_w, w, tw,
            )
        if not tick:
            far = pieces[2:-1]
            to_late = call(
                functools.partial(late_kernel, len(far)),
                bf16(len(far) * rows * cols),
                [],
                16,
                1,
                1,
                *far,
                payload,
                places=[VM] * len(far) + [pl.ANY],
            )
            from_late = lax.all_gather(to_late, "space", axis=0, tiled=False)
        arrived = []
        for d in range(chan):
            pairs = [
                (c * depth + p, (c ^ d) * depth + (p - 1) % depth)
                for p in range(depth)
                for c in range(chan)
            ]
            arrived.append(lax.ppermute(payload, ("chan", "pipe"), pairs))
        if not tick:
            operands = [*pieces, from_side, from_late, w]
            act_t, x_t, slope_s = call(
                functools.partial(tile_kernel, chan),
                (
                    jax.ShapeDtypeStruct((channels, count), BF16),
                    jax.ShapeDtypeStruct((channels, count), BF16),
                    jax.ShapeDtypeStruct((count, share), F32),
                ),
                [padded],
                large,
                1,
                1,
                *operands,
                arrived[0],
                places=[VM] * len(operands) + [pl.ANY],
            )
        g_all = gathered(arrived, () if tick else (slope_s,))
    grads, space_grad, time_grad = call(
        functools.partial(final_kernel, frames),
        (
            jax.ShapeDtypeStruct((clips, frames, rows, cols, channels), BF16),
            jax.ShapeDtypeStruct((9, share, channels), F32),
            jax.ShapeDtypeStruct((3, share, channels), F32),
        ),
        [
            padded,
            hg_win,
            pltpu.VMEM((height + 2, width + 2, steps, share), BF16),
            pltpu.VMEM((count, 9 * share), BF16),
            pltpu.VMEM((count, 3 * share), BF16),
        ],
        large,
        4 * win * 9 * channels * channels,
        8_000_000,
        *g_all, slope_w, slope_s, act_t, x_t, w, tw, pick,
    )
    return (
        grads[None],
        jnp.swapaxes(space_grad, 1, 2).reshape(3, 3, channels, share)[None],
        jnp.swapaxes(time_grad, 1, 2)[None],
    )


def solution(mesh):
    return jax.shard_map(
        per_device,
        mesh=mesh,
        in_specs=(
            P("pipe", "groups", None, "space", "chan", None),
            P("groups", None, "space", "chan", None),
            P("pipe", None, None, None, None),
            P("pipe", None, None, None),
        ),
        out_specs=(
            P("pipe", "groups", None, "space", "chan", None),
            P("pipe", "groups", None, None, "chan"),
            P("pipe", "groups", None, "chan"),
        ),
        check_vma=False,
    )
```

```python
import functools

import jax
import jax.numpy as jnp
from jax import lax
from jax.experimental import pallas as pl
from jax.experimental.pallas import tpu as pltpu
from jax.sharding import PartitionSpec as P

F32 = jnp.float32
BF16 = jnp.bfloat16
MIB = 1024 * 1024
ROWS_IN = (((1,), (1,)), ((), ()))


def dot(left, right):
    return jnp.dot(left, right, preferred_element_type=F32)


def dot_back(left, right):
    return lax.dot_general(left, right, ROWS_IN, preferred_element_type=F32)


def frame_shift(term, lag, frames):
    rows = term.shape[0]
    moved = pltpu.roll(term, rows - lag, 0)
    frame = lax.broadcasted_iota(jnp.int32, term.shape, 0) % frames
    return jnp.where(frame < frames - lag, moved, 0.0)


def slope_of(hidden):
    sig = jax.nn.sigmoid(hidden)
    return sig * (1.0 + hidden * (1.0 - sig))


def pack_kernel(both_ref, xc_ref, cc_ref, right_ref, left_ref):
    rows, cols, steps, channels = xc_ref.shape
    for n, dst in enumerate((xc_ref, cc_ref)):
        for r in range(rows):
            dst[r] = jnp.swapaxes(both_ref[n, :, :, r].reshape(steps, cols, channels), 0, 1)
    cells = rows * cols
    for msg, col in ((right_ref, cols - 1), (left_ref, 0)):
        msg[:cells] = xc_ref[...].reshape(cells, steps, channels)
        for r in range(rows):
            msg[cells + r] = cc_ref[r, col]


def weights_kernel(share, w_in, tw_in, after_ref, w_ref, tw_ref, pick_ref):
    channels = w_ref.shape[-1]
    w_ref[...] = w_in[...]
    tw_ref[...] = tw_in[...]
    first = pl.multiple_of(lax.axis_index("chan") * share, share)
    copies = pick_ref.shape[0] // (4 * share)
    for lag in range(3):
        for j in range(lag * copies, (lag + 1) * copies):
            pick_ref[j * share : (j + 1) * share, :] = tw_in[lag, pl.ds(first, share), :]
    at = lax.broadcasted_iota(jnp.int32, (share, channels), 1) - first
    chosen = at == lax.broadcasted_iota(jnp.int32, (share, channels), 0)
    for j in range(3 * copies, 4 * copies):
        pick_ref[j * share : (j + 1) * share, :] = jnp.where(chosen, 1.0, 0.0).astype(BF16)


def side_kernel(x_ref, l_ref, r_ref, cot_ref, after_ref, side_ref):
    rows, cols, steps, channels = x_ref.shape
    cells = rows * cols
    side_ref[:cells] = x_ref[...].reshape(cells, steps, channels)
    side_ref[cells : 2 * cells] = l_ref[:cells]
    side_ref[2 * cells : 3 * cells] = r_ref[:cells]
    row = (1 - lax.axis_index("space")) * (rows - 1)
    side_ref[3 * cells] = l_ref[cells + row]
    side_ref[3 * cells + 1 : 3 * cells + 1 + cols] = cot_ref[row]
    side_ref[3 * cells + 1 + cols] = r_ref[cells + row]


def late_kernel(count, *refs):
    pieces, late_ref = refs[:count], refs[-1]
    cells = pieces[0].shape[0]
    for n, piece in enumerate(pieces):
        late_ref[n * cells : (n + 1) * cells] = piece[...]


def conv_back(hg_ref, w_ref, rows, cols):
    channels = w_ref.shape[-1]
    conv = None
    for u in range(3):
        for v in range(3):
            piece = hg_ref[2 - u : 2 - u + rows, 2 - v : 2 - v + cols]
            term = dot_back(piece.reshape(-1, channels), w_ref[3 * u + v])
            conv = term if conv is None else conv + term
    return conv


def window_grad(window, slope_ref, tw_ref, hg_ref, frames):
    act = dot_back(window, tw_ref[0])
    for lag in (1, 2):
        act = act + frame_shift(dot_back(window, tw_ref[lag]), lag, frames)
    hg_ref[...] = (act * slope_ref[...]).astype(BF16).reshape(hg_ref.shape)


def send_on(out_ref, own, conv, cot_ref):
    first = lax.axis_index("pipe") == 0

    @pl.when(first)
    def _():
        out_ref[...] = cot_ref[...]

    @pl.when(jnp.logical_not(first))
    def _():
        out_ref[...] = (own.astype(F32) + conv).astype(BF16).reshape(out_ref.shape)


def first_kernel(
    frames, x_ref, cot_ref, l_ref, r_ref, side_ref, w_ref, tw_ref,
    slope_ref, out_ref, xw_ref, cw_ref, hg_ref,
):
    rows, cols, steps, channels = x_ref.shape
    cells = rows * cols
    chan = lax.axis_size("chan")
    bottom = lax.axis_index("space")
    xw_ref[2 : 2 + rows, 2 : 2 + cols] = x_ref[...]
    cw_ref[1 : 1 + rows, 1 : 1 + cols] = cot_ref[...]
    for r in range(rows):
        xw_ref[2 + r, 0:2] = l_ref[r * cols + cols - 2 : r * cols + cols]
        xw_ref[2 + r, cols + 2 : cols + 4] = r_ref[r * cols : r * cols + 2]
        cw_ref[1 + r, 0] = l_ref[cells + r]
        cw_ref[1 + r, cols + 1] = r_ref[cells + r]
    near = (1 - bottom) * (rows + 2)
    far = bottom * (rows + 2)
    for i in range(2):
        at = (bottom * (rows - 2) + i) * cols
        xw_ref[near + i, 2 : 2 + cols] = side_ref[pl.ds(at, cols)]
        xw_ref[near + i, 0:2] = side_ref[pl.ds(cells + at + cols - 2, 2)]
        xw_ref[near + i, cols + 2 : cols + 4] = side_ref[pl.ds(2 * cells + at, 2)]
        xw_ref[far + i] = jnp.zeros(xw_ref.shape[1:], BF16)
    near = (1 - bottom) * (rows + 1)
    far = bottom * (rows + 1)
    cw_ref[near] = side_ref[3 * cells :]
    cw_ref[far] = jnp.zeros(cw_ref.shape[1:], BF16)
    me = lax.axis_index("chan")
    for end, c in ((0, 0), (chan - 1, cols + 2)):

        @pl.when(me == end)
        def _(c=c):
            xw_ref[:, c : c + 2] = jnp.zeros((rows + 4, 2, steps, channels), BF16)
            edge = min(c, cols + 1)
            cw_ref[:, edge : edge + 1] = jnp.zeros((rows + 2, 1, steps, channels), BF16)

    hidden = None
    for u in range(3):
        for v in range(3):
            piece = xw_ref[u : u + rows + 2, v : v + cols + 2]
            term = dot(piece.reshape(-1, channels), w_ref[3 * u + v])
            hidden = term if hidden is None else hidden + term
    slope_ref[...] = slope_of(hidden)
    window_grad(cw_ref[...].reshape(-1, channels), slope_ref, tw_ref, hg_ref, frames)
    conv = conv_back(hg_ref, w_ref, rows, cols)
    send_on(out_ref, cot_ref[...].reshape(-1, channels), conv, cot_ref)


def collect_kernel(extra, *refs):
    pieces, out_ref = refs[: -1 - extra], refs[-1]
    chan = len(pieces)
    rows, cols, steps, channels = pieces[0].shape
    me = lax.axis_index("chan")
    for d, piece in enumerate(pieces):
        out_ref[:, pl.ds(lax.rem(me - d + chan, chan) * cols, cols)] = piece[...]


def clear_rim(padded):
    rows_all, cols_all, steps, channels = padded.shape
    zero_row = jnp.zeros((1, cols_all, steps, channels), padded.dtype)
    padded[0:1] = zero_row
    padded[rows_all - 1 :] = zero_row
    for r in range(1, rows_all - 1):
        for c in (0, cols_all - 1):
            padded[r, c] = jnp.zeros((steps, channels), padded.dtype)


def fill_padded(padded, own, other):
    clear_rim(padded)
    rows, cols = own.shape[0], own.shape[1]
    bottom = lax.axis_index("space")
    for half, top in ((own, bottom * rows), (other, (1 - bottom) * rows)):
        padded[pl.ds(1 + top, rows), 1 : 1 + cols] = half[...]


def fill_from_pieces(padded, rows, cols, pieces, side, late):
    clear_rim(padded)
    chan, cells = len(pieces), rows * cols
    me = lax.axis_index("chan")
    bottom = lax.axis_index("space")
    for d, piece in enumerate(pieces):
        place = 1 + lax.rem(me - d + chan, chan) * cols
        for r in range(rows):
            near = piece[r] if d == 0 else piece[r * cols : (r + 1) * cols]
            padded[1 + bottom * rows + r, pl.ds(place, cols)] = near
            source, n = (late, d - 2) if 1 < d < chan - 1 else (side, min(d, 2))
            at = n * cells + r * cols
            far = 1 + (1 - bottom) * rows + r
            if source is late:
                padded[far, pl.ds(place, cols)] = late[1 - bottom, at : at + cols]
            else:
                padded[far, pl.ds(place, cols)] = side[at : at + cols]


def own_window(gp_ref, r0, slope_ref, w_ref, tw_ref, hg_ref, frames, rows, cols):
    channels = w_ref.shape[-1]
    c0 = lax.axis_index("chan") * cols
    window = gp_ref[pl.ds(r0, rows + 2), pl.ds(c0, cols + 2)].reshape(-1, channels)
    window_grad(window, slope_ref, tw_ref, hg_ref, frames)
    own = gp_ref[pl.ds(r0 + 1, rows), pl.ds(c0 + 1, cols)].reshape(-1, channels)
    return own, conv_back(hg_ref, w_ref, rows, cols)


def tick_kernel(
    frames, g_ref, other_ref, cot_ref, slope_ref, w_ref, tw_ref, out_ref, gp_ref, hg_ref
):
    rows, cols = cot_ref.shape[:2]
    fill_padded(gp_ref, g_ref, other_ref)
    r0 = lax.axis_index("space") * rows
    own, conv = own_window(gp_ref, r0, slope_ref, w_ref, tw_ref, hg_ref, frames, rows, cols)
    send_on(out_ref, own, conv, cot_ref)


def tile_kernel(chan, *refs):
    pieces, (side, late, w_ref) = refs[:chan], refs[chan : chan + 3]
    act_ref, xt_ref, slope_ref, xp_ref = refs[-4:]
    rows, cols, steps, channels = pieces[0].shape
    width = chan * cols
    share = channels // chan
    fill_from_pieces(xp_ref, rows, cols, pieces, side, late)
    span = width * steps
    turn = lax.rem(channels - lax.axis_index("chan") * share, channels)
    for i in range(2 * rows):
        hidden = None
        for u in range(3):
            for v in range(3):
                piece = xp_ref[i + u, v : v + width].reshape(-1, channels)
                term = dot(piece, w_ref[3 * u + v])
                hidden = term if hidden is None else hidden + term
        active = (hidden * jax.nn.sigmoid(hidden)).astype(BF16)
        act_ref[:, i * span : (i + 1) * span] = active.T
        slope = slope_of(pltpu.roll(hidden, turn, 1)[:, :share])
        copies = slope_ref.shape[1] // share
        slope_ref[i * span : (i + 1) * span, :] = jnp.concatenate([slope] * copies, axis=1)
        xt_ref[:, i * span : (i + 1) * span] = xp_ref[i + 1, 1 : 1 + width].reshape(-1, channels).T


def lane_choice(values, share):
    part = lax.broadcasted_iota(jnp.int32, values[0].shape, 1) // share
    chosen = values[0]
    for j in range(1, len(values)):
        chosen = jnp.where(part == j, values[j], chosen)
    return chosen


def digest(block, slope, pick_ref, frames, share):
    lanes = slope.shape[1]
    copies = lanes // share
    mixed = dot_back(block, pick_ref[...])
    act = mixed[:, :lanes]
    for lag in (1, 2):
        act = act + frame_shift(mixed[:, lag * lanes : (lag + 1) * lanes], lag, frames)
    own = mixed[:, 3 * lanes :]
    lagged = [own, frame_shift(own, 1, frames), frame_shift(own, 2, frames)]
    groups = [lane_choice(lagged[t : t + copies], share) for t in range(0, 3, copies)]
    return (act * slope).astype(BF16), [group.astype(BF16) for group in groups]


def digest_half(half_ref, bottom, slope_ref, act_ref, pick_ref, put, gcols_ref, frames, share):
    rows, width, steps, channels = half_ref.shape
    span = width * steps
    lanes = slope_ref.shape[1]
    start = bottom * rows * span
    for r in range(rows):
        slope = slope_ref[pl.ds(pl.multiple_of(start + r * span, span), span), :]
        grad, groups = digest(
            half_ref[r].reshape(span, channels), slope, pick_ref, frames, share
        )
        put(r, grad.reshape(width, steps, lanes))
        for t, group in enumerate(groups):
            gcols_ref[r * span : (r + 1) * span, t * lanes : (t + 1) * lanes] = group
    here = pl.ds(pl.multiple_of(start, span), rows * span)
    return dot(act_ref[:, here], gcols_ref[...])


def near_kernel(
    frames, share, g_ref, slope_ref, act_ref, pick_ref, grad_ref, time_ref, gcols_ref
):
    def put(r, grad):
        grad_ref[r] = grad

    bottom = lax.axis_index("space")
    time_ref[...] = digest_half(
        g_ref, bottom, slope_ref, act_ref, pick_ref, put, gcols_ref, frames, share
    )


def final_kernel(
    frames, share, g_ref, other_ref, near_ref, time_near_ref, slope_w_ref, slope_s_ref, act_ref,
    xt_ref, w_ref, tw_ref, pick_ref,
    out_ref, space_ref, time_ref, gw_ref, hg_ref, hs_ref, hcols_ref, gcols_ref,
):
    rows, width, steps, channels = g_ref.shape
    clips, _, _, cols, _ = out_ref.shape
    height = 2 * rows
    span = width * steps
    lanes = slope_s_ref.shape[1]
    copies = lanes // share
    bottom = lax.axis_index("space")
    clear_rim(hs_ref)
    hs_ref[pl.ds(1 + bottom * rows, rows), 1 : 1 + width] = near_ref[...]

    def put(r, grad):
        hs_ref[1 + (1 - bottom) * rows + r, 1 : 1 + width] = grad

    time_sum = time_near_ref[...] + digest_half(
        other_ref, 1 - bottom, slope_s_ref, act_ref, pick_ref, put, gcols_ref, frames, share
    )
    time_ref[...] = time_sum.T[: 3 * share].reshape(time_ref.shape)
    for n, first in enumerate(range(0, 9, copies)):
        for i in range(height):
            taps = [
                hs_ref[i + 2 - tap // 3, 2 - tap % 3 : 2 - tap % 3 + width].reshape(span, lanes)
                for tap in range(first, min(first + copies, 9))
            ]
            hcols_ref[i * span : (i + 1) * span, n * lanes : (n + 1) * lanes] = lane_choice(
                taps, share
            )
    space_sum = dot(xt_ref[...], hcols_ref[...])
    space_ref[...] = space_sum.T[: 9 * share].reshape(space_ref.shape)
    clear_rim(gw_ref)
    gw_ref[1 : 1 + rows, 1 : 1 + width] = g_ref[...]
    gw_ref[(1 - bottom) * (rows + 1), 1 : 1 + width] = other_ref[bottom * (rows - 1)]
    own, conv = own_window(gw_ref, 0, slope_w_ref, w_ref, tw_ref, hg_ref, frames, rows, cols)
    grads = (own.astype(F32) + conv).astype(BF16).reshape(rows, cols, steps, channels)
    for r in range(rows):
        out_ref[:, :, r] = jnp.swapaxes(grads[r], 0, 1).reshape(clips, frames, cols, channels)


VM = pltpu.VMEM


def call(kernel, outs, scratch, limit, flops, moved, *operands, places=None):
    places = places or [VM] * len(operands)
    return pl.pallas_call(
        kernel,
        out_shape=outs,
        in_specs=[pl.BlockSpec(memory_space=place) for place in places],
        scratch_shapes=scratch,
        compiler_params=pltpu.CompilerParams(vmem_limit_bytes=limit * MIB),
        cost_estimate=pl.CostEstimate(flops=flops, bytes_accessed=moved, transcendentals=0),
    )(*operands)


def per_device(activations, cotangent, space_weight, time_weight):
    clips, frames, rows, cols, channels = activations.shape[1:]
    steps = clips * frames
    chan, depth = lax.axis_size("chan"), lax.axis_size("pipe")
    share = channels // chan
    copies = max(1, 128 // share)
    lanes = copies * share
    lag_groups, tap_groups = -(-3 // copies), -(-9 // copies)
    height, width = 2 * rows, chan * cols
    count = height * width * steps
    win = (rows + 2) * (cols + 2) * steps
    large = 24 if chan <= 4 else 56
    cell = (steps, channels)

    def bf16(*shape):
        return jax.ShapeDtypeStruct(shape + cell, BF16)

    beside = rows * cols + rows
    x_own, cot_own, to_right, to_left = call(
        pack_kernel,
        (bf16(rows, cols), bf16(rows, cols), bf16(beside), bf16(beside)),
        [],
        16,
        1_000_000,
        1_000_000,
        jnp.stack([activations[0], cotangent]),
    )
    w, tw, pick = call(
        functools.partial(weights_kernel, share),
        (
            jax.ShapeDtypeStruct((9, channels, channels), BF16),
            jax.ShapeDtypeStruct((3, channels, channels), BF16),
            jax.ShapeDtypeStruct((4 * copies * share, channels), BF16),
        ),
        [],
        16,
        1_000_000,
        3_000_000,
        space_weight[0].reshape(9, channels, channels),
        time_weight[0],
        x_own,
        places=[VM, VM, pl.ANY],
    )

    def turned(message, by):
        return lax.ppermute(message, "chan", [(i, (i + by) % chan) for i in range(chan)])

    x_flat = x_own.reshape((rows * cols,) + cell)
    pieces = [
        x_own,
        turned(to_right, 1),
        *[turned(x_flat, d) for d in range(2, chan - 1)],
        turned(to_left, chan - 1),
    ]
    swap = [(0, 1), (1, 0)]
    to_side = call(
        side_kernel,
        bf16(3 * rows * cols + cols + 2),
        [],
        16,
        1_000_000,
        1_000_000,
        x_own, pieces[1], pieces[-1], cot_own, pick,
        places=[VM] * 4 + [pl.ANY],
    )
    from_side = lax.ppermute(to_side, "space", swap)

    def gathered(parts, after=()):
        half = call(
            functools.partial(collect_kernel, len(after)),
            bf16(rows, width),
            [],
            16,
            1_000_000,
            1_000_000,
            *parts,
            *after,
            places=[VM] * len(parts) + [pl.ANY] * len(after),
        )
        return half, lax.ppermute(half, "space", swap)

    slope_w, payload = call(
        functools.partial(first_kernel, frames),
        (jax.ShapeDtypeStruct((win, channels), F32), bf16(rows, cols)),
        [
            pltpu.VMEM((rows + 4, cols + 4) + cell, BF16),
            pltpu.VMEM((rows + 2, cols + 2) + cell, BF16),
            pltpu.VMEM((rows + 2, cols + 2) + cell, BF16),
        ],
        20,
        1,
        1,
        x_own, cot_own, pieces[1], pieces[-1], from_side, w, tw,
    )

    padded = pltpu.VMEM((height + 2, width + 2) + cell, BF16)
    hg_win = pltpu.VMEM((rows + 2, cols + 2) + cell, BF16)
    for tick in range(depth - 1):
        if tick:
            payload = call(
                functools.partial(tick_kernel, frames),
                bf16(rows, cols),
                [padded, hg_win],
                large,
                2 * win * 12 * channels * channels,
                4_000_000,
                *g_all, cot_own, slope_w, w, tw,
            )
        if not tick:
            far = pieces[2:-1]
            to_late = call(
                functools.partial(late_kernel, len(far)),
                bf16(len(far) * rows * cols),
                [],
                16,
                1,
                1,
                *far,
                payload,
                places=[VM] * len(far) + [pl.ANY],
            )
            from_late = lax.all_gather(to_late, "space", axis=0, tiled=False)
        arrived = []
        for d in range(chan):
            pairs = [
                (c * depth + p, (c + d) % chan * depth + (p - 1) % depth)
                for p in range(depth)
                for c in range(chan)
            ]
            arrived.append(lax.ppermute(payload, ("chan", "pipe"), pairs))
        if not tick:
            operands = [*pieces, from_side, from_late, w]
            act_t, x_t, slope_s = call(
                functools.partial(tile_kernel, chan),
                (
                    jax.ShapeDtypeStruct((channels, count), BF16),
                    jax.ShapeDtypeStruct((channels, count), BF16),
                    jax.ShapeDtypeStruct((count, lanes), F32),
                ),
                [padded],
                large,
                1,
                1,
                *operands,
                arrived[0],
                places=[VM] * len(operands) + [pl.ANY],
            )
        g_all = gathered(arrived, () if tick else (slope_s,))
    grad_near, time_near = call(
        functools.partial(near_kernel, frames, share),
        (
            jax.ShapeDtypeStruct((rows, width, steps, lanes), BF16),
            jax.ShapeDtypeStruct((channels, lag_groups * lanes), F32),
        ),
        [pltpu.VMEM((count // 2, lag_groups * lanes), BF16)],
        large,
        count * channels * channels * 4,
        4_000_000,
        g_all[0],
        slope_s,
        act_t,
        pick,
    )
    grads, space_grad, time_grad = call(
        functools.partial(final_kernel, frames, share),
        (
            jax.ShapeDtypeStruct((clips, frames, rows, cols, channels), BF16),
            jax.ShapeDtypeStruct((9, share, channels), F32),
            jax.ShapeDtypeStruct((3, share, channels), F32),
        ),
        [
            pltpu.VMEM((rows + 2, width + 2) + cell, BF16),
            hg_win,
            pltpu.VMEM((height + 2, width + 2, steps, lanes), BF16),
            pltpu.VMEM((count, tap_groups * lanes), BF16),
            pltpu.VMEM((count // 2, lag_groups * lanes), BF16),
        ],
        large,
        4 * win * 9 * channels * channels,
        8_000_000,
        *g_all, grad_near, time_near, slope_w, slope_s, act_t, x_t, w, tw, pick,
    )
    return (
        grads[None],
        jnp.swapaxes(space_grad, 1, 2).reshape(3, 3, channels, share)[None],
        jnp.swapaxes(time_grad, 1, 2)[None],
    )


def solution(mesh):
    return jax.shard_map(
        per_device,
        mesh=mesh,
        in_specs=(
            P("pipe", "groups", None, "space", "chan", None),
            P("groups", None, "space", "chan", None),
            P("pipe", None, None, None, None),
            P("pipe", None, None, None),
        ),
        out_specs=(
            P("pipe", "groups", None, "space", "chan", None),
            P("pipe", "groups", None, None, "chan"),
            P("pipe", "groups", None, "chan"),
        ),
        check_vma=False,
    )
```

```python
import functools

import jax
import jax.numpy as jnp
from jax import lax
from jax.experimental import pallas as pl
from jax.experimental.pallas import tpu as pltpu
from jax.sharding import PartitionSpec as P

F32 = jnp.float32
BF16 = jnp.bfloat16
MIB = 1024 * 1024
ROWS_IN = (((1,), (1,)), ((), ()))


def dot(left, right):
    return jnp.dot(left, right, preferred_element_type=F32)


def dot_back(left, right):
    return lax.dot_general(left, right, ROWS_IN, preferred_element_type=F32)


def frame_shift(term, lag, frames):
    rows = term.shape[0]
    moved = pltpu.roll(term, rows - lag, 0)
    frame = lax.broadcasted_iota(jnp.int32, term.shape, 0) % frames
    return jnp.where(frame < frames - lag, moved, 0.0)


def slope_of(hidden):
    sig = jax.nn.sigmoid(hidden)
    return sig * (1.0 + hidden * (1.0 - sig))


def pack_kernel(both_ref, xc_ref, cc_ref, right_ref, left_ref):
    rows, cols, steps, channels = xc_ref.shape
    for n, dst in enumerate((xc_ref, cc_ref)):
        for r in range(rows):
            dst[r] = jnp.swapaxes(both_ref[n, :, :, r].reshape(steps, cols, channels), 0, 1)
    cells = rows * cols
    for msg, col in ((right_ref, cols - 1), (left_ref, 0)):
        msg[:cells] = xc_ref[...].reshape(cells, steps, channels)
        for r in range(rows):
            msg[cells + r] = cc_ref[r, col]


def weights_kernel(share, w_in, tw_in, after_ref, w_ref, tw_ref, pick_ref):
    channels = w_ref.shape[-1]
    w_ref[...] = w_in[...]
    tw_ref[...] = tw_in[...]
    first = pl.multiple_of(lax.axis_index("chan") * share, share)
    copies = pick_ref.shape[0] // (4 * share)
    for lag in range(3):
        for j in range(lag * copies, (lag + 1) * copies):
            pick_ref[j * share : (j + 1) * share, :] = tw_in[lag, pl.ds(first, share), :]
    at = lax.broadcasted_iota(jnp.int32, (share, channels), 1) - first
    chosen = at == lax.broadcasted_iota(jnp.int32, (share, channels), 0)
    for j in range(3 * copies, 4 * copies):
        pick_ref[j * share : (j + 1) * share, :] = jnp.where(chosen, 1.0, 0.0).astype(BF16)


def side_kernel(x_ref, l_ref, r_ref, cot_ref, after_ref, side_ref):
    rows, cols, steps, channels = x_ref.shape
    cells = rows * cols
    side_ref[:cells] = x_ref[...].reshape(cells, steps, channels)
    side_ref[cells : 2 * cells] = l_ref[:cells]
    side_ref[2 * cells : 3 * cells] = r_ref[:cells]
    row = (1 - lax.axis_index("space")) * (rows - 1)
    side_ref[3 * cells] = l_ref[cells + row]
    side_ref[3 * cells + 1 : 3 * cells + 1 + cols] = cot_ref[row]
    side_ref[3 * cells + 1 + cols] = r_ref[cells + row]


def late_kernel(count, *refs):
    pieces, late_ref = refs[:count], refs[-1]
    cells = pieces[0].shape[0]
    for n, piece in enumerate(pieces):
        late_ref[n * cells : (n + 1) * cells] = piece[...]


def conv_back(hg_ref, w_ref, rows, cols):
    channels = w_ref.shape[-1]
    conv = None
    for u in range(3):
        for v in range(3):
            piece = hg_ref[2 - u : 2 - u + rows, 2 - v : 2 - v + cols]
            term = dot_back(piece.reshape(-1, channels), w_ref[3 * u + v])
            conv = term if conv is None else conv + term
    return conv


def window_grad(window, slope_ref, tw_ref, hg_ref, frames):
    act = dot_back(window, tw_ref[0])
    for lag in (1, 2):
        act = act + frame_shift(dot_back(window, tw_ref[lag]), lag, frames)
    hg_ref[...] = (act * slope_ref[...]).astype(BF16).reshape(hg_ref.shape)


def send_on(out_ref, own, conv, cot_ref):
    first = lax.axis_index("pipe") == 0

    @pl.when(first)
    def _():
        out_ref[...] = cot_ref[...]

    @pl.when(jnp.logical_not(first))
    def _():
        out_ref[...] = (own.astype(F32) + conv).astype(BF16).reshape(out_ref.shape)


def first_kernel(
    frames, x_ref, cot_ref, l_ref, r_ref, side_ref, w_ref, tw_ref,
    slope_ref, out_ref, xw_ref, cw_ref, hg_ref,
):
    rows, cols, steps, channels = x_ref.shape
    cells = rows * cols
    chan = lax.axis_size("chan")
    bottom = lax.axis_index("space")
    xw_ref[2 : 2 + rows, 2 : 2 + cols] = x_ref[...]
    cw_ref[1 : 1 + rows, 1 : 1 + cols] = cot_ref[...]
    for r in range(rows):
        xw_ref[2 + r, 0:2] = l_ref[r * cols + cols - 2 : r * cols + cols]
        xw_ref[2 + r, cols + 2 : cols + 4] = r_ref[r * cols : r * cols + 2]
        cw_ref[1 + r, 0] = l_ref[cells + r]
        cw_ref[1 + r, cols + 1] = r_ref[cells + r]
    near = (1 - bottom) * (rows + 2)
    far = bottom * (rows + 2)
    for i in range(2):
        at = (bottom * (rows - 2) + i) * cols
        xw_ref[near + i, 2 : 2 + cols] = side_ref[pl.ds(at, cols)]
        xw_ref[near + i, 0:2] = side_ref[pl.ds(cells + at + cols - 2, 2)]
        xw_ref[near + i, cols + 2 : cols + 4] = side_ref[pl.ds(2 * cells + at, 2)]
        xw_ref[far + i] = jnp.zeros(xw_ref.shape[1:], BF16)
    near = (1 - bottom) * (rows + 1)
    far = bottom * (rows + 1)
    cw_ref[near] = side_ref[3 * cells :]
    cw_ref[far] = jnp.zeros(cw_ref.shape[1:], BF16)
    me = lax.axis_index("chan")
    for end, c in ((0, 0), (chan - 1, cols + 2)):

        @pl.when(me == end)
        def _(c=c):
            xw_ref[:, c : c + 2] = jnp.zeros((rows + 4, 2, steps, channels), BF16)
            edge = min(c, cols + 1)
            cw_ref[:, edge : edge + 1] = jnp.zeros((rows + 2, 1, steps, channels), BF16)

    hidden = None
    for u in range(3):
        for v in range(3):
            piece = xw_ref[u : u + rows + 2, v : v + cols + 2]
            term = dot(piece.reshape(-1, channels), w_ref[3 * u + v])
            hidden = term if hidden is None else hidden + term
    slope_ref[...] = slope_of(hidden)
    window_grad(cw_ref[...].reshape(-1, channels), slope_ref, tw_ref, hg_ref, frames)
    conv = conv_back(hg_ref, w_ref, rows, cols)
    send_on(out_ref, cot_ref[...].reshape(-1, channels), conv, cot_ref)


def collect_kernel(extra, *refs):
    pieces, out_ref = refs[: -1 - extra], refs[-1]
    chan = len(pieces)
    rows, cols, steps, channels = pieces[0].shape
    me = lax.axis_index("chan")
    for d, piece in enumerate(pieces):
        out_ref[:, pl.ds(lax.rem(me - d + chan, chan) * cols, cols)] = piece[...]


def clear_rim(padded):
    rows_all, cols_all, steps, channels = padded.shape
    zero_row = jnp.zeros((1, cols_all, steps, channels), padded.dtype)
    padded[0:1] = zero_row
    padded[rows_all - 1 :] = zero_row
    for r in range(1, rows_all - 1):
        for c in (0, cols_all - 1):
            padded[r, c] = jnp.zeros((steps, channels), padded.dtype)


def fill_padded(padded, own, other):
    clear_rim(padded)
    rows, cols = own.shape[0], own.shape[1]
    bottom = lax.axis_index("space")
    for half, top in ((own, bottom * rows), (other, (1 - bottom) * rows)):
        padded[pl.ds(1 + top, rows), 1 : 1 + cols] = half[...]


def fill_from_pieces(padded, rows, cols, pieces, side, late):
    clear_rim(padded)
    chan, cells = len(pieces), rows * cols
    me = lax.axis_index("chan")
    bottom = lax.axis_index("space")
    for d, piece in enumerate(pieces):
        place = 1 + lax.rem(me - d + chan, chan) * cols
        for r in range(rows):
            near = piece[r] if d == 0 else piece[r * cols : (r + 1) * cols]
            padded[1 + bottom * rows + r, pl.ds(place, cols)] = near
            source, n = (late, d - 2) if 1 < d < chan - 1 else (side, min(d, 2))
            at = n * cells + r * cols
            far = 1 + (1 - bottom) * rows + r
            if source is late:
                padded[far, pl.ds(place, cols)] = late[1 - bottom, at : at + cols]
            else:
                padded[far, pl.ds(place, cols)] = side[at : at + cols]


def own_window(gp_ref, r0, slope_ref, w_ref, tw_ref, hg_ref, frames, rows, cols):
    channels = w_ref.shape[-1]
    c0 = lax.axis_index("chan") * cols
    window = gp_ref[pl.ds(r0, rows + 2), pl.ds(c0, cols + 2)].reshape(-1, channels)
    window_grad(window, slope_ref, tw_ref, hg_ref, frames)
    own = gp_ref[pl.ds(r0 + 1, rows), pl.ds(c0 + 1, cols)].reshape(-1, channels)
    return own, conv_back(hg_ref, w_ref, rows, cols)


def tick_kernel(
    frames, g_ref, other_ref, cot_ref, slope_ref, w_ref, tw_ref, out_ref, gp_ref, hg_ref
):
    rows, cols = cot_ref.shape[:2]
    fill_padded(gp_ref, g_ref, other_ref)
    r0 = lax.axis_index("space") * rows
    own, conv = own_window(gp_ref, r0, slope_ref, w_ref, tw_ref, hg_ref, frames, rows, cols)
    send_on(out_ref, own, conv, cot_ref)


def tile_kernel(chan, *refs):
    pieces, (side, late, w_ref) = refs[:chan], refs[chan : chan + 3]
    act_ref, xt_ref, slope_ref, xp_ref = refs[-4:]
    rows, cols, steps, channels = pieces[0].shape
    width = chan * cols
    share = channels // chan
    fill_from_pieces(xp_ref, rows, cols, pieces, side, late)
    span = width * steps
    turn = lax.rem(channels - lax.axis_index("chan") * share, channels)
    for i in range(2 * rows):
        hidden = None
        for u in range(3):
            for v in range(3):
                piece = xp_ref[i + u, v : v + width].reshape(-1, channels)
                term = dot(piece, w_ref[3 * u + v])
                hidden = term if hidden is None else hidden + term
        active = (hidden * jax.nn.sigmoid(hidden)).astype(BF16)
        act_ref[:, i * span : (i + 1) * span] = active.T
        slope = slope_of(pltpu.roll(hidden, turn, 1)[:, :share])
        copies = slope_ref.shape[1] // share
        slope_ref[i * span : (i + 1) * span, :] = jnp.concatenate([slope] * copies, axis=1)
        xt_ref[:, i * span : (i + 1) * span] = xp_ref[i + 1, 1 : 1 + width].reshape(-1, channels).T


def lane_choice(values, share):
    part = lax.broadcasted_iota(jnp.int32, values[0].shape, 1) // share
    chosen = values[0]
    for j in range(1, len(values)):
        chosen = jnp.where(part == j, values[j], chosen)
    return chosen


def digest(block, slope, pick_ref, frames, share):
    lanes = slope.shape[1]
    copies = lanes // share
    mixed = dot_back(block, pick_ref[...])
    act = mixed[:, :lanes]
    for lag in (1, 2):
        act = act + frame_shift(mixed[:, lag * lanes : (lag + 1) * lanes], lag, frames)
    own = mixed[:, 3 * lanes :]
    lagged = [own, frame_shift(own, 1, frames), frame_shift(own, 2, frames)]
    groups = [lane_choice(lagged[t : t + copies], share) for t in range(0, 3, copies)]
    return (act * slope).astype(BF16), [group.astype(BF16) for group in groups]


def digest_half(half_ref, bottom, slope_ref, act_ref, pick_ref, put, gcols_ref, frames, share):
    rows, width, steps, channels = half_ref.shape
    span = width * steps
    lanes = slope_ref.shape[1]
    start = bottom * rows * span
    for r in range(rows):
        slope = slope_ref[pl.ds(pl.multiple_of(start + r * span, span), span), :]
        grad, groups = digest(
            half_ref[r].reshape(span, channels), slope, pick_ref, frames, share
        )
        put(r, grad.reshape(width, steps, lanes))
        for t, group in enumerate(groups):
            gcols_ref[r * span : (r + 1) * span, t * lanes : (t + 1) * lanes] = group
    here = pl.ds(pl.multiple_of(start, span), rows * span)
    return dot(act_ref[:, here], gcols_ref[...])


def tap_products(hs_ref, top, x_top, count, xt_ref, hcols_ref, share):
    width, steps, lanes = hs_ref.shape[1] - 2, *hs_ref.shape[2:]
    copies = lanes // share
    span = width * steps
    for n, first in enumerate(range(0, 9, copies)):
        for i in range(count):
            taps = [
                hs_ref[top + i + 2 - tap // 3, 2 - tap % 3 : 2 - tap % 3 + width].reshape(span, lanes)
                for tap in range(first, min(first + copies, 9))
            ]
            hcols_ref[i * span : (i + 1) * span, n * lanes : (n + 1) * lanes] = lane_choice(
                taps, share
            )
    here = pl.ds(pl.multiple_of(x_top * span, span), count * span)
    return dot(xt_ref[:, here], hcols_ref[...])


def near_kernel(
    frames, share, g_ref, slope_ref, act_ref, xt_ref, pick_ref,
    grad_ref, time_ref, space_ref, gcols_ref, hs_ref, hcols_ref,
):
    rows, width = g_ref.shape[:2]
    clear_rim(hs_ref)

    def put(r, grad):
        grad_ref[r] = grad
        hs_ref[1 + r, 1 : 1 + width] = grad

    bottom = lax.axis_index("space")
    time_ref[...] = digest_half(
        g_ref, bottom, slope_ref, act_ref, pick_ref, put, gcols_ref, frames, share
    )
    space_ref[...] = tap_products(
        hs_ref, bottom, bottom * (rows + 1), rows - 1, xt_ref, hcols_ref, share
    )


def final_kernel(
    frames, share, g_ref, other_ref, near_ref, time_near_ref, space_near_ref, slope_w_ref,
    slope_s_ref, act_ref, xt_ref, w_ref, tw_ref, pick_ref,
    out_ref, space_ref, time_ref, gw_ref, hg_ref, hs_ref, hcols_ref, gcols_ref,
):
    rows, width, steps, channels = g_ref.shape
    clips, _, _, cols, _ = out_ref.shape
    bottom = lax.axis_index("space")
    clear_rim(hs_ref)
    hs_ref[pl.ds(1 + bottom * rows, rows), 1 : 1 + width] = near_ref[...]

    def put(r, grad):
        hs_ref[1 + (1 - bottom) * rows + r, 1 : 1 + width] = grad

    time_sum = time_near_ref[...] + digest_half(
        other_ref, 1 - bottom, slope_s_ref, act_ref, pick_ref, put, gcols_ref, frames, share
    )
    time_ref[...] = time_sum.T[: 3 * share].reshape(time_ref.shape)
    top = (1 - bottom) * (rows - 1)
    space_sum = space_near_ref[...] + tap_products(
        hs_ref, top, top, rows + 1, xt_ref, hcols_ref, share
    )
    space_ref[...] = space_sum.T[: 9 * share].reshape(space_ref.shape)
    clear_rim(gw_ref)
    gw_ref[1 : 1 + rows, 1 : 1 + width] = g_ref[...]
    gw_ref[(1 - bottom) * (rows + 1), 1 : 1 + width] = other_ref[bottom * (rows - 1)]
    own, conv = own_window(gw_ref, 0, slope_w_ref, w_ref, tw_ref, hg_ref, frames, rows, cols)
    grads = (own.astype(F32) + conv).astype(BF16).reshape(rows, cols, steps, channels)
    for r in range(rows):
        out_ref[:, :, r] = jnp.swapaxes(grads[r], 0, 1).reshape(clips, frames, cols, channels)


VM = pltpu.VMEM


def call(kernel, outs, scratch, limit, flops, moved, *operands, places=None):
    places = places or [VM] * len(operands)
    return pl.pallas_call(
        kernel,
        out_shape=outs,
        in_specs=[pl.BlockSpec(memory_space=place) for place in places],
        scratch_shapes=scratch,
        compiler_params=pltpu.CompilerParams(vmem_limit_bytes=limit * MIB),
        cost_estimate=pl.CostEstimate(flops=flops, bytes_accessed=moved, transcendentals=0),
    )(*operands)


def per_device(activations, cotangent, space_weight, time_weight):
    clips, frames, rows, cols, channels = activations.shape[1:]
    steps = clips * frames
    chan, depth = lax.axis_size("chan"), lax.axis_size("pipe")
    share = channels // chan
    copies = max(1, 128 // share)
    lanes = copies * share
    lag_groups, tap_groups = -(-3 // copies), -(-9 // copies)
    height, width = 2 * rows, chan * cols
    count = height * width * steps
    win = (rows + 2) * (cols + 2) * steps
    large = 24 if chan <= 4 else 56
    cell = (steps, channels)

    def bf16(*shape):
        return jax.ShapeDtypeStruct(shape + cell, BF16)

    beside = rows * cols + rows
    x_own, cot_own, to_right, to_left = call(
        pack_kernel,
        (bf16(rows, cols), bf16(rows, cols), bf16(beside), bf16(beside)),
        [],
        16,
        1_000_000,
        1_000_000,
        jnp.stack([activations[0], cotangent]),
    )
    w, tw, pick = call(
        functools.partial(weights_kernel, share),
        (
            jax.ShapeDtypeStruct((9, channels, channels), BF16),
            jax.ShapeDtypeStruct((3, channels, channels), BF16),
            jax.ShapeDtypeStruct((4 * copies * share, channels), BF16),
        ),
        [],
        16,
        1_000_000,
        3_000_000,
        space_weight[0].reshape(9, channels, channels),
        time_weight[0],
        x_own,
        places=[VM, VM, pl.ANY],
    )

    def turned(message, by):
        return lax.ppermute(message, "chan", [(i, (i + by) % chan) for i in range(chan)])

    x_flat = x_own.reshape((rows * cols,) + cell)
    pieces = [
        x_own,
        turned(to_right, 1),
        *[turned(x_flat, d) for d in range(2, chan - 1)],
        turned(to_left, chan - 1),
    ]
    swap = [(0, 1), (1, 0)]
    to_side = call(
        side_kernel,
        bf16(3 * rows * cols + cols + 2),
        [],
        16,
        1_000_000,
        1_000_000,
        x_own, pieces[1], pieces[-1], cot_own, pick,
        places=[VM] * 4 + [pl.ANY],
    )
    from_side = lax.ppermute(to_side, "space", swap)

    def gathered(parts, after=()):
        half = call(
            functools.partial(collect_kernel, len(after)),
            bf16(rows, width),
            [],
            16,
            1_000_000,
            1_000_000,
            *parts,
            *after,
            places=[VM] * len(parts) + [pl.ANY] * len(after),
        )
        return half, lax.ppermute(half, "space", swap)

    slope_w, payload = call(
        functools.partial(first_kernel, frames),
        (jax.ShapeDtypeStruct((win, channels), F32), bf16(rows, cols)),
        [
            pltpu.VMEM((rows + 4, cols + 4) + cell, BF16),
            pltpu.VMEM((rows + 2, cols + 2) + cell, BF16),
            pltpu.VMEM((rows + 2, cols + 2) + cell, BF16),
        ],
        20,
        1,
        1,
        x_own, cot_own, pieces[1], pieces[-1], from_side, w, tw,
    )

    padded = pltpu.VMEM((height + 2, width + 2) + cell, BF16)
    hg_win = pltpu.VMEM((rows + 2, cols + 2) + cell, BF16)
    for tick in range(depth - 1):
        if tick:
            payload = call(
                functools.partial(tick_kernel, frames),
                bf16(rows, cols),
                [padded, hg_win],
                large,
                2 * win * 12 * channels * channels,
                4_000_000,
                *g_all, cot_own, slope_w, w, tw,
            )
        if not tick:
            far = pieces[2:-1]
            to_late = call(
                functools.partial(late_kernel, len(far)),
                bf16(len(far) * rows * cols),
                [],
                16,
                1,
                1,
                *far,
                payload,
                places=[VM] * len(far) + [pl.ANY],
            )
            from_late = lax.all_gather(to_late, "space", axis=0, tiled=False)
        arrived = []
        for d in range(chan):
            pairs = [
                (c * depth + p, (c + d) % chan * depth + (p - 1) % depth)
                for p in range(depth)
                for c in range(chan)
            ]
            arrived.append(lax.ppermute(payload, ("chan", "pipe"), pairs))
        if not tick:
            operands = [*pieces, from_side, from_late, w]
            act_t, x_t, slope_s = call(
                functools.partial(tile_kernel, chan),
                (
                    jax.ShapeDtypeStruct((channels, count), BF16),
                    jax.ShapeDtypeStruct((channels, count), BF16),
                    jax.ShapeDtypeStruct((count, lanes), F32),
                ),
                [padded],
                large,
                1,
                1,
                *operands,
                arrived[0],
                places=[VM] * len(operands) + [pl.ANY],
            )
        g_all = gathered(arrived, () if tick else (slope_s,))
    grad_near, time_near, space_near = call(
        functools.partial(near_kernel, frames, share),
        (
            jax.ShapeDtypeStruct((rows, width, steps, lanes), BF16),
            jax.ShapeDtypeStruct((channels, lag_groups * lanes), F32),
            jax.ShapeDtypeStruct((channels, tap_groups * lanes), F32),
        ),
        [
            pltpu.VMEM((count // 2, lag_groups * lanes), BF16),
            pltpu.VMEM((rows + 2, width + 2, steps, lanes), BF16),
            pltpu.VMEM(((rows - 1) * width * steps, tap_groups * lanes), BF16),
        ],
        large,
        count * channels * channels * 4,
        4_000_000,
        g_all[0],
        slope_s,
        act_t,
        x_t,
        pick,
    )
    grads, space_grad, time_grad = call(
        functools.partial(final_kernel, frames, share),
        (
            jax.ShapeDtypeStruct((clips, frames, rows, cols, channels), BF16),
            jax.ShapeDtypeStruct((9, share, channels), F32),
            jax.ShapeDtypeStruct((3, share, channels), F32),
        ),
        [
            pltpu.VMEM((rows + 2, width + 2) + cell, BF16),
            hg_win,
            pltpu.VMEM((height + 2, width + 2, steps, lanes), BF16),
            pltpu.VMEM(((rows + 1) * width * steps, tap_groups * lanes), BF16),
            pltpu.VMEM((count // 2, lag_groups * lanes), BF16),
        ],
        large,
        4 * win * 9 * channels * channels,
        8_000_000,
        *g_all, grad_near, time_near, space_near, slope_w, slope_s, act_t, x_t, w, tw, pick,
    )
    return (
        grads[None],
        jnp.swapaxes(space_grad, 1, 2).reshape(3, 3, channels, share)[None],
        jnp.swapaxes(time_grad, 1, 2)[None],
    )


def solution(mesh):
    return jax.shard_map(
        per_device,
        mesh=mesh,
        in_specs=(
            P("pipe", "groups", None, "space", "chan", None),
            P("groups", None, "space", "chan", None),
            P("pipe", None, None, None, None),
            P("pipe", None, None, None),
        ),
        out_specs=(
            P("pipe", "groups", None, "space", "chan", None),
            P("pipe", "groups", None, None, "chan"),
            P("pipe", "groups", None, "chan"),
        ),
        check_vma=False,
    )
```

```python
import functools

import jax
import jax.numpy as jnp
from jax import lax
from jax.experimental import pallas as pl
from jax.experimental.pallas import tpu as pltpu
from jax.sharding import PartitionSpec as P

F32 = jnp.float32
BF16 = jnp.bfloat16
MIB = 1024 * 1024
ROWS_IN = (((1,), (1,)), ((), ()))


def dot(left, right):
    return jnp.dot(left, right, preferred_element_type=F32)


def dot_back(left, right):
    return lax.dot_general(left, right, ROWS_IN, preferred_element_type=F32)


def frame_shift(term, lag, frames):
    rows = term.shape[0]
    moved = pltpu.roll(term, rows - lag, 0)
    frame = lax.broadcasted_iota(jnp.int32, term.shape, 0) % frames
    return jnp.where(frame < frames - lag, moved, 0.0)


def slope_of(hidden):
    sig = jax.nn.sigmoid(hidden)
    return sig * (1.0 + hidden * (1.0 - sig))


def pack_kernel(both_ref, xc_ref, cc_ref, right_ref, left_ref):
    rows, cols, steps, channels = xc_ref.shape
    for n, dst in enumerate((xc_ref, cc_ref)):
        for r in range(rows):
            dst[r] = jnp.swapaxes(both_ref[n, :, :, r].reshape(steps, cols, channels), 0, 1)
    cells = rows * cols
    for msg, col in ((right_ref, cols - 1), (left_ref, 0)):
        msg[:cells] = xc_ref[...].reshape(cells, steps, channels)
        for r in range(rows):
            msg[cells + r] = cc_ref[r, col]


def weights_kernel(share, w_in, tw_in, after_ref, w_ref, tw_ref, pick_ref):
    channels = w_ref.shape[-1]
    w_ref[...] = w_in[...]
    tw_ref[...] = tw_in[...]
    first = pl.multiple_of(lax.axis_index("chan") * share, share)
    copies = pick_ref.shape[0] // (4 * share)
    for lag in range(3):
        for j in range(lag * copies, (lag + 1) * copies):
            pick_ref[j * share : (j + 1) * share, :] = tw_in[lag, pl.ds(first, share), :]
    at = lax.broadcasted_iota(jnp.int32, (share, channels), 1) - first
    chosen = at == lax.broadcasted_iota(jnp.int32, (share, channels), 0)
    for j in range(3 * copies, 4 * copies):
        pick_ref[j * share : (j + 1) * share, :] = jnp.where(chosen, 1.0, 0.0).astype(BF16)


def side_kernel(x_ref, l_ref, r_ref, cot_ref, after_ref, side_ref):
    rows, cols, steps, channels = x_ref.shape
    cells = rows * cols
    side_ref[:cells] = x_ref[...].reshape(cells, steps, channels)
    side_ref[cells : 2 * cells] = l_ref[:cells]
    side_ref[2 * cells : 3 * cells] = r_ref[:cells]
    row = (1 - lax.axis_index("space")) * (rows - 1)
    side_ref[3 * cells] = l_ref[cells + row]
    side_ref[3 * cells + 1 : 3 * cells + 1 + cols] = cot_ref[row]
    side_ref[3 * cells + 1 + cols] = r_ref[cells + row]


def late_kernel(count, *refs):
    pieces, late_ref = refs[:count], refs[-1]
    cells = pieces[0].shape[0]
    for n, piece in enumerate(pieces):
        late_ref[n * cells : (n + 1) * cells] = piece[...]


def conv_back(hg_ref, w_ref, rows, cols):
    channels = w_ref.shape[-1]
    conv = None
    for u in range(3):
        for v in range(3):
            piece = hg_ref[2 - u : 2 - u + rows, 2 - v : 2 - v + cols]
            term = dot_back(piece.reshape(-1, channels), w_ref[3 * u + v])
            conv = term if conv is None else conv + term
    return conv


def window_grad(window, slope_ref, tw_ref, hg_ref, frames):
    act = dot_back(window, tw_ref[0])
    for lag in (1, 2):
        act = act + frame_shift(dot_back(window, tw_ref[lag]), lag, frames)
    hg_ref[...] = (act * slope_ref[...]).astype(BF16).reshape(hg_ref.shape)


def send_on(out_ref, own, conv, cot_ref):
    first = lax.axis_index("pipe") == 0

    @pl.when(first)
    def _():
        out_ref[...] = cot_ref[...]

    @pl.when(jnp.logical_not(first))
    def _():
        out_ref[...] = (own.astype(F32) + conv).astype(BF16).reshape(out_ref.shape)


def first_kernel(
    frames, x_ref, cot_ref, l_ref, r_ref, side_ref, w_ref, tw_ref,
    slope_ref, out_ref, xw_ref, cw_ref, hg_ref,
):
    rows, cols, steps, channels = x_ref.shape
    cells = rows * cols
    chan = lax.axis_size("chan")
    bottom = lax.axis_index("space")
    xw_ref[2 : 2 + rows, 2 : 2 + cols] = x_ref[...]
    cw_ref[1 : 1 + rows, 1 : 1 + cols] = cot_ref[...]
    for r in range(rows):
        xw_ref[2 + r, 0:2] = l_ref[r * cols + cols - 2 : r * cols + cols]
        xw_ref[2 + r, cols + 2 : cols + 4] = r_ref[r * cols : r * cols + 2]
        cw_ref[1 + r, 0] = l_ref[cells + r]
        cw_ref[1 + r, cols + 1] = r_ref[cells + r]
    near = (1 - bottom) * (rows + 2)
    far = bottom * (rows + 2)
    for i in range(2):
        at = (bottom * (rows - 2) + i) * cols
        xw_ref[near + i, 2 : 2 + cols] = side_ref[pl.ds(at, cols)]
        xw_ref[near + i, 0:2] = side_ref[pl.ds(cells + at + cols - 2, 2)]
        xw_ref[near + i, cols + 2 : cols + 4] = side_ref[pl.ds(2 * cells + at, 2)]
        xw_ref[far + i] = jnp.zeros(xw_ref.shape[1:], BF16)
    near = (1 - bottom) * (rows + 1)
    far = bottom * (rows + 1)
    cw_ref[near] = side_ref[3 * cells :]
    cw_ref[far] = jnp.zeros(cw_ref.shape[1:], BF16)
    me = lax.axis_index("chan")
    for end, c in ((0, 0), (chan - 1, cols + 2)):

        @pl.when(me == end)
        def _(c=c):
            xw_ref[:, c : c + 2] = jnp.zeros((rows + 4, 2, steps, channels), BF16)
            edge = min(c, cols + 1)
            cw_ref[:, edge : edge + 1] = jnp.zeros((rows + 2, 1, steps, channels), BF16)

    hidden = None
    for u in range(3):
        for v in range(3):
            piece = xw_ref[u : u + rows + 2, v : v + cols + 2]
            term = dot(piece.reshape(-1, channels), w_ref[3 * u + v])
            hidden = term if hidden is None else hidden + term
    slope_ref[...] = slope_of(hidden)
    window_grad(cw_ref[...].reshape(-1, channels), slope_ref, tw_ref, hg_ref, frames)
    conv = conv_back(hg_ref, w_ref, rows, cols)
    send_on(out_ref, cot_ref[...].reshape(-1, channels), conv, cot_ref)


def collect_kernel(extra, *refs):
    pieces, out_ref = refs[: -1 - extra], refs[-1]
    chan = len(pieces)
    rows, cols, steps, channels = pieces[0].shape
    me = lax.axis_index("chan")
    for d, piece in enumerate(pieces):
        out_ref[:, pl.ds(lax.rem(me - d + chan, chan) * cols, cols)] = piece[...]


def clear_rim(padded):
    rows_all, cols_all, steps, channels = padded.shape
    zero_row = jnp.zeros((1, cols_all, steps, channels), padded.dtype)
    padded[0:1] = zero_row
    padded[rows_all - 1 :] = zero_row
    for r in range(1, rows_all - 1):
        for c in (0, cols_all - 1):
            padded[r, c] = jnp.zeros((steps, channels), padded.dtype)


def fill_padded(padded, own, other):
    clear_rim(padded)
    rows, cols = own.shape[0], own.shape[1]
    bottom = lax.axis_index("space")
    for half, top in ((own, bottom * rows), (other, (1 - bottom) * rows)):
        padded[pl.ds(1 + top, rows), 1 : 1 + cols] = half[...]


def fill_from_pieces(padded, rows, cols, pieces, side, late):
    clear_rim(padded)
    chan, cells = len(pieces), rows * cols
    me = lax.axis_index("chan")
    bottom = lax.axis_index("space")
    for d, piece in enumerate(pieces):
        place = 1 + lax.rem(me - d + chan, chan) * cols
        for r in range(rows):
            near = piece[r] if d == 0 else piece[r * cols : (r + 1) * cols]
            padded[1 + bottom * rows + r, pl.ds(place, cols)] = near
            source, n = (late, d - 2) if 1 < d < chan - 1 else (side, min(d, 2))
            at = n * cells + r * cols
            far = 1 + (1 - bottom) * rows + r
            if source is late:
                padded[far, pl.ds(place, cols)] = late[1 - bottom, at : at + cols]
            else:
                padded[far, pl.ds(place, cols)] = side[at : at + cols]


def own_window(gp_ref, r0, slope_ref, w_ref, tw_ref, hg_ref, frames, rows, cols):
    channels = w_ref.shape[-1]
    c0 = lax.axis_index("chan") * cols
    window = gp_ref[pl.ds(r0, rows + 2), pl.ds(c0, cols + 2)].reshape(-1, channels)
    window_grad(window, slope_ref, tw_ref, hg_ref, frames)
    own = gp_ref[pl.ds(r0 + 1, rows), pl.ds(c0 + 1, cols)].reshape(-1, channels)
    return own, conv_back(hg_ref, w_ref, rows, cols)


def tick_kernel(
    frames, g_ref, other_ref, cot_ref, slope_ref, w_ref, tw_ref, out_ref, gp_ref, hg_ref
):
    rows, cols = cot_ref.shape[:2]
    fill_padded(gp_ref, g_ref, other_ref)
    r0 = lax.axis_index("space") * rows
    own, conv = own_window(gp_ref, r0, slope_ref, w_ref, tw_ref, hg_ref, frames, rows, cols)
    send_on(out_ref, own, conv, cot_ref)


def tile_kernel(chan, *refs):
    pieces, (side, late, w_ref) = refs[:chan], refs[chan : chan + 3]
    act_ref, xt_ref, slope_ref, xp_ref = refs[-4:]
    rows, cols, steps, channels = pieces[0].shape
    width = chan * cols
    share = channels // chan
    fill_from_pieces(xp_ref, rows, cols, pieces, side, late)
    span = width * steps
    turn = lax.rem(channels - lax.axis_index("chan") * share, channels)
    for i in range(2 * rows):
        hidden = None
        for u in range(3):
            for v in range(3):
                piece = xp_ref[i + u, v : v + width].reshape(-1, channels)
                term = dot(piece, w_ref[3 * u + v])
                hidden = term if hidden is None else hidden + term
        active = (hidden * jax.nn.sigmoid(hidden)).astype(BF16)
        act_ref[:, i * span : (i + 1) * span] = active.T
        slope = slope_of(pltpu.roll(hidden, turn, 1)[:, :share])
        copies = slope_ref.shape[1] // share
        slope_ref[i * span : (i + 1) * span, :] = jnp.concatenate([slope] * copies, axis=1)
        xt_ref[:, i * span : (i + 1) * span] = xp_ref[i + 1, 1 : 1 + width].reshape(-1, channels).T


def lane_choice(values, share):
    part = lax.broadcasted_iota(jnp.int32, values[0].shape, 1) // share
    chosen = values[0]
    for j in range(1, len(values)):
        chosen = jnp.where(part == j, values[j], chosen)
    return chosen


def digest(block, slope, pick_ref, frames, share):
    lanes = slope.shape[1]
    copies = lanes // share
    mixed = dot_back(block, pick_ref[...])
    act = mixed[:, :lanes]
    for lag in (1, 2):
        act = act + frame_shift(mixed[:, lag * lanes : (lag + 1) * lanes], lag, frames)
    own = mixed[:, 3 * lanes :]
    lagged = [own, frame_shift(own, 1, frames), frame_shift(own, 2, frames)]
    groups = [lane_choice(lagged[t : t + copies], share) for t in range(0, 3, copies)]
    return (act * slope).astype(BF16), [group.astype(BF16) for group in groups]


def digest_half(half_ref, bottom, slope_ref, act_ref, pick_ref, put, gcols_ref, frames, share):
    rows, width, steps, channels = half_ref.shape
    span = width * steps
    lanes = slope_ref.shape[1]
    start = bottom * rows * span
    for r in range(rows):
        slope = slope_ref[pl.ds(pl.multiple_of(start + r * span, span), span), :]
        grad, groups = digest(
            half_ref[r].reshape(span, channels), slope, pick_ref, frames, share
        )
        put(r, grad.reshape(width, steps, lanes))
        for t, group in enumerate(groups):
            gcols_ref[r * span : (r + 1) * span, t * lanes : (t + 1) * lanes] = group
    here = pl.ds(pl.multiple_of(start, span), rows * span)
    return dot(act_ref[:, here], gcols_ref[...])


def tap_products(hs_ref, top, x_top, count, xt_ref, hcols_ref, share):
    width, steps, lanes = hs_ref.shape[1] - 2, *hs_ref.shape[2:]
    copies = lanes // share
    span = width * steps
    for n, first in enumerate(range(0, 9, copies)):
        for i in range(count):
            taps = [
                hs_ref[top + i + 2 - tap // 3, 2 - tap % 3 : 2 - tap % 3 + width].reshape(span, lanes)
                for tap in range(first, min(first + copies, 9))
            ]
            hcols_ref[i * span : (i + 1) * span, n * lanes : (n + 1) * lanes] = lane_choice(
                taps, share
            )
    here = pl.ds(pl.multiple_of(x_top * span, span), count * span)
    return dot(xt_ref[:, here], hcols_ref[...])


def near_kernel(
    frames, share, g_ref, slope_ref, act_ref, xt_ref, pick_ref,
    grad_ref, time_ref, space_ref, gcols_ref, hs_ref, hcols_ref,
):
    rows, width = g_ref.shape[:2]
    clear_rim(hs_ref)

    def put(r, grad):
        grad_ref[r] = grad
        hs_ref[1 + r, 1 : 1 + width] = grad

    bottom = lax.axis_index("space")
    time_ref[...] = digest_half(
        g_ref, bottom, slope_ref, act_ref, pick_ref, put, gcols_ref, frames, share
    )
    space_ref[...] = tap_products(
        hs_ref, bottom, bottom * (rows + 1), rows - 1, xt_ref, hcols_ref, share
    )


def final_kernel(
    frames, share, g_ref, other_ref, near_ref, time_near_ref, space_near_ref, slope_w_ref,
    slope_s_ref, act_ref, xt_ref, w_ref, tw_ref, pick_ref,
    out_ref, space_out, time_out, gw_ref, hg_ref, hs_ref, hcols_ref, gcols_ref,
    space_ref, time_ref, sems,
):
    rows, width, steps, channels = g_ref.shape
    clips, _, _, cols, _ = out_ref.shape
    bottom = lax.axis_index("space")
    clear_rim(hs_ref)
    hs_ref[pl.ds(1 + bottom * rows, rows), 1 : 1 + width] = near_ref[...]

    def put(r, grad):
        hs_ref[1 + (1 - bottom) * rows + r, 1 : 1 + width] = grad

    time_sum = time_near_ref[...] + digest_half(
        other_ref, 1 - bottom, slope_s_ref, act_ref, pick_ref, put, gcols_ref, frames, share
    )
    time_ref[...] = time_sum.T[: 3 * share].reshape(time_ref.shape)
    time_copy = pltpu.make_async_copy(time_ref, time_out, sems.at[0])
    time_copy.start()
    top = (1 - bottom) * (rows - 1)
    space_sum = space_near_ref[...] + tap_products(
        hs_ref, top, top, rows + 1, xt_ref, hcols_ref, share
    )
    space_ref[...] = space_sum.T[: 9 * share].reshape(space_ref.shape)
    space_copy = pltpu.make_async_copy(space_ref, space_out, sems.at[1])
    space_copy.start()
    clear_rim(gw_ref)
    gw_ref[1 : 1 + rows, 1 : 1 + width] = g_ref[...]
    gw_ref[(1 - bottom) * (rows + 1), 1 : 1 + width] = other_ref[bottom * (rows - 1)]
    own, conv = own_window(gw_ref, 0, slope_w_ref, w_ref, tw_ref, hg_ref, frames, rows, cols)
    grads = (own.astype(F32) + conv).astype(BF16).reshape(rows, cols, steps, channels)
    for r in range(rows):
        out_ref[:, :, r] = jnp.swapaxes(grads[r], 0, 1).reshape(clips, frames, cols, channels)
    time_copy.wait()
    space_copy.wait()


VM = pltpu.VMEM


def call(kernel, outs, scratch, limit, flops, moved, *operands, places=None, out_places=None):
    places = places or [VM] * len(operands)
    return pl.pallas_call(
        kernel,
        out_shape=outs,
        in_specs=[pl.BlockSpec(memory_space=place) for place in places],
        **(
            {"out_specs": tuple(pl.BlockSpec(memory_space=place) for place in out_places)}
            if out_places
            else {}
        ),
        scratch_shapes=scratch,
        compiler_params=pltpu.CompilerParams(vmem_limit_bytes=limit * MIB),
        cost_estimate=pl.CostEstimate(flops=flops, bytes_accessed=moved, transcendentals=0),
    )(*operands)


def per_device(activations, cotangent, space_weight, time_weight):
    clips, frames, rows, cols, channels = activations.shape[1:]
    steps = clips * frames
    chan, depth = lax.axis_size("chan"), lax.axis_size("pipe")
    share = channels // chan
    copies = max(1, 128 // share)
    lanes = copies * share
    lag_groups, tap_groups = -(-3 // copies), -(-9 // copies)
    height, width = 2 * rows, chan * cols
    count = height * width * steps
    win = (rows + 2) * (cols + 2) * steps
    large = 24 if chan <= 4 else 56
    cell = (steps, channels)

    def bf16(*shape):
        return jax.ShapeDtypeStruct(shape + cell, BF16)

    beside = rows * cols + rows
    x_own, cot_own, to_right, to_left = call(
        pack_kernel,
        (bf16(rows, cols), bf16(rows, cols), bf16(beside), bf16(beside)),
        [],
        16,
        1_000_000,
        1_000_000,
        jnp.stack([activations[0], cotangent]),
    )
    w, tw, pick = call(
        functools.partial(weights_kernel, share),
        (
            jax.ShapeDtypeStruct((9, channels, channels), BF16),
            jax.ShapeDtypeStruct((3, channels, channels), BF16),
            jax.ShapeDtypeStruct((4 * copies * share, channels), BF16),
        ),
        [],
        16,
        1_000_000,
        3_000_000,
        space_weight[0].reshape(9, channels, channels),
        time_weight[0],
        x_own,
        places=[VM, VM, pl.ANY],
    )

    def turned(message, by):
        return lax.ppermute(message, "chan", [(i, (i + by) % chan) for i in range(chan)])

    x_flat = x_own.reshape((rows * cols,) + cell)
    pieces = [
        x_own,
        turned(to_right, 1),
        *[turned(x_flat, d) for d in range(2, chan - 1)],
        turned(to_left, chan - 1),
    ]
    swap = [(0, 1), (1, 0)]
    to_side = call(
        side_kernel,
        bf16(3 * rows * cols + cols + 2),
        [],
        16,
        1_000_000,
        1_000_000,
        x_own, pieces[1], pieces[-1], cot_own, pick,
        places=[VM] * 4 + [pl.ANY],
    )
    from_side = lax.ppermute(to_side, "space", swap)

    def gathered(parts, after=()):
        half = call(
            functools.partial(collect_kernel, len(after)),
            bf16(rows, width),
            [],
            16,
            1_000_000,
            1_000_000,
            *parts,
            *after,
            places=[VM] * len(parts) + [pl.ANY] * len(after),
        )
        return half, lax.ppermute(half, "space", swap)

    slope_w, payload = call(
        functools.partial(first_kernel, frames),
        (jax.ShapeDtypeStruct((win, channels), F32), bf16(rows, cols)),
        [
            pltpu.VMEM((rows + 4, cols + 4) + cell, BF16),
            pltpu.VMEM((rows + 2, cols + 2) + cell, BF16),
            pltpu.VMEM((rows + 2, cols + 2) + cell, BF16),
        ],
        20,
        1,
        1,
        x_own, cot_own, pieces[1], pieces[-1], from_side, w, tw,
    )

    padded = pltpu.VMEM((height + 2, width + 2) + cell, BF16)
    hg_win = pltpu.VMEM((rows + 2, cols + 2) + cell, BF16)
    for tick in range(depth - 1):
        if tick:
            payload = call(
                functools.partial(tick_kernel, frames),
                bf16(rows, cols),
                [padded, hg_win],
                large,
                2 * win * 12 * channels * channels,
                4_000_000,
                *g_all, cot_own, slope_w, w, tw,
            )
        if not tick:
            far = pieces[2:-1]
            to_late = call(
                functools.partial(late_kernel, len(far)),
                bf16(len(far) * rows * cols),
                [],
                16,
                1,
                1,
                *far,
                payload,
                places=[VM] * len(far) + [pl.ANY],
            )
            from_late = lax.all_gather(to_late, "space", axis=0, tiled=False)
        arrived = []
        for d in range(chan):
            pairs = [
                (c * depth + p, (c + d) % chan * depth + (p - 1) % depth)
                for p in range(depth)
                for c in range(chan)
            ]
            arrived.append(lax.ppermute(payload, ("chan", "pipe"), pairs))
        if not tick:
            operands = [*pieces, from_side, from_late, w]
            act_t, x_t, slope_s = call(
                functools.partial(tile_kernel, chan),
                (
                    jax.ShapeDtypeStruct((channels, count), BF16),
                    jax.ShapeDtypeStruct((channels, count), BF16),
                    jax.ShapeDtypeStruct((count, lanes), F32),
                ),
                [padded],
                large,
                1,
                1,
                *operands,
                arrived[0],
                places=[VM] * len(operands) + [pl.ANY],
            )
        g_all = gathered(arrived, () if tick else (slope_s,))
    grad_near, time_near, space_near = call(
        functools.partial(near_kernel, frames, share),
        (
            jax.ShapeDtypeStruct((rows, width, steps, lanes), BF16),
            jax.ShapeDtypeStruct((channels, lag_groups * lanes), F32),
            jax.ShapeDtypeStruct((channels, tap_groups * lanes), F32),
        ),
        [
            pltpu.VMEM((count // 2, lag_groups * lanes), BF16),
            pltpu.VMEM((rows + 2, width + 2, steps, lanes), BF16),
            pltpu.VMEM(((rows - 1) * width * steps, tap_groups * lanes), BF16),
        ],
        large,
        count * channels * channels * 4,
        4_000_000,
        g_all[0],
        slope_s,
        act_t,
        x_t,
        pick,
    )
    grads, space_grad, time_grad = call(
        functools.partial(final_kernel, frames, share),
        (
            jax.ShapeDtypeStruct((clips, frames, rows, cols, channels), BF16),
            jax.ShapeDtypeStruct((9, share, channels), F32),
            jax.ShapeDtypeStruct((3, share, channels), F32),
        ),
        [
            pltpu.VMEM((rows + 2, width + 2) + cell, BF16),
            hg_win,
            pltpu.VMEM((height + 2, width + 2, steps, lanes), BF16),
            pltpu.VMEM(((rows + 1) * width * steps, tap_groups * lanes), BF16),
            pltpu.VMEM((count // 2, lag_groups * lanes), BF16),
            pltpu.VMEM((9, share, channels), F32),
            pltpu.VMEM((3, share, channels), F32),
            pltpu.SemaphoreType.DMA((2,)),
        ],
        large,
        4 * win * 9 * channels * channels,
        8_000_000,
        *g_all, grad_near, time_near, space_near, slope_w, slope_s, act_t, x_t, w, tw, pick,
        out_places=[VM, pl.ANY, pl.ANY],
    )
    return (
        grads[None],
        jnp.swapaxes(space_grad, 1, 2).reshape(3, 3, channels, share)[None],
        jnp.swapaxes(time_grad, 1, 2)[None],
    )


def solution(mesh):
    return jax.shard_map(
        per_device,
        mesh=mesh,
        in_specs=(
            P("pipe", "groups", None, "space", "chan", None),
            P("groups", None, "space", "chan", None),
            P("pipe", None, None, None, None),
            P("pipe", None, None, None),
        ),
        out_specs=(
            P("pipe", "groups", None, "space", "chan", None),
            P("pipe", "groups", None, None, "chan"),
            P("pipe", "groups", None, "chan"),
        ),
        check_vma=False,
    )
```
